32 devices in a mesh: wide: 8 (over y, x, core), tp: 4 (over z).
Axes of the slice: x: 2, y: 2, z: 4, core: 2. Of those that a mesh axis runs over, the one named last changes fastest.
Arguments:
- tokens: bfloat16 [640, 16, 1024], P('tp', 'wide'), may hold values from -6 to 6
- cotangent: bfloat16 [640, 16, 1024], P('tp', 'wide'), may hold values from -6 to 6
- counts: int32 [8], P('wide'), may hold values from 1 to 2, as said below
- qkv_weight: float32 [2, 1024, 3, 1024], P(None, 'wide', None, 'tp'), may hold values from -0.1875 to 0.1875
- qkv_moment: float32 [2, 1024, 3, 1024], P(None, 'wide', None, 'tp'), may hold values from -96 to 96
- qkv_square: float32 [2, 1024, 3, 1024], P(None, 'wide', None, 'tp'), may hold values from 22.1568 to 88.6272
- out_weight: float32 [2, 1024, 1024], P(None, 'tp', 'wide'), may hold values from -1.25 to 1.25
- out_moment: float32 [2, 1024, 1024], P(None, 'tp', 'wide'), may hold values from -10 to 10
- out_square: float32 [2, 1024, 1024], P(None, 'tp', 'wide'), may hold values from 0.221568 to 0.886272
- up_weight: float32 [2, 1024, 4096], P(None, 'wide', 'tp'), may hold values from -0.1875 to 0.1875
- up_moment: float32 [2, 1024, 4096], P(None, 'wide', 'tp'), may hold values from -16 to 16
- up_square: float32 [2, 1024, 4096], P(None, 'wide', 'tp'), may hold values from 0.498528 to 1.994112
- down_weight: float32 [2, 4096, 1024], P(None, 'tp', 'wide'), may hold values from -0.09375 to 0.09375
- down_moment: float32 [2, 4096, 1024], P(None, 'tp', 'wide'), may hold values from -32 to 32
- down_square: float32 [2, 4096, 1024], P(None, 'tp', 'wide'), may hold values from 2.308 to 9.232
- row_vectors: float32 [2, 6, 1024], replicated, may hold values from -1.5 to 1.5, as said below
- row_moment: float32 [2, 6, 1024], replicated, may hold values from -80 to 80
- row_square: float32 [2, 6, 1024], replicated, may hold values from 12.4632 to 49.8528
- qv_bias: float32 [2, 2, 1024], P(None, None, 'tp'), may hold values from -4 to 4
- qv_moment: float32 [2, 2, 1024], P(None, None, 'tp'), may hold values from -96 to 96
- qv_square: float32 [2, 2, 1024], P(None, None, 'tp'), may hold values from 22.1568 to 88.6272
- up_bias: float32 [2, 4096], P(None, 'tp'), may hold values from -4 to 4
- bias_moment: float32 [2, 4096], P(None, 'tp'), may hold values from -16 to 16
- bias_square: float32 [2, 4096], P(None, 'tp'), may hold values from 0.498528 to 1.994112
Outputs:
- activations: bfloat16 [640, 16, 1024], P('tp', 'wide')
- input_grad: float32 [640, 16, 1024], P('tp', 'wide')
- qkv_new: float32 [2, 1024, 3, 1024], P(None, 'wide', None, 'tp')
- qkv_moment_new: float32 [2, 1024, 3, 1024], P(None, 'wide', None, 'tp')
- qkv_square_new: float32 [2, 1024, 3, 1024], P(None, 'wide', None, 'tp')
- qkv_copy: bfloat16 [2, 1024, 3, 1024], P(None, 'wide', None, 'tp')
- out_new: float32 [2, 1024, 1024], P(None, 'tp', 'wide')
- out_moment_new: float32 [2, 1024, 1024], P(None, 'tp', 'wide')
- out_square_new: float32 [2, 1024, 1024], P(None, 'tp', 'wide')
- out_copy: bfloat16 [2, 1024, 1024], P(None, 'tp', 'wide')
- up_new: float32 [2, 1024, 4096], P(None, 'wide', 'tp')
- up_moment_new: float32 [2, 1024, 4096], P(None, 'wide', 'tp')
- up_square_new: float32 [2, 1024, 4096], P(None, 'wide', 'tp')
- up_copy: bfloat16 [2, 1024, 4096], P(None, 'wide', 'tp')
- down_new: float32 [2, 4096, 1024], P(None, 'tp', 'wide')
- down_moment_new: float32 [2, 4096, 1024], P(None, 'tp', 'wide')
- down_square_new: float32 [2, 4096, 1024], P(None, 'tp', 'wide')
- down_copy: bfloat16 [2, 4096, 1024], P(None, 'tp', 'wide')
- row_new: float32 [2, 6, 1024], replicated
- row_moment_new: float32 [2, 6, 1024], replicated
- row_square_new: float32 [2, 6, 1024], replicated
- qv_new: float32 [2, 2, 1024], P(None, None, 'tp')
- qv_moment_new: float32 [2, 2, 1024], P(None, None, 'tp')
- qv_square_new: float32 [2, 2, 1024], P(None, None, 'tp')
- up_bias_new: float32 [2, 4096], P(None, 'tp')
- bias_moment_new: float32 [2, 4096], P(None, 'tp')
- bias_square_new: float32 [2, 4096], P(None, 'tp')
The draws below stay inside these ranges and needn't reach their ends.
Inputs may be any that keep to these rules, and one draw needn't show every extreme that they name: Slot s of group g holds an image where s < counts[g]; some group holds 2 images and some group 1. `row_vectors`: rows 0 and 2 of each layer are gains, the others biases.
All inputs are finite; a program needn't handle non-finite values.
Results may differ from the reference program's by a relative error of at most 0.014.
Values may be sent and summed in bfloat16 or wider, within the bound.
No kernel may reach another device: no remote copies, remote signals or barrier semaphores. Data moves between devices by JAX's collectives and lax.ppermute only.
A program may use at most 192 MiB of HBM per device.

```python
import math
import jax
import jax.numpy as jnp
from jax import lax

D = 1024
HEADS = 16
HDIM = 64
FF = 4096
SEQ = 640
VALID = 577
SLOTS = 2
LAYERS = 2
STEP = 10
IMAGES = 16
N_WIDE = 8


def draw_counts(key, part):
    key = jax.random.fold_in(key, 11)
    count_key, full_key, single_key = jax.random.split(key, 3)
    drawn_counts = jax.random.randint(count_key, (N_WIDE,), 1, SLOTS + 1)
    full_group = jax.random.randint(full_key, (), 0, N_WIDE)
    single_group = (full_group + 1 + jax.random.randint(single_key, (), 0, N_WIDE - 1)) % N_WIDE
    group_ids = jnp.arange(N_WIDE)
    drawn_counts = jnp.where(group_ids == full_group, SLOTS, drawn_counts)
    drawn_counts = jnp.where(group_ids == single_group, 1, drawn_counts)
    return drawn_counts.astype(jnp.int32)


def draw_row_vectors(key, part):
    key = jax.random.fold_in(key, 23)
    gain_key, bias_key = jax.random.split(key)
    gains = jax.random.uniform(gain_key, (LAYERS, 6, D), jnp.float32, 0.6, 1.4)
    biases = jnp.clip(0.3 * jax.random.normal(bias_key, (LAYERS, 6, D), jnp.float32), -1.5, 1.5)
    row_ids = jnp.arange(6)
    is_gain = (row_ids % 2 == 0) & (row_ids < 4)
    return jnp.where(is_gain[None, :, None], gains, biases)


def block_scale(stream_key, shape, shards, least, high):
    def one(position, shards_of):
        steps = jax.random.uniform(jax.random.fold_in(jax.random.fold_in(stream_key, 6), position), (shards_of,), jnp.float32, least / len(shards), high / len(shards))
        return jnp.repeat(jnp.exp(steps), shape[position] // shards_of).reshape((-1,) + (1,) * (len(shape) - position - 1))

    level = one(*shards[0])
    for cut in shards[1:]:
        level = level * one(*cut)
    return level


def gaussian(stream_key, dims, deviation, most, pieces=(), held_as=jnp.bfloat16):
    values = deviation * jax.random.normal(stream_key, dims, jnp.float32)
    if pieces:
        values = values * block_scale(stream_key, dims, pieces, -0.22, 0.18)
    return jnp.clip(values, -most, most).astype(held_as)


def setup_inputs(seed: int = 0) -> dict:
    key_list = jax.random.split(jax.random.key(seed), 25)
    return {
        "tokens": gaussian(key_list[0], (SEQ, IMAGES, D), 1.0, 6.0, ((0, 4), (1, 8))),
        "cotangent": gaussian(key_list[1], (SEQ, IMAGES, D), 1.0, 6.0, ((0, 4), (1, 8))),
        "counts": draw_counts(jax.random.fold_in(key_list[24], 71), 0),
        "qkv_weight": gaussian(key_list[3], (LAYERS, D, 3, D), D ** -0.5, 0.1875, ((1, 8), (3, 4)), jnp.float32),
        "qkv_moment": gaussian(key_list[4], (LAYERS, D, 3, D), (0.17 * (N_WIDE * SLOTS * VALID) ** 0.5), 96.0, ((1, 8), (3, 4)), jnp.float32),
        "qkv_square": jnp.clip(jnp.exp(math.log(88.6272) - 1.3862944 * jax.random.uniform(key_list[5], (LAYERS, D, 3, D), jnp.float32) ** block_scale(key_list[5], (LAYERS, D, 3, D), ((1, 8), (3, 4)), -0.2, 0.2)), 22.1568, 88.6272),
        "out_weight": gaussian(key_list[6], (LAYERS, D, D), (D * 16 // SEQ) ** -0.5, 1.25, ((1, 4), (2, 8)), jnp.float32),
        "out_moment": gaussian(key_list[7], (LAYERS, D, D), (0.017 * (N_WIDE * SLOTS * VALID) ** 0.5), 10.0, ((1, 4), (2, 8)), jnp.float32),
        "out_square": jnp.clip(jnp.exp(math.log(0.886272) - 1.3862944 * jax.random.uniform(key_list[8], (LAYERS, D, D), jnp.float32) ** block_scale(key_list[8], (LAYERS, D, D), ((1, 4), (2, 8)), -0.2, 0.2)), 0.221568, 0.886272),
        "up_weight": gaussian(key_list[9], (LAYERS, D, FF), D ** -0.5, 0.1875, ((1, 8), (2, 4)), jnp.float32),
        "up_moment": gaussian(key_list[10], (LAYERS, D, FF), (0.026 * (N_WIDE * SLOTS * VALID) ** 0.5), 16.0, ((1, 8), (2, 4)), jnp.float32),
        "up_square": jnp.clip(jnp.exp(math.log(1.994112) - 1.3862944 * jax.random.uniform(key_list[11], (LAYERS, D, FF), jnp.float32) ** block_scale(key_list[11], (LAYERS, D, FF), ((1, 8), (2, 4)), -0.2, 0.2)), 0.498528, 1.994112),
        "down_weight": gaussian(key_list[12], (LAYERS, FF, D), FF ** -0.5, 0.09375, ((1, 4), (2, 8)), jnp.float32),
        "down_moment": gaussian(key_list[13], (LAYERS, FF, D), (0.055 * (N_WIDE * SLOTS * VALID) ** 0.5), 32.0, ((1, 4), (2, 8)), jnp.float32),
        "down_square": jnp.clip(jnp.exp(math.log(9.232) - 1.3862944 * jax.random.uniform(key_list[14], (LAYERS, FF, D), jnp.float32) ** block_scale(key_list[14], (LAYERS, FF, D), ((1, 4), (2, 8)), -0.2, 0.2)), 2.308, 9.232),
        "row_vectors": draw_row_vectors(jax.random.fold_in(key_list[24], 71), 0),
        "row_moment": gaussian(key_list[16], (LAYERS, 6, D), (0.13 * (N_WIDE * SLOTS * VALID) ** 0.5), 80.0, (), jnp.float32),
        "row_square": jnp.clip(jnp.exp(jax.random.uniform(key_list[17], (LAYERS, 6, D), jnp.float32, math.log(12.4632), math.log(49.8528))), 12.4632, 49.8528),
        "qv_bias": gaussian(key_list[18], (LAYERS, 2, D), 0.3, 4.0, ((2, 4),), jnp.float32),
        "qv_moment": gaussian(key_list[19], (LAYERS, 2, D), (0.17 * (N_WIDE * SLOTS * VALID) ** 0.5), 96.0, ((2, 4),), jnp.float32),
        "qv_square": jnp.clip(jnp.exp(math.log(88.6272) - 1.3862944 * jax.random.uniform(key_list[20], (LAYERS, 2, D), jnp.float32) ** block_scale(key_list[20], (LAYERS, 2, D), ((2, 4),), -0.2, 0.2)), 22.1568, 88.6272),
        "up_bias": gaussian(key_list[21], (LAYERS, FF), 0.3, 4.0, ((1, 4),), jnp.float32),
        "bias_moment": gaussian(key_list[22], (LAYERS, FF), (0.026 * (N_WIDE * SLOTS * VALID) ** 0.5), 16.0, ((1, 4),), jnp.float32),
        "bias_square": jnp.clip(jnp.exp(math.log(1.994112) - 1.3862944 * jax.random.uniform(key_list[23], (LAYERS, FF), jnp.float32) ** block_scale(key_list[23], (LAYERS, FF), ((1, 4),), -0.2, 0.2)), 0.498528, 1.994112),
    }


NORM_EPS = 1e-05
BETA_ONE = 0.9
BETA_TWO = 0.999
ADAM_EPS = 1e-08
WEIGHT_DECAY = 0.01
VECTOR_RATE = 0.4
MASKED = -1e+30

@jax.custom_vjp
def low(v):
    return lax.optimization_barrier(v.astype(jnp.bfloat16)).astype(jnp.float32)

@jax.custom_vjp
def low_back(v):
    return v

def low_keep(v):
    return (low(v), None)

def low_pass(kept, grad):
    return (grad,)

def back_keep(v):
    return (v, None)

def back_low(kept, grad):
    return (low(grad),)
low.defvjp(low_keep, low_pass)
low_back.defvjp(back_keep, back_low)

def layer_norm(values, gain_vec, shift_vec):
    center = values - lax.optimization_barrier(jnp.mean(values, axis=-1, keepdims=True))
    spread = lax.optimization_barrier(jnp.mean(center * center, axis=-1, keepdims=True))
    return center * lax.rsqrt(spread + NORM_EPS) * gain_vec + shift_vec

def quick_gelu(values):
    return values * jax.nn.sigmoid(1.702 * values)

def adamw_step(weight, moment, square, gradient, step_rate, decay_rate):
    moment = BETA_ONE * moment + (1.0 - BETA_ONE) * gradient
    square = BETA_TWO * square + (1.0 - BETA_TWO) * gradient * gradient
    moment_hat = moment / (1.0 - BETA_ONE ** STEP)
    square_hat = square / (1.0 - BETA_TWO ** STEP)
    weight = weight - step_rate * (moment_hat / (jnp.sqrt(square_hat) + ADAM_EPS) + decay_rate * weight)
    return (weight, moment, square)

def dense(left_rows, right_mat):
    return jnp.einsum('rsk,km->rsm', left_rows, right_mat, precision=lax.Precision.HIGHEST)

def split_heads(values):
    return values.reshape(SEQ, SLOTS, HEADS, HDIM)

def group_forward(stream, valid_mask, weights):
    qkv_all, out_all, up_all, down_all, vector_all, qv_all, up_bias_all = weights
    keep_keys = valid_mask.T[:, None, None, :]
    for layer_index in range(LAYERS):
        vectors = vector_all[layer_index]
        normed = low(layer_norm(stream, vectors[0], vectors[1]))
        projected = dense(normed, qkv_all[layer_index].reshape(D, 3 * D)).reshape(SEQ, SLOTS, 3, D)
        queries = low(low_back(projected[:, :, 0] + qv_all[layer_index, 0]))
        key_rows = low(low_back(projected[:, :, 1]))
        value_rows = low(low_back(projected[:, :, 2] + qv_all[layer_index, 1]))
        scores = jnp.einsum('qnhd,knhd->nhqk', split_heads(queries), split_heads(key_rows), precision=lax.Precision.HIGHEST) * HDIM ** (-0.5)
        scores = jnp.where(keep_keys, low_back(scores), MASKED)
        softmax_out = low(jax.nn.softmax(scores, axis=-1))
        attended = jnp.einsum('nhqk,knhd->qnhd', softmax_out, split_heads(value_rows), precision=lax.Precision.HIGHEST).reshape(SEQ, SLOTS, D)
        attended = low(low_back(attended))
        stream = stream + low_back(dense(attended, out_all[layer_index]) + vectors[4])
        normed = low(layer_norm(stream, vectors[2], vectors[3]))
        pre_act = low_back(dense(normed, up_all[layer_index]) + up_bias_all[layer_index])
        hidden = low(quick_gelu(pre_act))
        stream = stream + low_back(dense(hidden, down_all[layer_index]) + vectors[5])
    return jnp.where(valid_mask[:, :, None], stream, 0.0)

def reference(tokens, cotangent, counts, qkv_weight, qkv_moment, qkv_square, out_weight, out_moment, out_square, up_weight, up_moment, up_square, down_weight, down_moment, down_square, row_vectors, row_moment, row_square, qv_bias, qv_moment, qv_square, up_bias, bias_moment, bias_square):
    positions = jnp.arange(SEQ, dtype=jnp.int32)[:, None]
    image_ids = jnp.arange(N_WIDE * SLOTS, dtype=jnp.int32)[None, :]
    image_limit = jnp.repeat(counts, SLOTS)[None, :]
    valid_mask = (positions < VALID) & (image_ids % SLOTS < image_limit)
    group_valid = valid_mask.reshape(SEQ, N_WIDE, SLOTS).transpose(1, 0, 2)
    group_tokens = tokens.astype(jnp.float32).reshape(SEQ, N_WIDE, SLOTS, D).transpose(1, 0, 2, 3)
    group_cot = cotangent.astype(jnp.float32).reshape(SEQ, N_WIDE, SLOTS, D).transpose(1, 0, 2, 3)

    def forward(stream, weights):
        lowered = (low(weights[0]), low(weights[1]), low(weights[2]), low(weights[3]), weights[4], weights[5], weights[6])

        def one_group(group_pair):
            return group_forward(group_pair[0], group_pair[1], lowered)
        return lax.map(jax.checkpoint(one_group), (stream, group_valid))
    weights = (qkv_weight, out_weight, up_weight, down_weight, row_vectors, qv_bias, up_bias)
    result, pullback = jax.vjp(forward, group_tokens, weights)
    grad_tokens, grad_weights = pullback(group_cot)
    activations = result.transpose(1, 0, 2, 3).reshape(SEQ, N_WIDE * SLOTS, D).astype(jnp.bfloat16)
    input_grad = grad_tokens.transpose(1, 0, 2, 3).reshape(SEQ, N_WIDE * SLOTS, D)
    qkv_new, qkv_moment_new, qkv_square_new = adamw_step(qkv_weight, qkv_moment, qkv_square, grad_weights[0], D ** (-0.5), WEIGHT_DECAY)
    out_new, out_moment_new, out_square_new = adamw_step(out_weight, out_moment, out_square, grad_weights[1], (D * 16 / SEQ) ** (-0.5), WEIGHT_DECAY)
    up_new, up_moment_new, up_square_new = adamw_step(up_weight, up_moment, up_square, grad_weights[2], D ** (-0.5), WEIGHT_DECAY)
    down_new, down_moment_new, down_square_new = adamw_step(down_weight, down_moment, down_square, grad_weights[3], FF ** (-0.5), WEIGHT_DECAY)
    row_new, row_moment_new, row_square_new = adamw_step(row_vectors, row_moment, row_square, grad_weights[4], VECTOR_RATE, 0.0)
    qv_new, qv_moment_new, qv_square_new = adamw_step(qv_bias, qv_moment, qv_square, grad_weights[5], VECTOR_RATE, 0.0)
    up_bias_new, bias_moment_new, bias_square_new = adamw_step(up_bias, bias_moment, bias_square, grad_weights[6], VECTOR_RATE, 0.0)
    return (activations, input_grad, qkv_new, qkv_moment_new, qkv_square_new, qkv_new.astype(jnp.bfloat16), out_new, out_moment_new, out_square_new, out_new.astype(jnp.bfloat16), up_new, up_moment_new, up_square_new, up_new.astype(jnp.bfloat16), down_new, down_moment_new, down_square_new, down_new.astype(jnp.bfloat16), row_new, row_moment_new, row_square_new, qv_new, qv_moment_new, qv_square_new, up_bias_new, bias_moment_new, bias_square_new)
```

```python
import jax
import jax.numpy as jnp
from jax import lax
from jax.sharding import PartitionSpec as P

D = 1024
HDIM = 64
FF = 4096
SEQ = 640
VALID = 577
LAYERS = 2
STEP = 10


NORM_EPS = 1e-05
BETA_ONE = 0.9
BETA_TWO = 0.999
ADAM_EPS = 1e-08
WEIGHT_DECAY = 0.01
VECTOR_RATE = 0.4
MASKED = -1e30


def layer_norm(values, gain_vec, shift_vec):
    center = values - jnp.mean(values, axis=-1, keepdims=True)
    spread = jnp.mean(center * center, axis=-1, keepdims=True)
    return center * lax.rsqrt(spread + NORM_EPS) * gain_vec + shift_vec


def quick_gelu(values):
    return values * jax.nn.sigmoid(1.702 * values)


def adamw_step(weight, moment, square, gradient, step_rate, decay_rate):
    moment = BETA_ONE * moment + (1.0 - BETA_ONE) * gradient
    square = BETA_TWO * square + (1.0 - BETA_TWO) * gradient * gradient
    moment_hat = moment / (1.0 - BETA_ONE**STEP)
    square_hat = square / (1.0 - BETA_TWO**STEP)
    weight = weight - step_rate * (
        moment_hat / (jnp.sqrt(square_hat) + ADAM_EPS) + decay_rate * weight
    )
    return (weight, moment, square)


def dense(left_rows, right_mat):
    return lax.dot_general(
        left_rows,
        right_mat,
        (((left_rows.ndim - 1,), (0,)), ((), ())),
        preferred_element_type=jnp.float32,
    )


def dense_back(left_rows, right_mat):
    return lax.dot_general(
        left_rows,
        right_mat,
        (((left_rows.ndim - 1,), (right_mat.ndim - 1,)), ((), ())),
        preferred_element_type=jnp.float32,
    )


def core_swap(values):
    return lax.ppermute(values, "wide", [(i, i ^ 1) for i in range(lax.axis_size("wide"))])


def pair_swap(values, bit):
    flip = 2 << bit
    return lax.ppermute(values, "wide", [(i, i ^ flip) for i in range(lax.axis_size("wide"))])


def tp_shift(values, distance):
    count = lax.axis_size("tp")
    return lax.ppermute(values, "tp", [(i, (i + distance) % count) for i in range(count)])


def tp_flip(values, bit):
    count = lax.axis_size("tp")
    return lax.ppermute(values, "tp", [(i, i ^ (1 << bit)) for i in range(count)])


def pair_bits():
    pairs = lax.axis_size("wide") // 2
    return pairs.bit_length() - 1


def by_core(mine, other, axis):
    lower = lax.axis_index("wide") % 2 == 0
    return jnp.where(
        lower,
        jnp.concatenate([mine, other], axis=axis),
        jnp.concatenate([other, mine], axis=axis),
    )


def half_of(values, which, axis):
    span = values.shape[axis] // 2
    return lax.dynamic_slice_in_dim(values, which * span, span, axis)


def relative(values, axis):
    pairs = lax.axis_size("wide") // 2
    pair = lax.axis_index("wide") // 2
    axis = axis % values.ndim
    span = values.shape[axis] // pairs
    shape = values.shape
    for bit in range(pair_bits()):
        step = span << bit
        split = values.reshape(shape[:axis] + (-1, 2, step) + shape[axis + 1 :])
        lower, upper = (lax.index_in_dim(split, k, axis + 1) for k in (0, 1))
        flipped = jnp.concatenate([upper, lower], axis=axis + 1).reshape(shape)
        values = jnp.where((pair >> bit) & 1 == 1, flipped, values)
    return values


def gather_matrix(shard):
    core = lax.axis_index("wide") % 2
    rows, kinds, columns = shard.shape
    low = shard.astype(jnp.bfloat16)
    mine = half_of(low, core, 2)
    other = core_swap(half_of(low, 1 - core, 2))
    own = by_core(mine, other, 0).reshape(2 * rows, kinds * columns // 2)
    own = jnp.concatenate(
        [own] + [tp_shift(own, d) for d in range(1, lax.axis_size("tp"))], axis=1
    )
    if pair_bits() == 2:
        over_x, over_y = pair_swap(own, 0), pair_swap(own, 1)
        far = [pair_swap(over_x[:rows], 1), pair_swap(over_y[rows:], 0)]
        return jnp.concatenate([own, over_x, over_y] + far, axis=0)
    for bit in range(pair_bits()):
        own = jnp.concatenate([own, pair_swap(own, bit)], axis=0)
    return own


def add_low(*terms):
    total = terms[0].astype(jnp.float32)
    for term in terms[1:]:
        total = total + term.astype(jnp.float32)
    return total


def scatter_matrix(grad, kinds):
    core = lax.axis_index("wide") % 2
    tp_count = lax.axis_size("tp")
    rows = grad.shape[0] // lax.axis_size("wide")
    grad = grad.astype(jnp.bfloat16)
    if pair_bits() == 2:
        block = 2 * rows
        own, over_x, over_y, far = (grad[k * block : (k + 1) * block] for k in range(4))
        far_x, far_y = pair_swap(far[:rows], 1), pair_swap(far[rows:], 0)
        over_x = jnp.concatenate(
            [add_low(over_x[:rows], far_x).astype(jnp.bfloat16), over_x[rows:]], axis=0
        )
        over_y = jnp.concatenate(
            [over_y[:rows], add_low(over_y[rows:], far_y).astype(jnp.bfloat16)], axis=0
        )
        own = add_low(own, pair_swap(over_x, 0), pair_swap(over_y, 1)).astype(jnp.bfloat16)
    else:
        own = grad
        for bit in reversed(range(pair_bits())):
            keep = own.shape[0] // 2
            own = add_low(own[:keep], pair_swap(own[keep:], bit)).astype(jnp.bfloat16)
    span = own.shape[1] // tp_count
    own = add_low(
        own[:, :span],
        *[tp_shift(own[:, d * span : (d + 1) * span], -d) for d in range(1, tp_count)],
    )
    own = own.reshape(2 * rows, kinds, span // kinds)
    mine = half_of(own, core, 0)
    other = core_swap(half_of(own, 1 - core, 0).astype(jnp.bfloat16)).astype(jnp.float32)
    return by_core(mine, other, 2)


def image_rows(values):
    core = lax.axis_index("wide") % 2
    tp_index = lax.axis_index("tp")
    tp_count = lax.axis_size("tp")
    values = values.astype(jnp.bfloat16)
    half = values.shape[0] // 2
    other = core_swap(half_of(values, 1 - core, 0))
    images = by_core(half_of(values, core, 0), other, 1)
    place = jnp.zeros((tp_count, half, values.shape[2]), jnp.bfloat16)
    for d in range(tp_count):
        block = lax.dynamic_index_in_dim(images, (tp_index + d) % tp_count, 1, keepdims=False)
        block = tp_shift(block, d) if d else block
        place = lax.dynamic_update_index_in_dim(
            place, block, (tp_index + tp_count - d) % tp_count, 0
        )
    both = by_core(place, core_swap(place), 1)
    return both.reshape(tp_count * 2 * half, values.shape[2])


def image_blocks(values):
    core = lax.axis_index("wide") % 2
    tp_index = lax.axis_index("tp")
    tp_count = lax.axis_size("tp")
    span = values.shape[0] // tp_count
    place = half_of(values.astype(jnp.bfloat16).reshape(tp_count, span, -1), core, 1)
    images = jnp.zeros((span // 2, tp_count, values.shape[1]), jnp.bfloat16)
    for d in range(tp_count):
        block = lax.dynamic_index_in_dim(place, (tp_index + d) % tp_count, 0, keepdims=False)
        block = tp_shift(block, d) if d else block
        images = lax.dynamic_update_index_in_dim(
            images, block, (tp_index + tp_count - d) % tp_count, 1
        )
    other = core_swap(half_of(images, 1 - core, 1))
    return by_core(half_of(images, core, 1), other, 0)


def core_sum(term):
    low = term.astype(jnp.bfloat16)
    return add_low(low, core_swap(low))


def vector_sum(values):
    for bit in range(pair_bits()):
        values = values + pair_swap(values, bit)
    for bit in range(lax.axis_size("tp").bit_length() - 1):
        values = values + tp_flip(values, bit)
    return values


def masked_scores(queries, key_rows, keep_keys):
    scores = jnp.einsum(
        "hqd,hkd->hqk", queries, key_rows, preferred_element_type=jnp.float32
    ) * HDIM ** (-0.5)
    return jnp.where(keep_keys[None, None, :], scores, MASKED)


def attend_one(queries, key_rows, value_rows, keep_keys):
    scores = masked_scores(queries, key_rows, keep_keys)
    highest = jnp.max(scores, axis=-1, keepdims=True)
    exponent = jnp.exp(scores - highest)
    totals = jnp.sum(exponent, axis=-1, keepdims=True)
    probs_low = (exponent / totals).astype(jnp.bfloat16)
    result = jnp.einsum("hqk,hkd->hqd", probs_low, value_rows, preferred_element_type=jnp.float32)
    return (result, highest[..., 0] + jnp.log(totals[..., 0]))


def attend_back(queries, key_rows, value_rows, keep_keys, log_total, grad_out):
    scores = masked_scores(queries, key_rows, keep_keys)
    attn_probs = jnp.exp(scores - log_total[..., None])
    grad_value = jnp.einsum(
        "hqk,hqd->hkd",
        attn_probs.astype(jnp.bfloat16),
        grad_out,
        preferred_element_type=jnp.float32,
    )
    grad_probs = jnp.einsum(
        "hqd,hkd->hqk", grad_out, value_rows, preferred_element_type=jnp.float32
    )
    inner_sum = jnp.sum(attn_probs * grad_probs, axis=-1, keepdims=True)
    grad_scores = (attn_probs * (grad_probs - inner_sum)).astype(jnp.bfloat16)
    grad_query = jnp.einsum(
        "hqk,hkd->hqd", grad_scores, key_rows, preferred_element_type=jnp.float32
    ) * HDIM ** (-0.5)
    grad_key = jnp.einsum(
        "hqk,hqd->hkd", grad_scores, queries, preferred_element_type=jnp.float32
    ) * HDIM ** (-0.5)
    return (grad_query, grad_key, grad_value)


def weight_grad(left, right):
    return lax.dot_general(
        left, right, (((0,), (0,)), ((), ())), preferred_element_type=jnp.float32
    )


def shards(
    tokens,
    cotangent,
    counts,
    qkv_weight,
    qkv_moment,
    qkv_square,
    out_weight,
    out_moment,
    out_square,
    up_weight,
    up_moment,
    up_square,
    down_weight,
    down_moment,
    down_square,
    row_vectors,
    row_moment,
    row_square,
    qv_bias,
    qv_moment,
    qv_square,
    up_bias,
    bias_moment,
    bias_square,
):
    row_count, slot_count, model_width = tokens.shape
    tp_count = lax.axis_size("tp")
    seq_len = row_count * tp_count
    local_width = qkv_weight.shape[3]
    local_hidden = up_weight.shape[2]
    tp_index = lax.axis_index("tp")
    core = lax.axis_index("wide") % 2
    half_width, half_hidden = local_width // 2, local_hidden // 2
    heads = tp_count * half_width // HDIM

    group = tp_index // slot_count
    group_count = jnp.where(group == core, counts, core_swap(counts))[0]
    live = (tp_index % slot_count) < group_count
    valid = (lax.iota(jnp.int32, seq_len) < VALID) & live

    def columns_half(values):
        return half_of(values, core, values.ndim - 1)

    def tp_all(values):
        return jnp.stack([values] + [tp_shift(values, d) for d in range(1, tp_count)], axis=-2)

    def to_heads(values):
        return values.reshape(seq_len, heads, HDIM).transpose(1, 0, 2)

    def from_heads(values):
        return values.transpose(1, 0, 2).reshape(seq_len, tp_count, half_width)

    qv_all = tp_all(columns_half(qv_bias))
    bias_all = tp_all(columns_half(up_bias))
    vectors_all = relative(row_vectors, 2)

    weights = []
    for layer_index in range(LAYERS):
        weights.append(
            (
                gather_matrix(qkv_weight[layer_index]),
                gather_matrix(out_weight[layer_index].T[:, None, :]),
                gather_matrix(up_weight[layer_index][:, None, :]),
                gather_matrix(down_weight[layer_index].T[:, None, :]),
            )
        )

    stream = relative(image_rows(tokens), 1).astype(jnp.float32)
    stored = []
    for layer_index in range(LAYERS):
        qkv_full, out_full, up_full, down_full = weights[layer_index]
        vectors = vectors_all[layer_index]
        normed = layer_norm(stream, vectors[0], vectors[1]).astype(jnp.bfloat16)
        projected = dense(normed, qkv_full).reshape(seq_len, tp_count, 3, half_width)
        query_low = to_heads((projected[:, :, 0] + qv_all[layer_index, 0]).astype(jnp.bfloat16))
        key_low = to_heads(projected[:, :, 1].astype(jnp.bfloat16))
        value_low = to_heads((projected[:, :, 2] + qv_all[layer_index, 1]).astype(jnp.bfloat16))
        head_out, log_total = attend_one(query_low, key_low, value_low, valid)
        attended = from_heads(head_out).astype(jnp.bfloat16).reshape(seq_len, heads * HDIM)
        stream_mid = stream + (core_sum(dense_back(attended, out_full)) + vectors[4])
        normed_two = layer_norm(stream_mid, vectors[2], vectors[3]).astype(jnp.bfloat16)
        pre_act = dense(normed_two, up_full) + bias_all[layer_index].reshape(-1)
        hidden = quick_gelu(pre_act).astype(jnp.bfloat16)
        stored.append(
            (
                stream,
                normed,
                query_low,
                key_low,
                value_low,
                log_total,
                attended,
                stream_mid,
                normed_two,
                pre_act,
                hidden,
            )
        )
        stream = stream_mid + (core_sum(dense_back(hidden, down_full)) + vectors[5])
    activations = image_blocks(
        relative(jnp.where(valid[:, None], stream, 0.0).astype(jnp.bfloat16), 1)
    )
    grad_stream = jnp.where(
        valid[:, None], relative(image_rows(cotangent), 1).astype(jnp.float32), 0.0
    )
    matrix_grads = [None] * LAYERS
    vector_sums = [None] * LAYERS
    for layer_index in reversed(range(LAYERS)):
        (
            stream_in,
            normed,
            query_low,
            key_low,
            value_low,
            log_total,
            attended,
            stream_mid,
            normed_two,
            pre_act,
            hidden,
        ) = stored[layer_index]
        qkv_full, out_full, up_full, down_full = weights[layer_index]
        vectors = vectors_all[layer_index]
        branch_low = grad_stream.astype(jnp.bfloat16)
        down_shard = scatter_matrix(weight_grad(branch_low, hidden), 1)
        grad_hidden = dense(branch_low, down_full)
        grad_pre = jax.vjp(quick_gelu, pre_act)[1](grad_hidden)[0].astype(jnp.bfloat16)
        up_shard = scatter_matrix(weight_grad(normed_two, grad_pre), 1)
        grad_normed_two = core_sum(dense_back(grad_pre, up_full))
        grad_mid, grad_gain_two, grad_shift_two = jax.vjp(
            layer_norm, stream_mid, vectors[2], vectors[3]
        )[1](grad_normed_two)
        grad_mid = grad_mid + grad_stream
        mid_low = grad_mid.astype(jnp.bfloat16)
        out_shard = scatter_matrix(weight_grad(mid_low, attended), 1)
        grad_att = dense(mid_low, out_full)
        grad_query, grad_key, grad_value = attend_back(
            query_low,
            key_low,
            value_low,
            valid,
            log_total,
            to_heads(grad_att.astype(jnp.bfloat16)),
        )
        grad_proj = jnp.stack(
            [from_heads(grad_query), from_heads(grad_key), from_heads(grad_value)], axis=2
        ).astype(jnp.bfloat16)
        grad_flat = grad_proj.reshape(seq_len, tp_count * 3 * half_width)
        qkv_shard = scatter_matrix(weight_grad(normed, grad_flat), 3)
        grad_normed = core_sum(dense_back(grad_flat, qkv_full))
        grad_in, grad_gain_one, grad_shift_one = jax.vjp(
            layer_norm, stream_in, vectors[0], vectors[1]
        )[1](grad_normed)
        grad_stream = grad_in + grad_mid
        matrix_grads[layer_index] = (
            qkv_shard,
            out_shard[:, 0].T,
            up_shard[:, 0],
            down_shard[:, 0].T,
        )
        row_grad = relative(
            jnp.stack(
                [
                    grad_gain_one,
                    grad_shift_one,
                    grad_gain_two,
                    grad_shift_two,
                    jnp.sum(mid_low, axis=0, dtype=jnp.float32),
                    jnp.sum(branch_low, axis=0, dtype=jnp.float32),
                ]
            ),
            1,
        )
        proj_sum = jnp.sum(grad_proj, axis=0, dtype=jnp.float32)
        pre_sum = jnp.sum(grad_pre, axis=0, dtype=jnp.float32).reshape(tp_count, half_hidden)

        def tp_rows(values):
            place = jnp.zeros_like(values)
            for d in range(tp_count):
                place = lax.dynamic_update_index_in_dim(
                    place, values[d], (tp_index + tp_count - d) % tp_count, 0
                )
            return place

        packed = jnp.concatenate(
            [
                row_grad.reshape(-1),
                tp_rows(proj_sum[:, 0]).reshape(-1),
                tp_rows(proj_sum[:, 2]).reshape(-1),
                tp_rows(pre_sum).reshape(-1),
            ]
        )
        vector_sums[layer_index] = vector_sum(packed)

    def own_block(values):
        mine = lax.dynamic_index_in_dim(values, tp_index, values.ndim - 2, keepdims=False)
        return by_core(mine, core_swap(mine), mine.ndim - 1)

    totals = jnp.stack(vector_sums)
    row_size = 6 * model_width
    qv_size = tp_count * half_width
    row_sum = totals[:, :row_size].reshape(LAYERS, 6, model_width)
    qv_total = own_block(
        totals[:, row_size : row_size + 2 * qv_size].reshape(LAYERS, 2, tp_count, half_width)
    )
    up_total = own_block(totals[:, row_size + 2 * qv_size :].reshape(LAYERS, tp_count, half_hidden))
    input_grad = image_blocks(relative(grad_stream.astype(jnp.bfloat16), 1)).astype(jnp.float32)
    qkv_grad = jnp.stack([layer_grads[0] for layer_grads in matrix_grads])
    out_grad = jnp.stack([layer_grads[1] for layer_grads in matrix_grads])
    up_grad = jnp.stack([layer_grads[2] for layer_grads in matrix_grads])
    down_grad = jnp.stack([layer_grads[3] for layer_grads in matrix_grads])
    qkv_new, qkv_moment_new, qkv_square_new = adamw_step(
        qkv_weight, qkv_moment, qkv_square, qkv_grad, D ** (-0.5), WEIGHT_DECAY
    )
    out_new, out_moment_new, out_square_new = adamw_step(
        out_weight, out_moment, out_square, out_grad, (D * 16 / SEQ) ** (-0.5), WEIGHT_DECAY
    )
    up_new, up_moment_new, up_square_new = adamw_step(
        up_weight, up_moment, up_square, up_grad, D ** (-0.5), WEIGHT_DECAY
    )
    down_new, down_moment_new, down_square_new = adamw_step(
        down_weight, down_moment, down_square, down_grad, FF ** (-0.5), WEIGHT_DECAY
    )
    row_new, row_moment_new, row_square_new = adamw_step(
        row_vectors, row_moment, row_square, row_sum, VECTOR_RATE, 0.0
    )
    qv_new, qv_moment_new, qv_square_new = adamw_step(
        qv_bias, qv_moment, qv_square, qv_total, VECTOR_RATE, 0.0
    )
    up_bias_new, bias_moment_new, bias_square_new = adamw_step(
        up_bias, bias_moment, bias_square, up_total, VECTOR_RATE, 0.0
    )
    return (
        activations,
        input_grad,
        qkv_new,
        qkv_moment_new,
        qkv_square_new,
        qkv_new.astype(jnp.bfloat16),
        out_new,
        out_moment_new,
        out_square_new,
        out_new.astype(jnp.bfloat16),
        up_new,
        up_moment_new,
        up_square_new,
        up_new.astype(jnp.bfloat16),
        down_new,
        down_moment_new,
        down_square_new,
        down_new.astype(jnp.bfloat16),
        row_new,
        row_moment_new,
        row_square_new,
        qv_new,
        qv_moment_new,
        qv_square_new,
        up_bias_new,
        bias_moment_new,
        bias_square_new,
    )


def solution(mesh):
    return jax.shard_map(
        shards,
        mesh=mesh,
        in_specs=(
            P("tp", "wide", None),
            P("tp", "wide", None),
            P("wide"),
            P(None, "wide", None, "tp"),
            P(None, "wide", None, "tp"),
            P(None, "wide", None, "tp"),
            P(None, "tp", "wide"),
            P(None, "tp", "wide"),
            P(None, "tp", "wide"),
            P(None, "wide", "tp"),
            P(None, "wide", "tp"),
            P(None, "wide", "tp"),
            P(None, "tp", "wide"),
            P(None, "tp", "wide"),
            P(None, "tp", "wide"),
            P(),
            P(),
            P(),
            P(None, None, "tp"),
            P(None, None, "tp"),
            P(None, None, "tp"),
            P(None, "tp"),
            P(None, "tp"),
            P(None, "tp"),
        ),
        out_specs=(
            P("tp", "wide", None),
            P("tp", "wide", None),
            P(None, "wide", None, "tp"),
            P(None, "wide", None, "tp"),
            P(None, "wide", None, "tp"),
            P(None, "wide", None, "tp"),
            P(None, "tp", "wide"),
            P(None, "tp", "wide"),
            P(None, "tp", "wide"),
            P(None, "tp", "wide"),
            P(None, "wide", "tp"),
            P(None, "wide", "tp"),
            P(None, "wide", "tp"),
            P(None, "wide", "tp"),
            P(None, "tp", "wide"),
            P(None, "tp", "wide"),
            P(None, "tp", "wide"),
            P(None, "tp", "wide"),
            P(),
            P(),
            P(),
            P(None, None, "tp"),
            P(None, None, "tp"),
            P(None, None, "tp"),
            P(None, "tp"),
            P(None, "tp"),
            P(None, "tp"),
        ),
        check_vma=False,
    )
```

```python
import functools

import jax
import jax.numpy as jnp
from jax import lax
from jax.experimental import pallas as pl
from jax.experimental.pallas import tpu as pltpu
from jax.sharding import PartitionSpec as P

D = 1024
HDIM = 64
FF = 4096
SEQ = 640
VALID = 577
LAYERS = 2
STEP = 10


NORM_EPS = 1e-05
BETA_ONE = 0.9
BETA_TWO = 0.999
ADAM_EPS = 1e-08
WEIGHT_DECAY = 0.01
VECTOR_RATE = 0.4
MASKED = -1e30
LOW = jnp.bfloat16
WIDE = jnp.float32
TILE = 128
MIB = 1 << 20

def adamw_step(weight, moment, square, gradient, step_rate, decay_rate):
    moment = BETA_ONE * moment + (1.0 - BETA_ONE) * gradient
    square = BETA_TWO * square + (1.0 - BETA_TWO) * gradient * gradient
    moment_hat = moment / (1.0 - BETA_ONE**STEP)
    square_hat = square / (1.0 - BETA_TWO**STEP)
    weight = weight - step_rate * (
        moment_hat / (jnp.sqrt(square_hat) + ADAM_EPS) + decay_rate * weight
    )
    return (weight, moment, square)


def core_swap(values):
    return lax.ppermute(values, "wide", [(i, i ^ 1) for i in range(lax.axis_size("wide"))])


def pair_swap(values, bit):
    flip = 2 << bit
    return lax.ppermute(values, "wide", [(i, i ^ flip) for i in range(lax.axis_size("wide"))])


def cross_swap(values, second):
    moves = [(i, i ^ (2 << ((i + second) % 2))) for i in range(lax.axis_size("wide"))]
    return lax.ppermute(values, "wide", moves)


def neighbours():
    pair, core = lax.axis_index("wide") // 2, lax.axis_index("wide") % 2
    return pair, pair ^ (1 << core), pair ^ (2 >> core), pair ^ 3


def tp_shift(values, distance):
    count = lax.axis_size("tp")
    return lax.ppermute(values, "tp", [(i, (i + distance) % count) for i in range(count)])


def tp_flip(values, bit):
    count = lax.axis_size("tp")
    return lax.ppermute(values, "tp", [(i, i ^ (1 << bit)) for i in range(count)])


class Move:
    def __init__(self, move, values):
        self.move, self.values, self.got = move, values, None

    def send(self, after=()):
        values = self.values
        if after:
            values, _ = lax.optimization_barrier((values, tuple(after)))
        self.got = self.move(values)
        return self.got


def first_way(values):
    return Move(lambda v: cross_swap(v, 0), values)


def second_way(values):
    return Move(lambda v: cross_swap(v, 1), values)


def along_tp(values, distance):
    return Move(lambda v: tp_shift(v, distance), values)


def behind(values, first):
    return lax.optimization_barrier((values, first))[0]


class Lane:
    def __init__(self):
        self.rounds = []

    def round(self, *moves, behind=1):
        after = self.rounds[-behind] if len(self.rounds) >= behind else ()
        self.rounds.append([move.send(after) for move in moves])


def pair_bits():
    return (lax.axis_size("wide") // 2).bit_length() - 1


def by_core(mine, other, axis):
    lower = lax.axis_index("wide") % 2 == 0
    return jnp.where(
        lower,
        jnp.concatenate([mine, other], axis=axis),
        jnp.concatenate([other, mine], axis=axis),
    )


def half_of(values, which, axis):
    span = values.shape[axis] // 2
    return lax.dynamic_slice_in_dim(values, which * span, span, axis)


def relative(values, axis):
    pairs = lax.axis_size("wide") // 2
    pair = lax.axis_index("wide") // 2
    span = values.shape[axis] // pairs
    shape = values.shape
    for bit in range(pair_bits()):
        step = span << bit
        split = values.reshape(shape[:axis] + (-1, 2, step) + shape[axis + 1 :])
        lower, upper = (lax.index_in_dim(split, k, axis + 1) for k in (0, 1))
        flipped = jnp.concatenate([upper, lower], axis=axis + 1).reshape(shape)
        values = jnp.where((pair >> bit) & 1 == 1, flipped, values)
    return values


def piece_places():
    if pair_bits() == 2:
        starts = [pair * (D // 4) for pair in neighbours()]
    else:
        starts = [0] * 4
    return jnp.stack([jnp.asarray(v, jnp.int32) for v in starts + [lax.axis_index("tp")]])


GATHERED = ((0, 4, 0), (0, 4, 1), (0, 4, 2), (0, 2, 3), (2, 2, 3))
SCATTERED = ((0, 4, 0), (0, 2, 1), (2, 2, 1), (0, 2, 2), (2, 2, 2), (0, 2, 3), (2, 2, 3))


def gathered_spans():
    return GATHERED if pair_bits() == 2 else ((0, lax.axis_size("tp"), 0),)


def scattered_spans():
    return SCATTERED if pair_bits() == 2 else ((0, lax.axis_size("tp"), 0),)


def tp_moves(block):
    return [along_tp(block, d) for d in range(1, lax.axis_size("tp"))]


def gather_plane(lane, own):
    if pair_bits() == 2:
        half = own.shape[0] // 2
        first, second = first_way(own), second_way(own)
        lane.round(first, second, behind=2)
        far = second_way(first.got[:half]), first_way(second.got[half:])
        lane.round(*far, behind=2)
        return [own, first.got, second.got] + [move.got for move in far]
    for bit in range(pair_bits()):
        own = jnp.concatenate([own, pair_swap(own, bit)], axis=1)
    return [relative(own, 1)]


def add_low(*terms):
    total = terms[0].astype(WIDE)
    for term in terms[1:]:
        total = total + term.astype(WIDE)
    return total


def own_sum_kernel(own, first_low, first_high, second_low, second_high, out):
    half = out.shape[0] // 2
    for d in range(out.shape[0]):
        first, second = (first_low, second_low) if d < half else (first_high, second_high)
        out[d] = add_low(own[d], first[d % half], second[d % half]).astype(LOW)


def scatter_plane(lane, pieces):
    if pair_bits() != 2:
        own = relative(pieces[0], 1)
        for bit in reversed(range(pair_bits())):
            keep = own.shape[1] // 2
            own = add_low(own[:, :keep], pair_swap(own[:, keep:], bit)).astype(LOW)
        return own
    own, first_low, first_high, second_low, second_high, far_low, far_high = pieces
    far_low, far_high = second_way(far_low), first_way(far_high)
    first_high, second_low = first_way(first_high), second_way(second_low)
    lane.round(far_low, far_high, behind=2)
    lane.round(first_high, second_low, behind=2)
    first_low = first_way(add_low(first_low, far_low.got).astype(LOW))
    second_high = second_way(add_low(second_high, far_high.got).astype(LOW))
    lane.round(first_low, second_high, behind=2)
    return pl.pallas_call(
        own_sum_kernel,
        out_shape=jax.ShapeDtypeStruct(own.shape, LOW),
        compiler_params=pltpu.CompilerParams(vmem_limit_bytes=24 * MIB),
        cost_estimate=cost(3),
    )(own, first_low.got, first_high.got, second_low.got, second_high.got)


def both_halves(total):
    core = lax.axis_index("wide") % 2
    other = core_swap(half_of(total, 1 - core, 0).astype(LOW))
    return half_of(total, core, 0).astype(WIDE), other.astype(WIDE)


def scatter_tp(blocks):
    return both_halves(lax.psum_scatter(blocks, "tp", scatter_dimension=0, tiled=False))


def by_source(got):
    tp_count = len(got)
    turned = jnp.stack(got[::-1] * 2)
    start = tp_count - 1 - lax.axis_index("tp")
    return lax.dynamic_slice_in_dim(turned, start, tp_count, 0)


class Exchange:
    def __init__(self, blocks):
        tp_index = lax.axis_index("tp")
        tp_count = lax.axis_size("tp")
        own, *others = (
            lax.dynamic_index_in_dim(blocks, (tp_index + d) % tp_count, 0, keepdims=False)
            for d in range(tp_count)
        )
        self.own = own
        self.moves = [along_tp(block, d + 1) for d, block in enumerate(others)]

    def result(self):
        return by_source([self.own] + [move.got for move in self.moves])


def image_parts(values):
    core = lax.axis_index("wide") % 2
    slots = jnp.stack([values[:, 0], values[:, 1]])
    other = core_swap(half_of(slots, 1 - core, 1))
    return Exchange(by_core(half_of(slots, core, 1), other, 0))


def image_rows(exchange):
    rows = exchange.result()
    return by_core(rows, core_swap(rows), 1).reshape(-1, rows.shape[2])


def group_parts(values):
    core = lax.axis_index("wide") % 2
    blocks = values.reshape(lax.axis_size("tp"), -1, values.shape[1])
    return Exchange(half_of(blocks, core, 1))


def group_rows(exchange):
    core = lax.axis_index("wide") % 2
    images = exchange.result()
    other = core_swap(half_of(images, 1 - core, 0))
    slots = by_core(half_of(images, core, 0), other, 1)
    return jnp.stack([slots[0], slots[1]], axis=1)


def vector_sum(values):
    for bit in range(lax.axis_size("tp").bit_length() - 1):
        values = values + tp_flip(values, bit)
    for bit in range(pair_bits()):
        values = values + pair_swap(values, bit)
    return values


def cost(time):
    return pl.CostEstimate(
        flops=int(time * 1.1e9), bytes_accessed=int(time * 3.4e6), transcendentals=0
    )


SCALARS = pl.BlockSpec(memory_space=pltpu.SMEM)
FAR = pl.BlockSpec(memory_space=pl.ANY)


def whole(shape):
    return pl.BlockSpec(shape, lambda *_: (0,) * len(shape))


def mat(left, right):
    return jnp.dot(left, right, preferred_element_type=WIDE)


def mat_back(left, right):
    return lax.dot_general(left, right, (((1,), (1,)), ((), ())), preferred_element_type=WIDE)


def flip(values):
    return values.T


def fetch(places, refs, held, sems, column, width, turned=False):
    copies = []
    for ref, (first, span, place) in zip(refs, gathered_spans()):
        rows = pl.ds(pl.multiple_of(places[place], TILE), ref.shape[1])
        columns = pl.ds(column, width)
        if turned:
            total = held.shape[0]
            for z in range(span):
                block = lax.rem(places[4] + (total - first - z), total)
                copies.append((ref.at[z, :, columns], held.at[block, rows, :]))
        else:
            copies.append((ref.at[:, :, columns], held.at[pl.ds(first, span), rows, :]))
    return [pltpu.make_async_copy(*pair, sems.at[k]) for k, pair in enumerate(copies)]


def fetch_joined(places, refs, held, sems, column, width):
    copies = []
    for ref, (first, span, place) in zip(refs, gathered_spans()):
        rows = pl.ds(pl.multiple_of(places[place], TILE), ref.shape[1])
        for z in range(span):
            there = held.at[rows, pl.ds((first + z) * width, width)]
            copies.append((ref.at[z, :, pl.ds(column, width)], there))
    return [pltpu.make_async_copy(*pair, sems.at[k]) for k, pair in enumerate(copies)]


def start_all(copies):
    for copy in copies:
        copy.start()


def wait_all(copies):
    for copy in copies:
        copy.wait()


def norm_parts(values):
    center = values - jnp.mean(values, axis=-1, keepdims=True)
    scale = lax.rsqrt(jnp.mean(center * center, axis=-1, keepdims=True) + NORM_EPS)
    return center * scale, scale


def norm_back(values, gain, grad):
    unit, scale = norm_parts(values)
    scaled = grad * gain
    inner = scaled - jnp.mean(scaled, axis=-1, keepdims=True)
    inner = inner - unit * jnp.mean(scaled * unit, axis=-1, keepdims=True)
    return (
        inner * scale,
        jnp.sum(grad * unit, axis=0, keepdims=True),
        jnp.sum(grad, axis=0, keepdims=True),
    )


def pack_attn_kernel(core, qkv, out, mine, other):
    half = qkv.shape[3] // 2

    def put(ref, first):
        for kind in range(3):
            ref[:, kind * half : (kind + 1) * half] = qkv[
                0, :, kind, first * half : (first + 1) * half
            ].astype(LOW)
        ref[:, 3 * half :] = out[0, first * half : (first + 1) * half, :].T.astype(LOW)

    @pl.when(core[0] == 0)
    def _():
        put(mine, 0)
        put(other, 1)

    @pl.when(core[0] == 1)
    def _():
        put(mine, 1)
        put(other, 0)


def pack_mlp_kernel(core, up, down, mine, other):
    half = up.shape[2] // 2

    def put(ref, first):
        ref[:, :half] = up[0, :, first * half : (first + 1) * half].astype(LOW)
        ref[:, half:] = down[0, first * half : (first + 1) * half, :].T.astype(LOW)

    @pl.when(core[0] == 0)
    def _():
        put(mine, 0)
        put(other, 1)

    @pl.when(core[0] == 1)
    def _():
        put(mine, 1)
        put(other, 0)


def layer_block(array, layer):
    shape = (1,) + array.shape[1:]
    return pl.BlockSpec(shape, lambda *_: (layer,) + (0,) * (len(shape) - 1))


def pack(kernel, layer, core, first, second, columns):
    rows = lax.axis_size("wide")
    shape = jax.ShapeDtypeStruct((D // rows, columns), LOW)
    return pl.pallas_call(
        kernel,
        grid=(1,),
        in_specs=[SCALARS, layer_block(first, layer), layer_block(second, layer)],
        out_specs=[whole(shape.shape)] * 2,
        out_shape=[shape] * 2,
        compiler_params=pltpu.CompilerParams(vmem_limit_bytes=16 * MIB),
        cost_estimate=cost(1),
    )(core, first, second)


def project_kernel(layer, joined, places, *refs):
    if joined:
        stream, own, got, vectors, bias, *refs = refs
        *weights, kept, normed, proj, held, sems = refs
    else:
        stream, vectors, bias, *refs = refs
        *weights, normed, proj, held, sems = refs
    width = held.shape[2]
    copies = fetch(places, weights, held, sems, 0, width)
    pl.when(pl.program_id(0) == 0)(lambda: start_all(copies))
    values = stream[...].astype(WIDE)
    if joined:
        values = values + (add_low(own[...], got[...]) + vectors[layer - 1, 5:6, :])
        kept[...] = values
    low = (norm_parts(values)[0] * vectors[layer, 0:1, :] + vectors[layer, 1:2, :]).astype(LOW)
    normed[...] = low
    pl.when(pl.program_id(0) == 0)(lambda: wait_all(copies))
    for z in range(held.shape[0]):
        here = slice(z * width, (z + 1) * width)
        proj[:, here] = (mat(low, held[z]) + bias[:, here]).astype(LOW)


def project(layer, stream, partial, vectors, bias, places, pieces):
    rows = stream.shape[0]
    steps = 2
    tp_count = lax.axis_size("tp")
    columns = bias.shape[1]
    tile = pl.BlockSpec((rows // steps, D), lambda i: (i, 0))
    streams = [stream] + list(partial)
    out_shape = [
        jax.ShapeDtypeStruct((rows, D), LOW),
        jax.ShapeDtypeStruct((rows, columns), LOW),
    ]
    out_specs = [tile, pl.BlockSpec((rows // steps, columns), lambda i: (i, 0))]
    if partial:
        out_shape = [jax.ShapeDtypeStruct((rows, D), WIDE)] + out_shape
        out_specs = [tile] + out_specs
    return pl.pallas_call(
        functools.partial(project_kernel, layer, bool(partial)),
        grid=(steps,),
        in_specs=[SCALARS]
        + [tile] * len(streams)
        + [whole(vectors.shape), whole(bias.shape)]
        + [FAR] * len(pieces),
        out_specs=out_specs,
        out_shape=out_shape,
        scratch_shapes=[
            pltpu.VMEM((tp_count, D, columns // tp_count), LOW),
            pltpu.SemaphoreType.DMA((len(pieces),)),
        ],
        compiler_params=pltpu.CompilerParams(vmem_limit_bytes=40 * MIB),
        cost_estimate=cost(6),
    )(places, *streams, vectors, bias, *pieces)


def head_rows(values):
    turned = flip(values)
    upper = lax.broadcasted_iota(jnp.int32, turned.shape, 0) < HDIM
    zero = jnp.zeros_like(turned)
    return jnp.where(upper, turned, zero), jnp.where(upper, zero, turned)


def put_head_rows(held, values):
    first, second = head_rows(values)
    for t in range(held.shape[0]):
        held[t, :, :TILE] = first[:, t * TILE : (t + 1) * TILE]
        held[t, :, TILE:] = second[:, t * TILE : (t + 1) * TILE]


def put_head_columns(held, values):
    left = lax.broadcasted_iota(jnp.int32, values.shape, 1) < HDIM
    zero = jnp.zeros_like(values)
    first, second = jnp.where(left, values, zero), jnp.where(left, zero, values)
    for t in range(held.shape[0]):
        held[t, :TILE, :] = first[t * TILE : (t + 1) * TILE, :]
        held[t, TILE:, :] = second[t * TILE : (t + 1) * TILE, :]


def merge_heads(values):
    upper = lax.broadcasted_iota(jnp.int32, (2 * HDIM, TILE), 0) < HDIM
    return jnp.where(upper, values[:, :TILE], values[:, TILE:]).T


def attend_kernel(places, proj, mask, *refs):
    *weights, attended, totals, partial, held_out, held_att, turned, sems = refs
    z = pl.program_id(0)
    width = 2 * HDIM
    tiles = turned.shape[0]
    copies = fetch_joined(places, weights, held_out, sems, 3 * width, width)
    pl.when(z == 0)(lambda: start_all(copies))
    put_head_rows(turned, proj[:, :width] * LOW(HDIM**-0.5))
    value_rows = flip(proj[:, 2 * width :])
    key_rows = proj[:, width : 2 * width]

    def one(t, carried):
        scores = mat(key_rows, turned[t]) + jnp.concatenate([mask[...], mask[...]], axis=1)
        highest = jnp.max(scores, axis=0, keepdims=True)
        exponent = jnp.exp(scores - highest)
        total = jnp.sum(exponent, axis=0, keepdims=True)
        probs = (exponent * (1.0 / total)).astype(LOW)
        totals[0, pl.ds(t, 1), :] = highest + jnp.log(total)
        result = merge_heads(mat(value_rows, probs)).astype(LOW)
        attended[pl.ds(pl.multiple_of(t * TILE, TILE), TILE), :] = result
        return carried

    lax.fori_loop(0, tiles, one, 0)
    for k in range(held_att.shape[1] // width):

        @pl.when(z == k)
        def _():
            held_att[:, k * width : (k + 1) * width] = attended[...]

    @pl.when(z == pl.num_programs(0) - 1)
    def _():
        wait_all(copies)
        partial[...] = mat_back(held_att[...], held_out[...]).astype(LOW)


def attend(proj, mask, places, pieces):
    rows = proj.shape[0]
    tp_count = lax.axis_size("tp")
    width = 2 * HDIM
    tiles = rows // TILE
    return pl.pallas_call(
        attend_kernel,
        grid=(tp_count,),
        in_specs=[SCALARS, pl.BlockSpec((rows, 3 * width), lambda z: (0, z)), whole(mask.shape)]
        + [FAR] * len(pieces),
        out_specs=[
            pl.BlockSpec((rows, width), lambda z: (0, z)),
            pl.BlockSpec((1, tiles, 2 * TILE), lambda z: (z, 0, 0)),
            whole((rows, D)),
        ],
        out_shape=[
            jax.ShapeDtypeStruct((rows, tp_count * width), LOW),
            jax.ShapeDtypeStruct((tp_count, tiles, 2 * TILE), WIDE),
            jax.ShapeDtypeStruct((rows, D), LOW),
        ],
        scratch_shapes=[
            pltpu.VMEM((D, tp_count * width), LOW),
            pltpu.VMEM((rows, tp_count * width), LOW),
            pltpu.VMEM((tiles, width, 2 * TILE), LOW),
            pltpu.SemaphoreType.DMA((tp_count * len(pieces),)),
        ],
        compiler_params=pltpu.CompilerParams(vmem_limit_bytes=40 * MIB),
        cost_estimate=cost(18),
    )(places, proj, mask, *pieces)


def mlp_kernel(layer, turned, places, stream, own, got, vectors, bias, *refs):
    *weights, middle, normed, pre_act, hidden, partial, held_up, held_down, sems = refs
    width = held_up.shape[2]
    ups = fetch(places, weights, held_up, sems.at[0], 0, width, turned)
    downs = fetch(places, weights, held_down, sems.at[1], width, width, turned)
    first = pl.program_id(0) == 0
    pl.when(first)(lambda: start_all(ups))
    pl.when(first)(lambda: start_all(downs))
    values = stream[...].astype(WIDE) + (
        add_low(own[...], got[...]) + vectors[layer, 4:5, :]
    )
    middle[...] = values
    low = (norm_parts(values)[0] * vectors[layer, 2:3, :] + vectors[layer, 3:4, :]).astype(LOW)
    normed[...] = low
    total = None
    pl.when(first)(lambda: wait_all(ups))
    for z in range(held_up.shape[0]):
        here = slice(z * width, (z + 1) * width)
        pre = mat(low, held_up[z]) + bias[:, here]
        pre_act[:, here] = pre
        act = (pre / (1.0 + jnp.exp(-1.702 * pre))).astype(LOW)
        hidden[:, here] = act
        if z == 0:
            pl.when(first)(lambda: wait_all(downs))
        term = mat_back(act, held_down[z])
        total = term if total is None else total + term
    partial[...] = total.astype(LOW)


def mlp(layer, stream, partial, vectors, bias, places, pieces, turned):
    rows = stream.shape[0]
    steps = 2
    tp_count = lax.axis_size("tp")
    columns = bias.shape[1]
    tile = pl.BlockSpec((rows // steps, D), lambda i: (i, 0))
    broad = pl.BlockSpec((rows // steps, columns), lambda i: (i, 0))
    held = pltpu.VMEM((tp_count, D, columns // tp_count), LOW)
    return pl.pallas_call(
        functools.partial(mlp_kernel, layer, turned),
        grid=(steps,),
        in_specs=[SCALARS]
        + [tile] * 3
        + [whole(vectors.shape), whole(bias.shape)]
        + [FAR] * len(pieces),
        out_specs=[tile, tile, broad, broad, tile],
        out_shape=[
            jax.ShapeDtypeStruct((rows, D), WIDE),
            jax.ShapeDtypeStruct((rows, D), LOW),
            jax.ShapeDtypeStruct((rows, columns), WIDE),
            jax.ShapeDtypeStruct((rows, columns), LOW),
            jax.ShapeDtypeStruct((rows, D), LOW),
        ],
        scratch_shapes=[held, held, pltpu.SemaphoreType.DMA((2, tp_count * len(pieces)))],
        compiler_params=pltpu.CompilerParams(vmem_limit_bytes=52 * MIB),
        cost_estimate=cost(15),
    )(places, stream, *partial, vectors, bias, *pieces)


def put_pieces(places, held, outs, shape, columns=slice(None)):
    z = pl.program_id(0)
    for out, (first, span, place) in zip(outs, shape):

        @pl.when((z >= first) & (z < first + span))
        def _():
            rows = pl.ds(pl.multiple_of(places[place], TILE), out.shape[1])
            out[0, :, columns] = held[rows, :]


def mlp_back_kernel(
    count, turned, places, grad, normed, hidden, pre_act, *refs
):
    weights, refs = refs[:count], refs[count:]
    outs, refs = refs[: len(scattered_spans())], refs[len(scattered_spans()) :]
    partial, bias_sum, row_sum, *refs = refs
    held_up, held_down, low, low_turned, normed_turned, result, total, sems = refs
    z = pl.program_id(0)
    width = held_up.shape[2]
    downs = fetch(places, weights, held_down, sems.at[1], width, width, turned)
    ups = fetch(places, weights, held_up, sems.at[0], 0, width, turned)

    @pl.when(z == 0)
    def _():
        start_all(downs)
        start_all(ups)
        values = grad[...].astype(LOW)
        low[...] = values
        low_turned[...] = flip(values)
        normed_turned[...] = flip(normed[...])
        row_sum[...] = jnp.sum(values.astype(WIDE), axis=0, keepdims=True)

    result[...] = mat(low_turned[...], hidden[...]).astype(LOW)
    put_pieces(places, result, outs, scattered_spans(), slice(width, 2 * width))
    pl.when(z == 0)(lambda: wait_all(downs))
    pl.when(z == 0)(lambda: wait_all(ups))
    pre = pre_act[...]
    gate = 1.0 / (1.0 + jnp.exp(-1.702 * pre))
    slope = gate * (1.0 + 1.702 * pre * (1.0 - gate))
    grad_pre = (mat(low[...], held_down[z]) * slope).astype(LOW)
    bias_sum[0] = jnp.sum(grad_pre.astype(WIDE), axis=0, keepdims=True)
    result[...] = mat(normed_turned[...], grad_pre).astype(LOW)
    put_pieces(places, result, outs, scattered_spans(), slice(0, width))
    term = mat_back(grad_pre, held_up[z])

    @pl.when(z == 0)
    def _():
        total[...] = term

    @pl.when(z > 0)
    def _():
        total[...] += term

    @pl.when(z == pl.num_programs(0) - 1)
    def _():
        partial[...] = total[...].astype(LOW)


def piece_outs(width):
    spans = scattered_spans()
    rows = D // 4 if len(spans) > 1 else D

    def spec(first, span):
        return pl.BlockSpec((1, rows, width), lambda z: (jnp.clip(z - first, 0, span - 1), 0, 0))

    shapes = [jax.ShapeDtypeStruct((span, rows, width), LOW) for _, span, _ in spans]
    return shapes, [spec(first, span) for first, span, _ in spans]


def mlp_back(grad, normed, hidden, pre_act, places, pieces, turned):
    rows = grad.shape[0]
    tp_count = lax.axis_size("tp")
    columns = hidden.shape[1]
    width = columns // tp_count
    shapes, specs = piece_outs(2 * width)
    block = pl.BlockSpec((rows, width), lambda z: (0, z))
    held = pltpu.VMEM((tp_count, D, width), LOW)
    outs = pl.pallas_call(
        functools.partial(mlp_back_kernel, len(pieces), turned),
        grid=(tp_count,),
        in_specs=[SCALARS, whole((rows, D)), whole((rows, D)), block, block]
        + [FAR] * len(pieces),
        out_specs=specs
        + [
            whole((rows, D)),
            pl.BlockSpec((1, 1, width), lambda z: (z, 0, 0)),
            whole((1, D)),
        ],
        out_shape=shapes
        + [
            jax.ShapeDtypeStruct((rows, D), LOW),
            jax.ShapeDtypeStruct((tp_count, 1, width), WIDE),
            jax.ShapeDtypeStruct((1, D), WIDE),
        ],
        scratch_shapes=[
            held,
            held,
            pltpu.VMEM((rows, D), LOW),
            pltpu.VMEM((D, rows), LOW),
            pltpu.VMEM((D, rows), LOW),
            pltpu.VMEM((D, width), LOW),
            pltpu.VMEM((rows, D), WIDE),
            pltpu.SemaphoreType.DMA((2, tp_count * len(pieces))),
        ],
        compiler_params=pltpu.CompilerParams(vmem_limit_bytes=56 * MIB),
        cost_estimate=cost(25),
    )(places, grad, normed, hidden, pre_act, *pieces)
    return outs[:-3], *outs[-3:]


def middle_back_kernel(
    layer, count, places, grad, own, got, middle, vectors, attended, *refs
):
    weights, refs = refs[:count], refs[count:]
    grad_out, grad_mid, grad_att, sums, held, low, kept_sums, sems = refs
    step = pl.program_id(0)
    width = 2 * HDIM
    copies = fetch_joined(places, weights, held, sems, 3 * width, width)
    pl.when(step == 0)(lambda: start_all(copies))
    back, gain_sum, shift_sum = norm_back(
        middle[...], vectors[layer, 2:3, :], add_low(own[...], got[...])
    )
    values = grad[...] + back
    grad_mid[...] = values
    values = values.astype(LOW)
    tile = values.shape[0]
    low[pl.ds(pl.multiple_of(step * tile, tile), tile), :] = values
    parts = jnp.concatenate(
        [gain_sum, shift_sum, jnp.sum(values.astype(WIDE), axis=0, keepdims=True)], axis=0
    )

    @pl.when(step == 0)
    def _():
        kept_sums[0:3, :] = parts

    @pl.when(step > 0)
    def _():
        kept_sums[0:3, :] += parts

    @pl.when(step == pl.num_programs(0) - 1)
    def _():
        sums[...] = kept_sums[...]
        grad_out[...] = mat(flip(low[...]), attended[...]).astype(LOW)
        wait_all(copies)
        grad_att[...] = mat(low[...], held[...]).astype(LOW)


def middle_back(
    layer, grad, partial, middle, vectors, attended, places, pieces
):
    rows = grad.shape[0]
    steps = 4
    tp_count = lax.axis_size("tp")
    columns = attended.shape[1]
    tile = pl.BlockSpec((rows // steps, D), lambda i: (i, 0))
    outs = pl.pallas_call(
        functools.partial(middle_back_kernel, layer, len(pieces)),
        grid=(steps,),
        in_specs=[SCALARS]
        + [tile] * 4
        + [whole(vectors.shape), whole((rows, columns))]
        + [FAR] * len(pieces),
        out_specs=[whole((D, columns)), tile, whole((rows, columns)), whole((8, D))],
        out_shape=[
            jax.ShapeDtypeStruct((D, columns), LOW),
            jax.ShapeDtypeStruct((rows, D), WIDE),
            jax.ShapeDtypeStruct((rows, columns), LOW),
            jax.ShapeDtypeStruct((8, D), WIDE),
        ],
        scratch_shapes=[
            pltpu.VMEM((D, columns), LOW),
            pltpu.VMEM((rows, D), LOW),
            pltpu.VMEM((8, D), WIDE),
            pltpu.SemaphoreType.DMA((tp_count * len(pieces),)),
        ],
        compiler_params=pltpu.CompilerParams(vmem_limit_bytes=48 * MIB),
        cost_estimate=cost(9),
    )(places, grad, *partial, middle, vectors, attended, *pieces)
    return outs


def attend_back_kernel(
    count, places, proj, mask, totals, grad_att, normed, grad_out, *refs
):
    weights, refs = refs[:count], refs[count:]
    outs, refs = refs[: len(scattered_spans())], refs[len(scattered_spans()) :]
    (
        partial,
        sums,
        held,
        normed_turned,
        query_rows,
        grad_rows,
        query_columns,
        grad_columns,
        grad_proj,
        result,
        total,
        key_sum,
        value_sum,
        key_turned,
        sems,
    ) = refs
    z = pl.program_id(0)
    width = 2 * HDIM
    tiles = query_rows.shape[0]
    copies = fetch(places, weights, held, sems, 0, 3 * width)

    @pl.when(z == 0)
    def _():
        start_all(copies)
        normed_turned[...] = flip(normed[...])

    scaled = proj[:, :width] * LOW(HDIM**-0.5)
    put_head_rows(query_rows, scaled)
    put_head_columns(query_columns, scaled)
    put_head_rows(grad_rows, grad_att[...])
    put_head_columns(grad_columns, grad_att[...])
    key_rows = proj[:, width : 2 * width]
    value_rows = proj[:, 2 * width :]
    key_turned[...] = flip(key_rows)
    key_sum[...] = jnp.zeros_like(key_sum)
    value_sum[...] = jnp.zeros_like(value_sum)

    def one(t, carried):
        scores = mat(key_rows, query_rows[t]) + jnp.concatenate([mask[...], mask[...]], axis=1)
        probs = jnp.exp(scores - totals[0, pl.ds(t, 1), :])
        value_sum[...] += mat(probs.astype(LOW), grad_columns[t])
        grad_probs = mat(value_rows, grad_rows[t])
        inner = jnp.sum(probs * grad_probs, axis=0, keepdims=True)
        grad_scores = (probs * (grad_probs - inner)).astype(LOW)
        key_sum[...] += mat(grad_scores, query_columns[t])
        grad_query = merge_heads(mat(key_turned[...], grad_scores)) * HDIM**-0.5
        grad_proj[pl.ds(pl.multiple_of(t * TILE, TILE), TILE), :width] = grad_query.astype(LOW)
        return carried

    lax.fori_loop(0, tiles, one, 0)
    grad_proj[:, width : 2 * width] = key_sum[...].astype(LOW)
    grad_proj[:, 2 * width :] = value_sum[...].astype(LOW)
    grads = grad_proj[...]
    sums[0] = jnp.sum(grads.astype(WIDE), axis=0, keepdims=True)
    result[...] = mat(normed_turned[...], grads).astype(LOW)
    put_pieces(places, result, outs, scattered_spans(), slice(0, 3 * width))
    put_pieces(places, grad_out, outs, scattered_spans(), slice(3 * width, 4 * width))
    pl.when(z == 0)(lambda: wait_all(copies))
    term = mat_back(grads, held[z])

    @pl.when(z == 0)
    def _():
        total[...] = term

    @pl.when(z > 0)
    def _():
        total[...] += term

    @pl.when(z == pl.num_programs(0) - 1)
    def _():
        partial[...] = total[...].astype(LOW)


def attend_back(
    proj, mask, totals, grad_att, normed, grad_out, places, pieces
):
    rows = proj.shape[0]
    tp_count = lax.axis_size("tp")
    width = 2 * HDIM
    tiles = rows // TILE
    shapes, specs = piece_outs(4 * width)
    outs = pl.pallas_call(
        functools.partial(attend_back_kernel, len(pieces)),
        grid=(tp_count,),
        in_specs=[
            SCALARS,
            pl.BlockSpec((rows, 3 * width), lambda z: (0, z)),
            whole(mask.shape),
            pl.BlockSpec((1, tiles, 2 * TILE), lambda z: (z, 0, 0)),
            pl.BlockSpec((rows, width), lambda z: (0, z)),
            whole((rows, D)),
            pl.BlockSpec((D, width), lambda z: (0, z)),
        ]
        + [FAR] * len(pieces),
        out_specs=specs
        + [whole((rows, D)), pl.BlockSpec((1, 1, 3 * width), lambda z: (z, 0, 0))],
        out_shape=shapes
        + [
            jax.ShapeDtypeStruct((rows, D), LOW),
            jax.ShapeDtypeStruct((tp_count, 1, 3 * width), WIDE),
        ],
        scratch_shapes=[
            pltpu.VMEM((tp_count, D, 3 * width), LOW),
            pltpu.VMEM((D, rows), LOW),
            pltpu.VMEM((tiles, width, 2 * TILE), LOW),
            pltpu.VMEM((tiles, width, 2 * TILE), LOW),
            pltpu.VMEM((tiles, 2 * TILE, width), LOW),
            pltpu.VMEM((tiles, 2 * TILE, width), LOW),
            pltpu.VMEM((rows, 3 * width), LOW),
            pltpu.VMEM((D, 3 * width), LOW),
            pltpu.VMEM((rows, D), WIDE),
            pltpu.VMEM((rows, width), WIDE),
            pltpu.VMEM((rows, width), WIDE),
            pltpu.VMEM((width, rows), LOW),
            pltpu.SemaphoreType.DMA((len(pieces),)),
        ],
        compiler_params=pltpu.CompilerParams(vmem_limit_bytes=48 * MIB),
        cost_estimate=cost(31),
    )(places, proj, mask, totals, grad_att, normed, grad_out, *pieces)
    return outs[:-2], *outs[-2:]


def input_back_kernel(layer, grad, own, got, stream, vectors, grad_in, sums, kept):
    back, gain_sum, shift_sum = norm_back(
        stream[...].astype(WIDE), vectors[layer, 0:1, :], add_low(own[...], got[...])
    )
    grad_in[...] = (grad[...] + back).astype(grad_in.dtype)
    parts = jnp.concatenate([gain_sum, shift_sum], axis=0)

    @pl.when(pl.program_id(0) == 0)
    def _():
        kept[0:2, :] = parts

    @pl.when(pl.program_id(0) > 0)
    def _():
        kept[0:2, :] += parts

    sums[...] = kept[...]


def input_back(layer, grad, partial, stream, vectors, dtype):
    rows = grad.shape[0]
    steps = 4
    tile = pl.BlockSpec((rows // steps, D), lambda i: (i, 0))
    return pl.pallas_call(
        functools.partial(input_back_kernel, layer),
        grid=(steps,),
        in_specs=[tile] * 4 + [whole(vectors.shape)],
        out_specs=[tile, whole((8, D))],
        out_shape=[jax.ShapeDtypeStruct((rows, D), dtype), jax.ShapeDtypeStruct((8, D), WIDE)],
        scratch_shapes=[pltpu.VMEM((8, D), WIDE)],
        compiler_params=pltpu.CompilerParams(vmem_limit_bytes=24 * MIB),
        cost_estimate=cost(4),
    )(grad, *partial, stream, vectors)


def shards(
    tokens,
    cotangent,
    counts,
    qkv_weight,
    qkv_moment,
    qkv_square,
    out_weight,
    out_moment,
    out_square,
    up_weight,
    up_moment,
    up_square,
    down_weight,
    down_moment,
    down_square,
    row_vectors,
    row_moment,
    row_square,
    qv_bias,
    qv_moment,
    qv_square,
    up_bias,
    bias_moment,
    bias_square,
):
    row_count, slot_count, model_width = tokens.shape
    tp_count = lax.axis_size("tp")
    seq_len = row_count * tp_count
    half_width = qkv_weight.shape[3] // 2
    half_hidden = up_weight.shape[2] // 2
    core = lax.axis_index("wide") % 2
    tp_index = lax.axis_index("tp")
    core_scalar = core.astype(jnp.int32).reshape(1)

    group_count = jnp.where(tp_index // slot_count == core, counts, core_swap(counts))[0]
    live = (tp_index % slot_count) < group_count
    valid = (lax.iota(jnp.int32, seq_len) < VALID) & live
    mask = jnp.broadcast_to(jnp.where(valid, 0.0, MASKED)[:, None], (seq_len, TILE))

    own_bias = jnp.concatenate(
        [half_of(qv_bias, core, 2).reshape(-1), half_of(up_bias, core, 1).reshape(-1)]
    )
    bias_moves = tp_moves(own_bias)
    bias_blocks = by_source([own_bias] + [move.send() for move in bias_moves])
    qv_size = LAYERS * 2 * half_width
    qv_blocks = bias_blocks[:, :qv_size].reshape(tp_count, LAYERS, 2, half_width)
    up_blocks = bias_blocks[:, qv_size:].reshape(tp_count, LAYERS, half_hidden)

    places = piece_places()
    plane, line = Lane(), Lane()

    def bundle_rows(kernel, layer, first, second, columns):
        mine, other = pack(kernel, layer, core_scalar, first, second, columns)
        return by_core(mine, core_swap(other), 0)

    owns = []
    for layer in range(LAYERS):
        owns.append(
            bundle_rows(pack_attn_kernel, layer, qkv_weight, out_weight, 4 * half_width)
        )
        owns.append(
            bundle_rows(pack_mlp_kernel, layer, up_weight, down_weight, 2 * half_hidden)
        )
    token_parts, grad_parts = image_parts(tokens), image_parts(cotangent)
    near, across, back = (0, 1, 2)
    attn_first = lax.all_gather(owns[0], "tp")
    moves = tp_moves(owns[1])
    line.round(moves[near], moves[back])
    line.round(moves[across])
    line.round(token_parts.moves[near], token_parts.moves[back])
    line.round(token_parts.moves[across])
    wide_first = jnp.stack([owns[1]] + [move.got for move in moves])
    second_layer = behind(jnp.concatenate(owns[2:], axis=1), line.rounds[1][0])
    second_layer = lax.all_gather(second_layer, "tp")
    attn_columns = owns[2].shape[1]
    line.round(grad_parts.moves[near], grad_parts.moves[back])
    line.round(grad_parts.moves[across])
    pieces_of = [
        gather_plane(plane, rows)
        for rows in (
            attn_first,
            wide_first,
            second_layer[:, :, :attn_columns],
            second_layer[:, :, attn_columns:],
        )
    ]
    bundles = [(pieces_of[2 * k], pieces_of[2 * k + 1]) for k in range(LAYERS)]
    stream = image_rows(token_parts)
    grad = jnp.where(valid[:, None], image_rows(grad_parts).astype(WIDE), 0.0)

    partial = []
    stored = []
    for layer in range(LAYERS):
        attn, wide = bundles[layer]
        qv_layer = qv_blocks[:, layer]
        proj_bias = jnp.stack(
            [qv_layer[:, 0], jnp.zeros_like(qv_layer[:, 0]), qv_layer[:, 1]], axis=1
        ).reshape(1, -1)
        made = project(layer, stream, partial, row_vectors, proj_bias, places, attn)
        if partial:
            stream, normed, proj = made
        else:
            normed, proj = made
        if layer:
            proj = behind(proj, grad)
        attended, totals, part = attend(proj, mask, places, attn)
        middle, normed_two, pre_act, hidden, part = mlp(
            layer,
            stream,
            (part, core_swap(part)),
            row_vectors,
            up_blocks[:, layer].reshape(1, -1),
            places,
            wide,
            layer == 0,
        )
        partial = (part, core_swap(part))
        stored.append((stream, normed, proj, attended, totals, middle, normed_two, pre_act, hidden))
        stream = middle
    last = stream + (add_low(*partial) + row_vectors[LAYERS - 1, 5])
    last_parts = group_parts(jnp.where(valid[:, None], last, 0.0).astype(LOW))

    matrix_grads = [None] * LAYERS
    vector_grads = [None] * LAYERS
    pending = [None] * LAYERS
    line.round(last_parts.moves[near], last_parts.moves[back])
    line.round(last_parts.moves[across])
    for layer in reversed(range(LAYERS)):
        attn, wide = bundles[layer]
        stream, normed, proj, attended, totals, middle, normed_two, pre_act, hidden = stored[layer]
        wide_pieces, part, bias_sum, last_sum = mlp_back(
            grad, normed_two, hidden, pre_act, places, wide, layer == 0
        )
        wide_grad = scatter_tp(scatter_plane(plane, wide_pieces))
        grad_out, grad_mid, grad_att, middle_sums = middle_back(
            layer,
            grad,
            (part, core_swap(part)),
            middle,
            row_vectors,
            attended,
            places,
            attn,
        )
        attn_pieces, part, proj_sums = attend_back(
            proj, mask, totals, grad_att, normed, grad_out, places, attn
        )
        attn_blocks = scatter_plane(plane, attn_pieces)
        if layer:
            attn_grad = scatter_tp(attn_blocks)
        else:
            attn_grad = None
        pending[layer] = (wide_grad, attn_grad)
        grad, input_sums = input_back(
            layer, grad_mid, (part, core_swap(part)), stream, row_vectors, WIDE if layer else LOW
        )
        proj_sums = proj_sums.reshape(tp_count, 3, half_width)
        vector_grads[layer] = jnp.concatenate(
            [
                input_sums[:2].reshape(-1),
                middle_sums[:3].reshape(-1),
                last_sum.reshape(-1),
                proj_sums[:, 0].reshape(-1),
                proj_sums[:, 2].reshape(-1),
                bias_sum[:, 0].reshape(-1),
            ]
        )
    grad_out_parts = group_parts(grad)
    line.round(grad_out_parts.moves[near], grad_out_parts.moves[back])
    line.round(grad_out_parts.moves[across])
    parts = Exchange(attn_blocks)
    line.round(*parts.moves)
    terms = [parts.own] + [move.got for move in parts.moves]
    pending[0] = (pending[0][0], both_halves(add_low(*terms)))
    activations = group_rows(last_parts)
    input_grad = group_rows(grad_out_parts).astype(WIDE)
    for layer in range(LAYERS):
        wide_grad, attn_grad = pending[layer]
        out_start = 3 * half_width
        matrix_grads[layer] = (
            by_core(*[v[:, :out_start].reshape(-1, 3, half_width) for v in attn_grad], 2),
            by_core(*[v[:, out_start:] for v in attn_grad], 1).T,
            by_core(*[v[:, :half_hidden] for v in wide_grad], 1),
            by_core(*[v[:, half_hidden:] for v in wide_grad], 1).T,
        )
    vector_totals = vector_sum(jnp.stack(vector_grads))

    def own_block(values):
        mine = lax.dynamic_index_in_dim(values, tp_index, values.ndim - 2, keepdims=False)
        return by_core(mine, core_swap(mine), mine.ndim - 1)

    row_size = 6 * model_width
    block_size = tp_count * half_width
    row_sum = vector_totals[:, :row_size].reshape(LAYERS, 6, model_width)
    qv_total = own_block(
        vector_totals[:, row_size : row_size + 2 * block_size].reshape(
            LAYERS, 2, tp_count, half_width
        )
    )
    up_total = own_block(
        vector_totals[:, row_size + 2 * block_size :].reshape(LAYERS, tp_count, half_hidden)
    )
    qkv_grad = jnp.stack([layer_grads[0] for layer_grads in matrix_grads])
    out_grad = jnp.stack([layer_grads[1] for layer_grads in matrix_grads])
    up_grad = jnp.stack([layer_grads[2] for layer_grads in matrix_grads])
    down_grad = jnp.stack([layer_grads[3] for layer_grads in matrix_grads])
    qkv_new, qkv_moment_new, qkv_square_new = adamw_step(
        qkv_weight, qkv_moment, qkv_square, qkv_grad, D ** (-0.5), WEIGHT_DECAY
    )
    out_new, out_moment_new, out_square_new = adamw_step(
        out_weight, out_moment, out_square, out_grad, (D * 16 / SEQ) ** (-0.5), WEIGHT_DECAY
    )
    up_new, up_moment_new, up_square_new = adamw_step(
        up_weight, up_moment, up_square, up_grad, D ** (-0.5), WEIGHT_DECAY
    )
    down_new, down_moment_new, down_square_new = adamw_step(
        down_weight, down_moment, down_square, down_grad, FF ** (-0.5), WEIGHT_DECAY
    )
    row_new, row_moment_new, row_square_new = adamw_step(
        row_vectors, row_moment, row_square, row_sum, VECTOR_RATE, 0.0
    )
    qv_new, qv_moment_new, qv_square_new = adamw_step(
        qv_bias, qv_moment, qv_square, qv_total, VECTOR_RATE, 0.0
    )
    up_bias_new, bias_moment_new, bias_square_new = adamw_step(
        up_bias, bias_moment, bias_square, up_total, VECTOR_RATE, 0.0
    )
    return (
        activations,
        input_grad,
        qkv_new,
        qkv_moment_new,
        qkv_square_new,
        qkv_new.astype(jnp.bfloat16),
        out_new,
        out_moment_new,
        out_square_new,
        out_new.astype(jnp.bfloat16),
        up_new,
        up_moment_new,
        up_square_new,
        up_new.astype(jnp.bfloat16),
        down_new,
        down_moment_new,
        down_square_new,
        down_new.astype(jnp.bfloat16),
        row_new,
        row_moment_new,
        row_square_new,
        qv_new,
        qv_moment_new,
        qv_square_new,
        up_bias_new,
        bias_moment_new,
        bias_square_new,
    )


def solution(mesh):
    return jax.shard_map(
        shards,
        mesh=mesh,
        in_specs=(
            P("tp", "wide", None),
            P("tp", "wide", None),
            P("wide"),
            P(None, "wide", None, "tp"),
            P(None, "wide", None, "tp"),
            P(None, "wide", None, "tp"),
            P(None, "tp", "wide"),
            P(None, "tp", "wide"),
            P(None, "tp", "wide"),
            P(None, "wide", "tp"),
            P(None, "wide", "tp"),
            P(None, "wide", "tp"),
            P(None, "tp", "wide"),
            P(None, "tp", "wide"),
            P(None, "tp", "wide"),
            P(),
            P(),
            P(),
            P(None, None, "tp"),
            P(None, None, "tp"),
            P(None, None, "tp"),
            P(None, "tp"),
            P(None, "tp"),
            P(None, "tp"),
        ),
        out_specs=(
            P("tp", "wide", None),
            P("tp", "wide", None),
            P(None, "wide", None, "tp"),
            P(None, "wide", None, "tp"),
            P(None, "wide", None, "tp"),
            P(None, "wide", None, "tp"),
            P(None, "tp", "wide"),
            P(None, "tp", "wide"),
            P(None, "tp", "wide"),
            P(None, "tp", "wide"),
            P(None, "wide", "tp"),
            P(None, "wide", "tp"),
            P(None, "wide", "tp"),
            P(None, "wide", "tp"),
            P(None, "tp", "wide"),
            P(None, "tp", "wide"),
            P(None, "tp", "wide"),
            P(None, "tp", "wide"),
            P(),
            P(),
            P(),
            P(None, None, "tp"),
            P(None, None, "tp"),
            P(None, None, "tp"),
            P(None, "tp"),
            P(None, "tp"),
            P(None, "tp"),
        ),
        check_vma=False,
    )
```

```python
import functools

import jax
import jax.numpy as jnp
from jax import lax
from jax.experimental import pallas as pl
from jax.experimental.pallas import tpu as pltpu
from jax.sharding import PartitionSpec as P

D = 1024
HDIM = 64
FF = 4096
SEQ = 640
VALID = 577
LAYERS = 2
STEP = 10


NORM_EPS = 1e-05
BETA_ONE = 0.9
BETA_TWO = 0.999
ADAM_EPS = 1e-08
WEIGHT_DECAY = 0.01
VECTOR_RATE = 0.4
MASKED = -1e30
LOW = jnp.bfloat16
WIDE = jnp.float32
TILE = 128
MIB = 1 << 20
COST_PART = 1.0

def adamw_step(weight, moment, square, gradient, step_rate, decay_rate):
    moment = BETA_ONE * moment + (1.0 - BETA_ONE) * gradient
    square = BETA_TWO * square + (1.0 - BETA_TWO) * gradient * gradient
    moment_hat = moment / (1.0 - BETA_ONE**STEP)
    square_hat = square / (1.0 - BETA_TWO**STEP)
    weight = weight - step_rate * (
        moment_hat / (jnp.sqrt(square_hat) + ADAM_EPS) + decay_rate * weight
    )
    return (weight, moment, square)


def core_swap(values):
    return lax.ppermute(values, "wide", [(i, i ^ 1) for i in range(lax.axis_size("wide"))])


def pair_swap(values, bit):
    flip = 2 << bit
    return lax.ppermute(values, "wide", [(i, i ^ flip) for i in range(lax.axis_size("wide"))])


def cross_swap(values, second):
    moves = [(i, i ^ (2 << ((i + second) % 2))) for i in range(lax.axis_size("wide"))]
    return lax.ppermute(values, "wide", moves)


def neighbours():
    pair, core = lax.axis_index("wide") // 2, lax.axis_index("wide") % 2
    return pair, pair ^ (1 << core), pair ^ (2 >> core), pair ^ 3


def tp_shift(values, distance):
    count = lax.axis_size("tp")
    return lax.ppermute(values, "tp", [(i, (i + distance) % count) for i in range(count)])


def tp_flip(values, bit):
    count = lax.axis_size("tp")
    return lax.ppermute(values, "tp", [(i, i ^ (1 << bit)) for i in range(count)])


class Move:
    def __init__(self, move, values):
        self.move, self.values, self.got = move, values, None

    def send(self, after=()):
        values = self.values
        if after:
            values, _ = lax.optimization_barrier((values, tuple(after)))
        self.got = self.move(values)
        return self.got


def first_way(values):
    return Move(lambda v: cross_swap(v, 0), values)


def second_way(values):
    return Move(lambda v: cross_swap(v, 1), values)


def along_tp(values, distance):
    return Move(lambda v: tp_shift(v, distance), values)


def behind(values, first):
    return lax.optimization_barrier((values, first))[0]


class Steps:
    def __init__(self):
        self.ended = ()
        self.sent = []

    def gate(self, values):
        return behind(values, self.ended)

    def send(self, *moves, wait=True):
        for move in moves:
            move.send(self.ended)
        if wait:
            self.sent += moves

    def end(self, *arrays):
        self.ended = arrays + tuple(move.got for move in self.sent)
        for move in self.sent:
            move.got = self.gate(move.got)
        self.sent = []


def pair_bits():
    return (lax.axis_size("wide") // 2).bit_length() - 1


def by_core(mine, other, axis):
    lower = lax.axis_index("wide") % 2 == 0
    return jnp.where(
        lower,
        jnp.concatenate([mine, other], axis=axis),
        jnp.concatenate([other, mine], axis=axis),
    )


def half_of(values, which, axis):
    span = values.shape[axis] // 2
    return lax.dynamic_slice_in_dim(values, which * span, span, axis)


def relative(values, axis):
    pairs = lax.axis_size("wide") // 2
    pair = lax.axis_index("wide") // 2
    span = values.shape[axis] // pairs
    shape = values.shape
    for bit in range(pair_bits()):
        step = span << bit
        split = values.reshape(shape[:axis] + (-1, 2, step) + shape[axis + 1 :])
        lower, upper = (lax.index_in_dim(split, k, axis + 1) for k in (0, 1))
        flipped = jnp.concatenate([upper, lower], axis=axis + 1).reshape(shape)
        values = jnp.where((pair >> bit) & 1 == 1, flipped, values)
    return values


def piece_places():
    if pair_bits() == 2:
        starts = [pair * (D // 4) for pair in neighbours()]
    else:
        starts = [0] * 4
    return jnp.stack([jnp.asarray(v, jnp.int32) for v in starts + [lax.axis_index("tp")]])


GATHERED = ((0, 4, 0), (0, 4, 1), (0, 4, 2), (0, 2, 3), (2, 2, 3))
def gathered_spans():
    return GATHERED if pair_bits() == 2 else ((0, lax.axis_size("tp"), 0),)


def tp_moves(block):
    return [along_tp(block, d) for d in range(1, lax.axis_size("tp"))]


class Gather:
    def __init__(self, own):
        self.own = own
        self.near_moves, self.far_moves = [], []
        if pair_bits() == 2:
            self.near_moves = [first_way(own), second_way(own)]

    def near(self):
        return self.near_moves

    def far(self):
        if self.near_moves:
            half = self.own.shape[0] // 2
            first, second = (move.got for move in self.near_moves)
            self.far_moves = [second_way(first[:half]), first_way(second[half:])]
        return self.far_moves

    def pieces(self):
        if self.near_moves:
            return [self.own] + [move.got for move in self.near_moves + self.far_moves]
        own = self.own
        for bit in range(pair_bits()):
            own = jnp.concatenate([own, pair_swap(own, bit)], axis=1)
        return [relative(own, 1)]


def add_low(*terms):
    total = terms[0].astype(WIDE)
    for term in terms[1:]:
        total = total + term.astype(WIDE)
    return total


def own_sum_kernel(own, first, second, out):
    out[...] = add_low(own[...], first[...], second[...]).astype(LOW)


def merge_kernel(whole_part, half_part, out):
    out[...] = add_low(whole_part[...], half_part[...]).astype(LOW)


def merge(whole_part, half_part, first):
    span, rows, columns = half_part.shape
    block = pl.BlockSpec((1, rows, columns), lambda d: (first + d, 0, 0))
    return pl.pallas_call(
        merge_kernel,
        grid=(span,),
        in_specs=[block, pl.BlockSpec((1, rows, columns), lambda d: (d, 0, 0))],
        out_specs=block,
        out_shape=jax.ShapeDtypeStruct(whole_part.shape, LOW),
        input_output_aliases={0: 0},
        compiler_params=pltpu.CompilerParams(vmem_limit_bytes=24 * MIB),
        cost_estimate=cost(2),
    )(whole_part, half_part)


class Scatter:
    def __init__(self, pieces):
        self.pieces = pieces
        self.far_moves, self.rest_moves = [], []
        if len(pieces) > 1:
            self.far_moves = [second_way(pieces[-2]), first_way(pieces[-1])]

    def far(self):
        return self.far_moves

    def rest(self):
        if self.far_moves:
            low, high = (move.got for move in self.far_moves)
            first = merge(self.pieces[1], low, 0)
            second = merge(self.pieces[2], high, high.shape[0])
            self.rest_moves = [first_way(first), second_way(second)]
        return self.rest_moves

    def merged(self):
        return tuple(move.values for move in self.rest_moves)

    def total(self, after=()):
        own = behind(self.pieces[0], after)
        if not self.far_moves:
            own = relative(own, 1)
            for bit in reversed(range(pair_bits())):
                keep = own.shape[1] // 2
                own = add_low(own[:, :keep], pair_swap(own[:, keep:], bit)).astype(LOW)
            return own
        return pl.pallas_call(
            own_sum_kernel,
            out_shape=jax.ShapeDtypeStruct(own.shape, LOW),
            compiler_params=pltpu.CompilerParams(vmem_limit_bytes=24 * MIB),
            cost_estimate=cost(2),
        )(own, *[move.got for move in self.rest_moves])


def both_halves(total):
    core = lax.axis_index("wide") % 2
    return total, core_swap(half_of(total, 1 - core, 0).astype(LOW))


def scatter_tp(blocks):
    return lax.psum_scatter(blocks, "tp", scatter_dimension=0, tiled=False)


def by_source_kernel(place, *refs):
    *blocks, out = refs
    total = len(blocks)
    for d, block in enumerate(blocks):
        out[lax.rem(place[0] + (total - d), total)] = block[...]


def by_source(got):
    place = lax.axis_index("tp").astype(jnp.int32).reshape(1)
    return pl.pallas_call(
        by_source_kernel,
        in_specs=[pl.BlockSpec(memory_space=pltpu.SMEM)]
        + [pl.BlockSpec(memory_space=pltpu.VMEM)] * len(got),
        out_shape=jax.ShapeDtypeStruct((len(got),) + got[0].shape, got[0].dtype),
        compiler_params=pltpu.CompilerParams(vmem_limit_bytes=16 * MIB),
        cost_estimate=cost(1),
    )(place, *got)


class Exchange:
    def __init__(self, blocks):
        tp_index = lax.axis_index("tp")
        tp_count = lax.axis_size("tp")
        own, *others = (
            lax.dynamic_index_in_dim(blocks, (tp_index + d) % tp_count, 0, keepdims=False)
            for d in range(tp_count)
        )
        self.own = own
        self.moves = [along_tp(block, d + 1) for d, block in enumerate(others)]

    def result(self):
        return by_source([self.own] + [move.got for move in self.moves])


def image_parts(values):
    core = lax.axis_index("wide") % 2
    slots = jnp.stack([values[:, 0], values[:, 1]])
    other = core_swap(half_of(slots, 1 - core, 1))
    return Exchange(by_core(half_of(slots, core, 1), other, 0))


def image_rows(exchange):
    rows = exchange.result()
    return by_core(rows, core_swap(rows), 1).reshape(-1, rows.shape[2])


def group_parts(arrays):
    core = lax.axis_index("wide") % 2
    tp_count = lax.axis_size("tp")
    halves = [half_of(a.reshape(tp_count, -1, a.shape[1]), core, 1) for a in arrays]
    return Exchange(jnp.concatenate(halves, axis=1))


def group_rows(exchange, count):
    core = lax.axis_index("wide") % 2
    images = exchange.result()
    other = core_swap(half_of(images, 1 - core, 0))
    mine = half_of(images, core, 0)
    rows = images.shape[1] // count
    outs = []
    for k in range(count):
        here = slice(k * rows, (k + 1) * rows)
        slots = by_core(mine[:, here], other[:, here], 1)
        outs.append(jnp.stack([slots[0], slots[1]], axis=1))
    return outs


def vector_tp(values):
    for bit in range(lax.axis_size("tp").bit_length() - 1):
        values = values + tp_flip(values, bit)
    return values


def vector_plane(values):
    for bit in range(pair_bits()):
        values = values + pair_swap(values, bit)
    return values


def cost(time):
    return pl.CostEstimate(
        flops=int(time * COST_PART * 1.1e9),
        bytes_accessed=int(time * COST_PART * 3.4e6),
        transcendentals=0,
    )


SCALARS = pl.BlockSpec(memory_space=pltpu.SMEM)
FAR = pl.BlockSpec(memory_space=pl.ANY)


def whole(shape):
    return pl.BlockSpec(shape, lambda *_: (0,) * len(shape))


def mat(left, right):
    return jnp.dot(left, right, preferred_element_type=WIDE)


def mat_back(left, right):
    return lax.dot_general(left, right, (((1,), (1,)), ((), ())), preferred_element_type=WIDE)


def flip(values):
    return values.T


def fetch(places, refs, held, sems, column, width, turned=False):
    copies = []
    for ref, (first, span, place) in zip(refs, gathered_spans()):
        rows = pl.ds(pl.multiple_of(places[place], TILE), ref.shape[1])
        columns = pl.ds(column, width)
        if turned:
            total = held.shape[0]
            for z in range(span):
                block = lax.rem(places[4] + (total - first - z), total)
                copies.append((ref.at[z, :, columns], held.at[block, rows, :]))
        else:
            copies.append((ref.at[:, :, columns], held.at[pl.ds(first, span), rows, :]))
    return [pltpu.make_async_copy(*pair, sems.at[k]) for k, pair in enumerate(copies)]


def fetch_joined(places, refs, held, sems, column, width, turned=False):
    copies = []
    for ref, (first, span, place) in zip(refs, gathered_spans()):
        rows = pl.ds(pl.multiple_of(places[place], TILE), ref.shape[1])
        total = held.shape[1] // width
        for z in range(span):
            block = lax.rem(places[4] + (total - first - z), total) if turned else first + z
            there = held.at[rows, pl.ds(pl.multiple_of(block * width, TILE), width)]
            copies.append((ref.at[z, :, pl.ds(column, width)], there))
    return [pltpu.make_async_copy(*pair, sems.at[k]) for k, pair in enumerate(copies)]


def start_all(copies):
    for copy in copies:
        copy.start()


def wait_all(copies):
    for copy in copies:
        copy.wait()


def norm_parts(values):
    center = values - jnp.mean(values, axis=-1, keepdims=True)
    scale = lax.rsqrt(jnp.mean(center * center, axis=-1, keepdims=True) + NORM_EPS)
    return center * scale, scale


def norm_back(values, gain, grad):
    unit, scale = norm_parts(values)
    scaled = grad * gain
    inner = scaled - jnp.mean(scaled, axis=-1, keepdims=True)
    inner = inner - unit * jnp.mean(scaled * unit, axis=-1, keepdims=True)
    return (
        inner * scale,
        jnp.sum(grad * unit, axis=0, keepdims=True),
        jnp.sum(grad, axis=0, keepdims=True),
    )


def pack_attn_kernel(core, qkv, out, mine, other):
    half = qkv.shape[3] // 2

    def put(ref, first):
        for kind in range(3):
            ref[:, kind * half : (kind + 1) * half] = qkv[
                0, :, kind, first * half : (first + 1) * half
            ].astype(LOW)
        ref[:, 3 * half :] = out[0, first * half : (first + 1) * half, :].T.astype(LOW)

    @pl.when(core[0] == 0)
    def _():
        put(mine, 0)
        put(other, 1)

    @pl.when(core[0] == 1)
    def _():
        put(mine, 1)
        put(other, 0)


def pack_mlp_kernel(core, up, down, mine, other):
    half = up.shape[2] // 2

    def put(ref, first):
        ref[:, :half] = up[0, :, first * half : (first + 1) * half].astype(LOW)
        ref[:, half:] = down[0, first * half : (first + 1) * half, :].T.astype(LOW)

    @pl.when(core[0] == 0)
    def _():
        put(mine, 0)
        put(other, 1)

    @pl.when(core[0] == 1)
    def _():
        put(mine, 1)
        put(other, 0)


def adam_kernel(is_attn, rates, core, *refs):
    grads, refs = refs[: 2 if is_attn else 4], refs[2 if is_attn else 4 :]
    ins, outs = refs[:6], refs[-8:]
    half_rows = grads[1].shape[0]
    first = pl.ds(pl.multiple_of(core[0] * half_rows, 16), half_rows)

    def grad_of(mine, which, columns):
        total, other = grads[2 * which : 2 * which + 2] if not is_attn else grads
        return (total[first, columns] if mine else other[:, columns]).astype(WIDE)

    def step(which, index, grad):
        weight, moment, square = (r[index] for r in ins[3 * which : 3 * which + 3])
        new, moment, square = adamw_step(weight, moment, square, grad, rates[which], WEIGHT_DECAY)
        for out, value in zip(outs[4 * which :], (new, moment, square, new.astype(LOW))):
            out[index] = value

    def put(here):
        width = ins[0].shape[-1] // 2
        for side in (0, 1):
            columns = slice(side * width, (side + 1) * width)
            if is_attn:
                for kind in range(3):
                    part = grad_of(side == here, 0, slice(kind * width, (kind + 1) * width))
                    step(0, (0, slice(None), kind, columns), part)
                rest = grad_of(side == here, 0, slice(3 * width, 4 * width))
            else:
                step(0, (0, slice(None), columns), grad_of(side == here, 0, slice(None)))
                rest = grad_of(side == here, 1, slice(None))
            step(1, (0, columns, slice(None)), rest.T)

    pl.when(core[0] == 0)(lambda: put(0))
    pl.when(core[0] == 1)(lambda: put(1))


def adam(is_attn, rates, layer, core, grads, arrays, before):
    shapes = [
        jax.ShapeDtypeStruct(arrays[3 * m].shape, LOW if k == 3 else WIDE)
        for m in range(2)
        for k in range(4)
    ]
    first = 1 + len(grads) + len(arrays)
    return pl.pallas_call(
        functools.partial(adam_kernel, is_attn, rates),
        grid=(1,),
        in_specs=[SCALARS]
        + [whole(g.shape) for g in grads]
        + [layer_block(a, layer) for a in arrays]
        + [FAR] * len(before),
        out_specs=[layer_block(s, layer) for s in shapes],
        out_shape=shapes,
        input_output_aliases={first + k: k for k in range(len(before))},
        compiler_params=pltpu.CompilerParams(vmem_limit_bytes=60 * MIB),
        cost_estimate=cost(5),
    )(core, *grads, *arrays, *before)


def layer_block(array, layer):
    shape = (1,) + array.shape[1:]
    return pl.BlockSpec(shape, lambda *_: (layer,) + (0,) * (len(shape) - 1))


def pack(kernel, layer, core, first, second, columns):
    rows = lax.axis_size("wide")
    shape = jax.ShapeDtypeStruct((D // rows, columns), LOW)
    return pl.pallas_call(
        kernel,
        grid=(1,),
        in_specs=[SCALARS, layer_block(first, layer), layer_block(second, layer)],
        out_specs=[whole(shape.shape)] * 2,
        out_shape=[shape] * 2,
        compiler_params=pltpu.CompilerParams(vmem_limit_bytes=16 * MIB),
        cost_estimate=cost(1),
    )(core, first, second)


def project_kernel(layer, joined, turned, places, *refs):
    if joined:
        stream, own, got, vectors, bias, *refs = refs
        *weights, kept, normed, proj, held, sems = refs
    else:
        stream, vectors, bias, *refs = refs
        *weights, normed, proj, held, sems = refs
    width = held.shape[2]
    copies = fetch(places, weights, held, sems, 0, width, turned)
    pl.when(pl.program_id(0) == 0)(lambda: start_all(copies))
    values = stream[...].astype(WIDE)
    if joined:
        values = values + (add_low(own[...], got[...]) + vectors[layer - 1, 5:6, :])
        kept[...] = values
    low = (norm_parts(values)[0] * vectors[layer, 0:1, :] + vectors[layer, 1:2, :]).astype(LOW)
    normed[...] = low
    pl.when(pl.program_id(0) == 0)(lambda: wait_all(copies))
    for z in range(held.shape[0]):
        here = slice(z * width, (z + 1) * width)
        proj[:, here] = (mat(low, held[z]) + bias[:, here]).astype(LOW)


def project(layer, stream, partial, vectors, bias, places, pieces, turned):
    rows = stream.shape[0]
    steps = 2
    tp_count = lax.axis_size("tp")
    columns = bias.shape[1]
    tile = pl.BlockSpec((rows // steps, D), lambda i: (i, 0))
    streams = [stream] + list(partial)
    out_shape = [
        jax.ShapeDtypeStruct((rows, D), LOW),
        jax.ShapeDtypeStruct((rows, columns), LOW),
    ]
    out_specs = [tile, pl.BlockSpec((rows // steps, columns), lambda i: (i, 0))]
    if partial:
        out_shape = [jax.ShapeDtypeStruct((rows, D), WIDE)] + out_shape
        out_specs = [tile] + out_specs
    return pl.pallas_call(
        functools.partial(project_kernel, layer, bool(partial), turned),
        grid=(steps,),
        in_specs=[SCALARS]
        + [tile] * len(streams)
        + [whole(vectors.shape), whole(bias.shape)]
        + [FAR] * len(pieces),
        out_specs=out_specs,
        out_shape=out_shape,
        scratch_shapes=[
            pltpu.VMEM((tp_count, D, columns // tp_count), LOW),
            pltpu.SemaphoreType.DMA((tp_count * len(pieces),)),
        ],
        compiler_params=pltpu.CompilerParams(vmem_limit_bytes=40 * MIB),
        cost_estimate=cost(6),
    )(places, *streams, vectors, bias, *pieces)


def head_rows(values):
    turned = flip(values)
    upper = lax.broadcasted_iota(jnp.int32, turned.shape, 0) < HDIM
    zero = jnp.zeros_like(turned)
    return jnp.where(upper, turned, zero), jnp.where(upper, zero, turned)


def put_head_rows(held, values):
    first, second = head_rows(values)
    for t in range(held.shape[0]):
        held[t, :, :TILE] = first[:, t * TILE : (t + 1) * TILE]
        held[t, :, TILE:] = second[:, t * TILE : (t + 1) * TILE]


def put_head_columns(held, values):
    left = lax.broadcasted_iota(jnp.int32, values.shape, 1) < HDIM
    zero = jnp.zeros_like(values)
    first, second = jnp.where(left, values, zero), jnp.where(left, zero, values)
    for t in range(held.shape[0]):
        held[t, :TILE, :] = first[t * TILE : (t + 1) * TILE, :]
        held[t, TILE:, :] = second[t * TILE : (t + 1) * TILE, :]


def merge_heads(values):
    upper = lax.broadcasted_iota(jnp.int32, (2 * HDIM, TILE), 0) < HDIM
    return jnp.where(upper, values[:, :TILE], values[:, TILE:]).T


def attend_kernel(turned, places, proj, mask, *refs):
    *weights, attended, totals, partial, held_out, held_att, query_rows, sems = refs
    z = pl.program_id(0)
    width = 2 * HDIM
    tiles = query_rows.shape[0]
    copies = fetch_joined(places, weights, held_out, sems, 3 * width, width, turned)
    pl.when(z == 0)(lambda: start_all(copies))
    put_head_rows(query_rows, proj[:, :width] * LOW(HDIM**-0.5))
    value_rows = flip(proj[:, 2 * width :])
    key_rows = proj[:, width : 2 * width]

    def one(t, carried):
        scores = mat(key_rows, query_rows[t]) + jnp.concatenate([mask[...], mask[...]], axis=1)
        highest = jnp.max(scores, axis=0, keepdims=True)
        exponent = jnp.exp(scores - highest)
        total = jnp.sum(exponent, axis=0, keepdims=True)
        probs = (exponent * (1.0 / total)).astype(LOW)
        totals[0, pl.ds(t, 1), :] = highest + jnp.log(total)
        result = merge_heads(mat(value_rows, probs)).astype(LOW)
        attended[pl.ds(pl.multiple_of(t * TILE, TILE), TILE), :] = result
        return carried

    lax.fori_loop(0, tiles, one, 0)
    for k in range(held_att.shape[1] // width):

        @pl.when(z == k)
        def _():
            held_att[:, k * width : (k + 1) * width] = attended[...]

    @pl.when(z == pl.num_programs(0) - 1)
    def _():
        wait_all(copies)
        partial[...] = mat_back(held_att[...], held_out[...]).astype(LOW)


def attend(proj, mask, places, pieces, turned):
    rows = proj.shape[0]
    tp_count = lax.axis_size("tp")
    width = 2 * HDIM
    tiles = rows // TILE
    return pl.pallas_call(
        functools.partial(attend_kernel, turned),
        grid=(tp_count,),
        in_specs=[SCALARS, pl.BlockSpec((rows, 3 * width), lambda z: (0, z)), whole(mask.shape)]
        + [FAR] * len(pieces),
        out_specs=[
            pl.BlockSpec((rows, width), lambda z: (0, z)),
            pl.BlockSpec((1, tiles, 2 * TILE), lambda z: (z, 0, 0)),
            whole((rows, D)),
        ],
        out_shape=[
            jax.ShapeDtypeStruct((rows, tp_count * width), LOW),
            jax.ShapeDtypeStruct((tp_count, tiles, 2 * TILE), WIDE),
            jax.ShapeDtypeStruct((rows, D), LOW),
        ],
        scratch_shapes=[
            pltpu.VMEM((D, tp_count * width), LOW),
            pltpu.VMEM((rows, tp_count * width), LOW),
            pltpu.VMEM((tiles, width, 2 * TILE), LOW),
            pltpu.SemaphoreType.DMA((tp_count * len(pieces),)),
        ],
        compiler_params=pltpu.CompilerParams(vmem_limit_bytes=40 * MIB),
        cost_estimate=cost(18),
    )(places, proj, mask, *pieces)


def mlp_kernel(layer, turned, count, down_too, places, stream, own, got, vectors, bias, *refs):
    ups, refs = refs[:count], refs[count:]
    if down_too:
        downs, refs = refs[:count], refs[count:]
        middle, normed, pre_act, hidden, partial, held_up, up_sems, held_down, down_sems = refs
    else:
        middle, normed, pre_act, hidden, held_up, up_sems = refs
    width = held_up.shape[2]
    first = pl.program_id(0) == 0
    up_copies = fetch(places, ups, held_up, up_sems, 0, width, turned)
    pl.when(first)(lambda: start_all(up_copies))
    if down_too:
        down_copies = fetch(places, downs, held_down, down_sems, 0, width, turned)
        pl.when(first)(lambda: start_all(down_copies))
    values = stream[...].astype(WIDE) + (add_low(own[...], got[...]) + vectors[layer, 4:5, :])
    middle[...] = values
    low = (norm_parts(values)[0] * vectors[layer, 2:3, :] + vectors[layer, 3:4, :]).astype(LOW)
    normed[...] = low
    total = None
    pl.when(first)(lambda: wait_all(up_copies))
    for z in range(held_up.shape[0]):
        here = slice(z * width, (z + 1) * width)
        pre = mat(low, held_up[z]) + bias[:, here]
        pre_act[:, here] = pre
        act = (pre / (1.0 + jnp.exp(-1.702 * pre))).astype(LOW)
        hidden[:, here] = act
        if down_too:
            if z == 0:
                pl.when(first)(lambda: wait_all(down_copies))
            term = mat_back(act, held_down[z])
            total = term if total is None else total + term
    if down_too:
        partial[...] = total.astype(LOW)


def mlp(layer, stream, partial, vectors, bias, places, ups, downs, turned):
    rows = stream.shape[0]
    steps = 2
    tp_count = lax.axis_size("tp")
    columns = bias.shape[1]
    tile = pl.BlockSpec((rows // steps, D), lambda i: (i, 0))
    broad = pl.BlockSpec((rows // steps, columns), lambda i: (i, 0))
    held = [
        pltpu.VMEM((tp_count, D, columns // tp_count), LOW),
        pltpu.SemaphoreType.DMA((tp_count * len(ups),)),
    ]
    down_too = 1 if downs else 0
    return pl.pallas_call(
        functools.partial(mlp_kernel, layer, turned, len(ups), bool(downs)),
        grid=(steps,),
        in_specs=[SCALARS]
        + [tile] * 3
        + [whole(vectors.shape), whole(bias.shape)]
        + [FAR] * (len(ups) + len(downs)),
        out_specs=[tile, tile, broad, broad] + [tile] * down_too,
        out_shape=[
            jax.ShapeDtypeStruct((rows, D), WIDE),
            jax.ShapeDtypeStruct((rows, D), LOW),
            jax.ShapeDtypeStruct((rows, columns), WIDE),
            jax.ShapeDtypeStruct((rows, columns), LOW),
        ]
        + [jax.ShapeDtypeStruct((rows, D), LOW)] * down_too,
        scratch_shapes=held * (1 + down_too),
        compiler_params=pltpu.CompilerParams(vmem_limit_bytes=52 * MIB),
        cost_estimate=cost(15 if downs else 9),
    )(places, stream, *partial, vectors, bias, *ups, *downs)


def mlp_down_kernel(turned, places, hidden, *refs):
    *downs, partial, held, sems = refs
    width = held.shape[2]
    copies = fetch(places, downs, held, sems, 0, width, turned)
    start_all(copies)
    wait_all(copies)
    total = None
    for z in range(held.shape[0]):
        term = mat_back(hidden[:, z * width : (z + 1) * width], held[z])
        total = term if total is None else total + term
    partial[...] = total.astype(LOW)


def mlp_down(hidden, places, downs, turned):
    rows, columns = hidden.shape
    tp_count = lax.axis_size("tp")
    return pl.pallas_call(
        functools.partial(mlp_down_kernel, turned),
        grid=(1,),
        in_specs=[SCALARS, whole(hidden.shape)] + [FAR] * len(downs),
        out_specs=whole((rows, D)),
        out_shape=jax.ShapeDtypeStruct((rows, D), LOW),
        scratch_shapes=[
            pltpu.VMEM((tp_count, D, columns // tp_count), LOW),
            pltpu.SemaphoreType.DMA((tp_count * len(downs),)),
        ],
        compiler_params=pltpu.CompilerParams(vmem_limit_bytes=48 * MIB),
        cost_estimate=cost(8),
    )(places, hidden, *downs)


def put_pieces(places, held, outs, shape, columns=slice(None)):
    z = pl.program_id(0)
    for out, (first, span, place) in zip(outs, shape):

        @pl.when((z >= first) & (z < first + span))
        def _():
            rows = pl.ds(pl.multiple_of(places[place], TILE), out.shape[1])
            out[0, :, columns] = held[rows, :]


def down_grad_kernel(places, grad, hidden, *refs):
    *outs, row_sum, low_turned, result = refs

    @pl.when(pl.program_id(0) == 0)
    def _():
        values = grad[...].astype(LOW)
        low_turned[...] = flip(values)
        row_sum[...] = jnp.sum(values.astype(WIDE), axis=0, keepdims=True)

    result[...] = mat(low_turned[...], hidden[...]).astype(LOW)
    put_pieces(places, result, outs, gathered_spans())


def mlp_back_kernel(count, turned, places, grad, normed, pre_act, *refs):
    ups, downs, refs = refs[:count], refs[count : 2 * count], refs[2 * count :]
    outs, refs = refs[:count], refs[count:]
    partial, bias_sum, held_up, held_down, low, normed_turned, result, total, sems = refs
    z = pl.program_id(0)
    width = held_up.shape[2]
    down_copies = fetch(places, downs, held_down, sems.at[1], 0, width, turned)
    up_copies = fetch(places, ups, held_up, sems.at[0], 0, width, turned)

    @pl.when(z == 0)
    def _():
        start_all(down_copies)
        start_all(up_copies)
        low[...] = grad[...].astype(LOW)
        normed_turned[...] = flip(normed[...])

    pre = pre_act[...]
    gate = 1.0 / (1.0 + jnp.exp(-1.702 * pre))
    slope = gate * (1.0 + 1.702 * pre * (1.0 - gate))
    pl.when(z == 0)(lambda: wait_all(down_copies))
    grad_pre = (mat(low[...], held_down[z]) * slope).astype(LOW)
    bias_sum[0] = jnp.sum(grad_pre.astype(WIDE), axis=0, keepdims=True)
    result[...] = mat(normed_turned[...], grad_pre).astype(LOW)
    put_pieces(places, result, outs, gathered_spans())
    pl.when(z == 0)(lambda: wait_all(up_copies))
    term = mat_back(grad_pre, held_up[z])

    @pl.when(z == 0)
    def _():
        total[...] = term

    @pl.when(z > 0)
    def _():
        total[...] += term

    @pl.when(z == pl.num_programs(0) - 1)
    def _():
        partial[...] = total[...].astype(LOW)


def piece_outs(width):
    spans = gathered_spans()
    rows = D // 4 if len(spans) > 1 else D

    def spec(first, span):
        return pl.BlockSpec((1, rows, width), lambda z: (jnp.clip(z - first, 0, span - 1), 0, 0))

    shapes = [jax.ShapeDtypeStruct((span, rows, width), LOW) for _, span, _ in spans]
    return shapes, [spec(first, span) for first, span, _ in spans]


def down_grad(grad, hidden, places):
    rows, columns = hidden.shape
    tp_count = lax.axis_size("tp")
    width = columns // tp_count
    shapes, specs = piece_outs(width)
    outs = pl.pallas_call(
        down_grad_kernel,
        grid=(tp_count,),
        in_specs=[SCALARS, whole((rows, D)), pl.BlockSpec((rows, width), lambda z: (0, z))],
        out_specs=specs + [whole((1, D))],
        out_shape=shapes + [jax.ShapeDtypeStruct((1, D), WIDE)],
        scratch_shapes=[pltpu.VMEM((D, rows), LOW), pltpu.VMEM((D, width), LOW)],
        compiler_params=pltpu.CompilerParams(vmem_limit_bytes=40 * MIB),
        cost_estimate=cost(7),
    )(places, grad, hidden)
    return outs[:-1], outs[-1]


def mlp_back(grad, normed, pre_act, places, ups, downs, turned):
    rows, columns = pre_act.shape
    tp_count = lax.axis_size("tp")
    width = columns // tp_count
    shapes, specs = piece_outs(width)
    held = pltpu.VMEM((tp_count, D, width), LOW)
    outs = pl.pallas_call(
        functools.partial(mlp_back_kernel, len(ups), turned),
        grid=(tp_count,),
        in_specs=[
            SCALARS,
            whole((rows, D)),
            whole((rows, D)),
            pl.BlockSpec((rows, width), lambda z: (0, z)),
        ]
        + [FAR] * (len(ups) + len(downs)),
        out_specs=specs + [whole((rows, D)), pl.BlockSpec((1, 1, width), lambda z: (z, 0, 0))],
        out_shape=shapes
        + [
            jax.ShapeDtypeStruct((rows, D), LOW),
            jax.ShapeDtypeStruct((tp_count, 1, width), WIDE),
        ],
        scratch_shapes=[
            held,
            held,
            pltpu.VMEM((rows, D), LOW),
            pltpu.VMEM((D, rows), LOW),
            pltpu.VMEM((D, width), LOW),
            pltpu.VMEM((rows, D), WIDE),
            pltpu.SemaphoreType.DMA((2, tp_count * len(ups))),
        ],
        compiler_params=pltpu.CompilerParams(vmem_limit_bytes=56 * MIB),
        cost_estimate=cost(20),
    )(places, grad, normed, pre_act, *ups, *downs)
    return outs[:-2], *outs[-2:]


def middle_back_kernel(
    layer, count, turned, places, grad, own, got, middle, vectors, attended, *refs
):
    weights, refs = refs[:count], refs[count:]
    grad_out, grad_mid, grad_att, sums, held, low, kept_sums, sems = refs
    step = pl.program_id(0)
    width = 2 * HDIM
    copies = fetch_joined(places, weights, held, sems, 3 * width, width, turned)
    pl.when(step == 0)(lambda: start_all(copies))
    back, gain_sum, shift_sum = norm_back(
        middle[...], vectors[layer, 2:3, :], add_low(own[...], got[...])
    )
    values = grad[...] + back
    grad_mid[...] = values
    values = values.astype(LOW)
    tile = values.shape[0]
    low[pl.ds(pl.multiple_of(step * tile, tile), tile), :] = values
    parts = jnp.concatenate(
        [gain_sum, shift_sum, jnp.sum(values.astype(WIDE), axis=0, keepdims=True)], axis=0
    )

    @pl.when(step == 0)
    def _():
        kept_sums[0:3, :] = parts

    @pl.when(step > 0)
    def _():
        kept_sums[0:3, :] += parts

    @pl.when(step == pl.num_programs(0) - 1)
    def _():
        sums[...] = kept_sums[...]
        grad_out[...] = mat(flip(low[...]), attended[...]).astype(LOW)
        wait_all(copies)
        grad_att[...] = mat(low[...], held[...]).astype(LOW)


def middle_back(
    layer, grad, partial, middle, vectors, attended, places, pieces, turned
):
    rows = grad.shape[0]
    steps = 4
    tp_count = lax.axis_size("tp")
    columns = attended.shape[1]
    tile = pl.BlockSpec((rows // steps, D), lambda i: (i, 0))
    outs = pl.pallas_call(
        functools.partial(middle_back_kernel, layer, len(pieces), turned),
        grid=(steps,),
        in_specs=[SCALARS]
        + [tile] * 4
        + [whole(vectors.shape), whole((rows, columns))]
        + [FAR] * len(pieces),
        out_specs=[whole((D, columns)), tile, whole((rows, columns)), whole((8, D))],
        out_shape=[
            jax.ShapeDtypeStruct((D, columns), LOW),
            jax.ShapeDtypeStruct((rows, D), WIDE),
            jax.ShapeDtypeStruct((rows, columns), LOW),
            jax.ShapeDtypeStruct((8, D), WIDE),
        ],
        scratch_shapes=[
            pltpu.VMEM((D, columns), LOW),
            pltpu.VMEM((rows, D), LOW),
            pltpu.VMEM((8, D), WIDE),
            pltpu.SemaphoreType.DMA((tp_count * len(pieces),)),
        ],
        compiler_params=pltpu.CompilerParams(vmem_limit_bytes=48 * MIB),
        cost_estimate=cost(9),
    )(places, grad, *partial, middle, vectors, attended, *pieces)
    return outs


def attend_back_kernel(
    count, turned, places, proj, mask, totals, grad_att, normed, grad_out, *refs
):
    weights, refs = refs[:count], refs[count:]
    outs, refs = refs[: len(gathered_spans())], refs[len(gathered_spans()) :]
    (
        partial,
        sums,
        held,
        normed_turned,
        query_rows,
        grad_rows,
        query_columns,
        grad_columns,
        grad_proj,
        result,
        total,
        key_sum,
        value_sum,
        key_turned,
        sems,
    ) = refs
    z = pl.program_id(0)
    width = 2 * HDIM
    tiles = query_rows.shape[0]
    copies = fetch(places, weights, held, sems, 0, 3 * width, turned)

    @pl.when(z == 0)
    def _():
        start_all(copies)
        normed_turned[...] = flip(normed[...])

    scaled = proj[:, :width] * LOW(HDIM**-0.5)
    put_head_rows(query_rows, scaled)
    put_head_columns(query_columns, scaled)
    put_head_rows(grad_rows, grad_att[...])
    put_head_columns(grad_columns, grad_att[...])
    key_rows = proj[:, width : 2 * width]
    value_rows = proj[:, 2 * width :]
    key_turned[...] = flip(key_rows)
    key_sum[...] = jnp.zeros_like(key_sum)
    value_sum[...] = jnp.zeros_like(value_sum)

    def one(t, carried):
        scores = mat(key_rows, query_rows[t]) + jnp.concatenate([mask[...], mask[...]], axis=1)
        probs = jnp.exp(scores - totals[0, pl.ds(t, 1), :])
        value_sum[...] += mat(probs.astype(LOW), grad_columns[t])
        grad_probs = mat(value_rows, grad_rows[t])
        inner = jnp.sum(probs * grad_probs, axis=0, keepdims=True)
        grad_scores = (probs * (grad_probs - inner)).astype(LOW)
        key_sum[...] += mat(grad_scores, query_columns[t])
        grad_query = merge_heads(mat(key_turned[...], grad_scores)) * HDIM**-0.5
        grad_proj[pl.ds(pl.multiple_of(t * TILE, TILE), TILE), :width] = grad_query.astype(LOW)
        return carried

    lax.fori_loop(0, tiles, one, 0)
    grad_proj[:, width : 2 * width] = key_sum[...].astype(LOW)
    grad_proj[:, 2 * width :] = value_sum[...].astype(LOW)
    grads = grad_proj[...]
    sums[0] = jnp.sum(grads.astype(WIDE), axis=0, keepdims=True)
    result[...] = mat(normed_turned[...], grads).astype(LOW)
    put_pieces(places, result, outs, gathered_spans(), slice(0, 3 * width))
    put_pieces(places, grad_out, outs, gathered_spans(), slice(3 * width, 4 * width))
    pl.when(z == 0)(lambda: wait_all(copies))
    term = mat_back(grads, held[z])

    @pl.when(z == 0)
    def _():
        total[...] = term

    @pl.when(z > 0)
    def _():
        total[...] += term

    @pl.when(z == pl.num_programs(0) - 1)
    def _():
        partial[...] = total[...].astype(LOW)


def attend_back(
    proj, mask, totals, grad_att, normed, grad_out, places, pieces, turned
):
    rows = proj.shape[0]
    tp_count = lax.axis_size("tp")
    width = 2 * HDIM
    tiles = rows // TILE
    shapes, specs = piece_outs(4 * width)
    outs = pl.pallas_call(
        functools.partial(attend_back_kernel, len(pieces), turned),
        grid=(tp_count,),
        in_specs=[
            SCALARS,
            pl.BlockSpec((rows, 3 * width), lambda z: (0, z)),
            whole(mask.shape),
            pl.BlockSpec((1, tiles, 2 * TILE), lambda z: (z, 0, 0)),
            pl.BlockSpec((rows, width), lambda z: (0, z)),
            whole((rows, D)),
            pl.BlockSpec((D, width), lambda z: (0, z)),
        ]
        + [FAR] * len(pieces),
        out_specs=specs
        + [whole((rows, D)), pl.BlockSpec((1, 1, 3 * width), lambda z: (z, 0, 0))],
        out_shape=shapes
        + [
            jax.ShapeDtypeStruct((rows, D), LOW),
            jax.ShapeDtypeStruct((tp_count, 1, 3 * width), WIDE),
        ],
        scratch_shapes=[
            pltpu.VMEM((tp_count, D, 3 * width), LOW),
            pltpu.VMEM((D, rows), LOW),
            pltpu.VMEM((tiles, width, 2 * TILE), LOW),
            pltpu.VMEM((tiles, width, 2 * TILE), LOW),
            pltpu.VMEM((tiles, 2 * TILE, width), LOW),
            pltpu.VMEM((tiles, 2 * TILE, width), LOW),
            pltpu.VMEM((rows, 3 * width), LOW),
            pltpu.VMEM((D, 3 * width), LOW),
            pltpu.VMEM((rows, D), WIDE),
            pltpu.VMEM((rows, width), WIDE),
            pltpu.VMEM((rows, width), WIDE),
            pltpu.VMEM((width, rows), LOW),
            pltpu.SemaphoreType.DMA((tp_count * len(pieces),)),
        ],
        compiler_params=pltpu.CompilerParams(vmem_limit_bytes=48 * MIB),
        cost_estimate=cost(31),
    )(places, proj, mask, totals, grad_att, normed, grad_out, *pieces)
    return outs[:-2], *outs[-2:]


def input_back_kernel(layer, grad, own, got, stream, vectors, grad_in, sums, kept):
    back, gain_sum, shift_sum = norm_back(
        stream[...].astype(WIDE), vectors[layer, 0:1, :], add_low(own[...], got[...])
    )
    grad_in[...] = (grad[...] + back).astype(grad_in.dtype)
    parts = jnp.concatenate([gain_sum, shift_sum], axis=0)

    @pl.when(pl.program_id(0) == 0)
    def _():
        kept[0:2, :] = parts

    @pl.when(pl.program_id(0) > 0)
    def _():
        kept[0:2, :] += parts

    sums[...] = kept[...]


def input_back(layer, grad, partial, stream, vectors, dtype):
    rows = grad.shape[0]
    steps = 4
    tile = pl.BlockSpec((rows // steps, D), lambda i: (i, 0))
    return pl.pallas_call(
        functools.partial(input_back_kernel, layer),
        grid=(steps,),
        in_specs=[tile] * 4 + [whole(vectors.shape)],
        out_specs=[tile, whole((8, D))],
        out_shape=[jax.ShapeDtypeStruct((rows, D), dtype), jax.ShapeDtypeStruct((8, D), WIDE)],
        scratch_shapes=[pltpu.VMEM((8, D), WIDE)],
        compiler_params=pltpu.CompilerParams(vmem_limit_bytes=24 * MIB),
        cost_estimate=cost(4),
    )(grad, *partial, stream, vectors)


def shards(
    tokens,
    cotangent,
    counts,
    qkv_weight,
    qkv_moment,
    qkv_square,
    out_weight,
    out_moment,
    out_square,
    up_weight,
    up_moment,
    up_square,
    down_weight,
    down_moment,
    down_square,
    row_vectors,
    row_moment,
    row_square,
    qv_bias,
    qv_moment,
    qv_square,
    up_bias,
    bias_moment,
    bias_square,
):
    row_count, slot_count, model_width = tokens.shape
    tp_count = lax.axis_size("tp")
    seq_len = row_count * tp_count
    half_width = qkv_weight.shape[3] // 2
    half_hidden = up_weight.shape[2] // 2
    core = lax.axis_index("wide") % 2
    tp_index = lax.axis_index("tp")
    core_scalar = core.astype(jnp.int32).reshape(1)

    places = piece_places()
    def bundle_rows(kernel, layer, first, second, columns, start):
        mine, other = pack(kernel, layer, start, first, second, columns)
        return by_core(mine, core_swap(other), 0)

    steps = Steps()
    near, across, back = (0, 1, 2)
    owns = [
        bundle_rows(pack_attn_kernel, 0, qkv_weight, out_weight, 4 * half_width, core_scalar)
    ]
    steps.end(owns[0])

    attn_moves = tp_moves(owns[0])
    steps.send(attn_moves[near], attn_moves[back])
    later = steps.gate(core_scalar)
    tokens, cotangent, counts, qv_bias_here, up_bias_here = (
        steps.gate(v) for v in (tokens, cotangent, counts, qv_bias, up_bias)
    )
    owns.append(bundle_rows(pack_mlp_kernel, 0, up_weight, down_weight, 2 * half_hidden, later))
    owns.append(bundle_rows(pack_attn_kernel, 1, qkv_weight, out_weight, 4 * half_width, later))
    owns.append(bundle_rows(pack_mlp_kernel, 1, up_weight, down_weight, 2 * half_hidden, later))
    token_parts = image_parts(tokens)

    group_count = jnp.where(tp_index // slot_count == core, counts, core_swap(counts))[0]
    live = (tp_index % slot_count) < group_count
    valid = (lax.iota(jnp.int32, seq_len) < VALID) & live
    mask = jnp.broadcast_to(jnp.where(valid, 0.0, MASKED)[:, None], (seq_len, TILE))

    own_bias = jnp.concatenate(
        [half_of(qv_bias_here, core, 2).reshape(-1), half_of(up_bias_here, core, 1).reshape(-1)]
    ).reshape(-1, TILE)
    bias_moves = tp_moves(own_bias)
    steps.end(own_bias, token_parts.own)

    up_own, down_own = owns[1][:, :half_hidden], owns[1][:, half_hidden:]
    up_moves, down_moves = tp_moves(up_own), tp_moves(down_own)
    steps.send(
        attn_moves[across],
        token_parts.moves[near],
        token_parts.moves[back],
        bias_moves[near],
        bias_moves[back],
    )
    steps.end(up_own, down_own)
    attn = Gather(jnp.stack([owns[0]] + [move.got for move in attn_moves]))

    steps.send(*attn.near(), up_moves[near], up_moves[back], token_parts.moves[across])
    steps.end()

    stream = image_rows(token_parts)
    steps.send(*attn.far(), up_moves[across], bias_moves[across])
    steps.end(stream)
    ups = Gather(jnp.stack([up_own] + [move.got for move in up_moves]))
    bias_blocks = by_source([own_bias] + [move.got for move in bias_moves]).reshape(tp_count, -1)
    qv_size = LAYERS * 2 * half_width
    qv_blocks = bias_blocks[:, :qv_size].reshape(tp_count, LAYERS, 2, half_width)
    up_blocks = bias_blocks[:, qv_size:].reshape(tp_count, LAYERS, half_hidden)

    def proj_bias(layer):
        qv_layer = qv_blocks[:, layer]
        return jnp.stack(
            [qv_layer[:, 0], jnp.zeros_like(qv_layer[:, 0]), qv_layer[:, 1]], axis=1
        ).reshape(1, -1)

    def up_bias_of(layer):
        return up_blocks[:, layer].reshape(1, -1)

    attn_rows = lax.all_gather(steps.gate(owns[2]), "tp")
    up_rows = lax.all_gather(behind(owns[3][:, :half_hidden], attn_rows), "tp")
    down_rows = lax.all_gather(behind(owns[3][:, half_hidden:], up_rows), "tp")
    steps.send(*ups.near(), down_moves[near], down_moves[back])
    attn_zero = attn.pieces()
    normed, proj = project(
        0, stream, (), row_vectors, proj_bias(0), places, attn_zero, True
    )
    attended, totals, part = attend(proj, mask, places, attn_zero, True)
    steps.end(part)
    part = steps.gate(part)
    partial = (part, core_swap(part))
    steps.send(*ups.far(), down_moves[across])
    grad_parts = image_parts(steps.gate(cotangent))
    steps.end(grad_parts.own)
    downs = Gather(jnp.stack([down_own] + [move.got for move in down_moves]))
    steps.send(*downs.near(), grad_parts.moves[near], grad_parts.moves[back])
    steps.end()

    attn = Gather(steps.gate(attn_rows))
    steps.send(*downs.far(), *attn.near(), grad_parts.moves[across])
    steps.end()
    up_zero, down_zero = ups.pieces(), downs.pieces()
    ups = Gather(steps.gate(up_rows))
    steps.send(*attn.far())
    middle, normed_two, pre_act, hidden, part = mlp(
        0, stream, partial, row_vectors, up_bias_of(0), places, up_zero, down_zero, True
    )
    stored = [(stream, normed, proj, attended, totals, middle, normed_two, pre_act, hidden)]
    steps.end(part)
    part = steps.gate(part)
    partial = (part, core_swap(part))
    attn_one = attn.pieces()
    downs = Gather(steps.gate(down_rows))
    steps.send(*ups.near(), *downs.near())
    stream, normed, proj = project(
        1, middle, partial, row_vectors, proj_bias(1), places, attn_one, False
    )
    attended, totals, part = attend(proj, mask, places, attn_one, False)
    steps.end(part)
    part = steps.gate(part)
    partial = (part, core_swap(part))
    steps.send(*ups.far())
    grad = jnp.where(valid[:, None], image_rows(grad_parts).astype(WIDE), 0.0)
    steps.end(*partial, grad)
    partial = tuple(steps.gate(v) for v in partial)
    grad = steps.gate(grad)
    steps.send(*downs.far())
    up_one = ups.pieces()
    middle, normed_two, pre_act, hidden = mlp(
        1, stream, partial, row_vectors, up_bias_of(1), places, up_one, (), False
    )
    stored.append((stream, normed, proj, attended, totals, middle, normed_two, pre_act, hidden))
    steps.end(hidden)
    down_one = downs.pieces()
    bundles = [(attn_zero, up_zero, down_zero), (attn_one, up_one, down_one)]

    def mlp_grads(layer, grad):
        _, ups, downs = bundles[layer]
        *_, normed_two, pre_act, _ = stored[layer]
        return mlp_back(grad, normed_two, pre_act, places, ups, downs, layer == 0)

    def attn_grads(layer, grad, part):
        stream, normed, proj, attended, totals, middle, *_ = stored[layer]
        attn = bundles[layer][0]
        grad_out, grad_mid, grad_att, sums = middle_back(
            layer,
            grad,
            (part, core_swap(part)),
            middle,
            row_vectors,
            attended,
            places,
            attn,
            layer == 0,
        )
        return (grad_mid, sums) + tuple(
            attend_back(
                proj, mask, totals, grad_att, normed, grad_out, places, attn, layer == 0
            )
        )

    def vector_grad(input_sums, middle_sums, last_sum, proj_sums, bias_sum):
        proj_sums = proj_sums.reshape(tp_count, 3, half_width)
        return jnp.concatenate(
            [
                input_sums[:2].reshape(-1),
                middle_sums[:3].reshape(-1),
                last_sum.reshape(-1),
                proj_sums[:, 0].reshape(-1),
                proj_sums[:, 2].reshape(-1),
                bias_sum[:, 0].reshape(-1),
            ]
        )

    attn_new, wide_new = (), ()
    rate = D ** (-0.5)
    attn_rates, wide_rates = (rate, (D * 16 / SEQ) ** (-0.5)), (rate, FF ** (-0.5))
    attn_state = (qkv_weight, qkv_moment, qkv_square, out_weight, out_moment, out_square)
    wide_state = (up_weight, up_moment, up_square, down_weight, down_moment, down_square)

    pieces, last_sum = down_grad(grad, hidden, places)
    steps.end(last_sum)
    down_one_grad = Scatter(pieces)
    steps.send(*down_one_grad.far())
    pieces, part, bias_sum = mlp_grads(1, steps.gate(grad))
    steps.end(part)
    part = steps.gate(part)

    up_one_grad = Scatter(pieces)
    steps.send(*down_one_grad.rest(), *up_one_grad.far())
    grad_mid, middle_sums, pieces, part, proj_sums = attn_grads(1, grad, part)
    steps.end(part)
    part = steps.gate(part)

    attn_one_grad = Scatter(pieces)
    steps.send(*up_one_grad.rest(), *attn_one_grad.far())
    total = down_one_grad.total(up_one_grad.merged())
    down_grad_sum = scatter_tp(total)
    part = behind(part, total)
    grad, input_sums = input_back(
        1, grad_mid, (part, core_swap(part)), stored[1][0], row_vectors, WIDE
    )
    vector_one = vector_grad(input_sums, middle_sums, last_sum, proj_sums, bias_sum)
    pieces, last_sum = down_grad(grad, stored[0][-1], places)
    steps.end(last_sum)

    down_zero_grad = Scatter(pieces)
    steps.send(*attn_one_grad.rest(), *down_zero_grad.far())
    total = up_one_grad.total(attn_one_grad.merged())
    up_grad_sum = scatter_tp(total)
    pieces, part, bias_sum = mlp_grads(0, steps.gate(behind(grad, total)))
    steps.end(part)
    part = steps.gate(part)

    up_zero_grad = Scatter(pieces)
    steps.send(*down_zero_grad.rest(), *up_zero_grad.far())
    total = attn_one_grad.total(down_zero_grad.merged())
    attn_grad = scatter_tp(total)
    part = behind(part, total)
    grad_mid, middle_sums, pieces, part, proj_sums = attn_grads(0, grad, part)
    steps.end(part)
    part = steps.gate(part)

    attn_zero_grad = Scatter(pieces)
    steps.send(*up_zero_grad.rest(), *attn_zero_grad.far())
    grad, input_sums = input_back(
        0, grad_mid, (part, core_swap(part)), stored[0][0], row_vectors, LOW
    )
    total = down_zero_grad.total((grad,))
    down_zero_sum = scatter_tp(total)
    vector_zero = vector_grad(input_sums, middle_sums, last_sum, proj_sums, bias_sum)
    vectors = jnp.stack([vector_zero, vector_one])
    last_part = mlp_down(behind(steps.gate(hidden), total), places, down_one, False)
    wide_new = adam(
        False,
        wide_rates,
        1,
        behind(steps.gate(core_scalar), last_part),
        both_halves(steps.gate(up_grad_sum)) + both_halves(steps.gate(down_grad_sum)),
        wide_state,
        (),
    )
    last = middle + (add_low(last_part, core_swap(last_part)) + row_vectors[1, 5])
    last = jnp.where(valid[:, None], last, 0.0).astype(LOW)
    out_parts = group_parts([grad, last])
    vectors = vector_tp(vectors)
    steps.end(out_parts.own, vectors, wide_new[0])

    steps.send(*attn_zero_grad.rest())
    total = up_zero_grad.total(attn_zero_grad.merged())
    up_zero_sum = scatter_tp(total)
    steps.send(*out_parts.moves)
    steps.end(total)

    parts = Exchange(attn_zero_grad.total())
    steps.send(*parts.moves)
    vectors = vector_plane(steps.gate(vectors))
    attn_new = adam(
        True,
        attn_rates,
        1,
        steps.gate(core_scalar),
        both_halves(steps.gate(attn_grad)),
        attn_state,
        (),
    )
    input_grad, activations = group_rows(out_parts, 2)
    input_grad = input_grad.astype(WIDE)
    wide_new = adam(
        False,
        wide_rates,
        0,
        behind(core_scalar, attn_new[0]),
        both_halves(steps.gate(up_zero_sum)) + both_halves(steps.gate(down_zero_sum)),
        wide_state,
        wide_new,
    )
    steps.end(input_grad, activations, vectors, attn_new[0], wide_new[0])
    terms = [parts.own] + [move.got for move in parts.moves]
    attn_halves = both_halves(add_low(*terms).astype(LOW))
    attn_new = adam(True, attn_rates, 0, core_scalar, attn_halves, attn_state, attn_new)
    vector_totals = vectors
    qkv_new, qkv_moment_new, qkv_square_new, qkv_copy = attn_new[:4]
    out_new, out_moment_new, out_square_new, out_copy = attn_new[4:]
    up_new, up_moment_new, up_square_new, up_copy = wide_new[:4]
    down_new, down_moment_new, down_square_new, down_copy = wide_new[4:]

    def own_block(values):
        mine = lax.dynamic_index_in_dim(values, tp_index, values.ndim - 2, keepdims=False)
        return by_core(mine, core_swap(mine), mine.ndim - 1)

    row_size = 6 * model_width
    block_size = tp_count * half_width
    row_sum = vector_totals[:, :row_size].reshape(LAYERS, 6, model_width)
    qv_total = own_block(
        vector_totals[:, row_size : row_size + 2 * block_size].reshape(
            LAYERS, 2, tp_count, half_width
        )
    )
    up_total = own_block(
        vector_totals[:, row_size + 2 * block_size :].reshape(LAYERS, tp_count, half_hidden)
    )
    row_new, row_moment_new, row_square_new = adamw_step(
        row_vectors, row_moment, row_square, row_sum, VECTOR_RATE, 0.0
    )
    qv_new, qv_moment_new, qv_square_new = adamw_step(
        qv_bias, qv_moment, qv_square, qv_total, VECTOR_RATE, 0.0
    )
    up_bias_new, bias_moment_new, bias_square_new = adamw_step(
        up_bias, bias_moment, bias_square, up_total, VECTOR_RATE, 0.0
    )
    return (
        activations,
        input_grad,
        qkv_new,
        qkv_moment_new,
        qkv_square_new,
        qkv_copy,
        out_new,
        out_moment_new,
        out_square_new,
        out_copy,
        up_new,
        up_moment_new,
        up_square_new,
        up_copy,
        down_new,
        down_moment_new,
        down_square_new,
        down_copy,
        row_new,
        row_moment_new,
        row_square_new,
        qv_new,
        qv_moment_new,
        qv_square_new,
        up_bias_new,
        bias_moment_new,
        bias_square_new,
    )


def solution(mesh):
    return jax.shard_map(
        shards,
        mesh=mesh,
        in_specs=(
            P("tp", "wide", None),
            P("tp", "wide", None),
            P("wide"),
            P(None, "wide", None, "tp"),
            P(None, "wide", None, "tp"),
            P(None, "wide", None, "tp"),
            P(None, "tp", "wide"),
            P(None, "tp", "wide"),
            P(None, "tp", "wide"),
            P(None, "wide", "tp"),
            P(None, "wide", "tp"),
            P(None, "wide", "tp"),
            P(None, "tp", "wide"),
            P(None, "tp", "wide"),
            P(None, "tp", "wide"),
            P(),
            P(),
            P(),
            P(None, None, "tp"),
            P(None, None, "tp"),
            P(None, None, "tp"),
            P(None, "tp"),
            P(None, "tp"),
            P(None, "tp"),
        ),
        out_specs=(
            P("tp", "wide", None),
            P("tp", "wide", None),
            P(None, "wide", None, "tp"),
            P(None, "wide", None, "tp"),
            P(None, "wide", None, "tp"),
            P(None, "wide", None, "tp"),
            P(None, "tp", "wide"),
            P(None, "tp", "wide"),
            P(None, "tp", "wide"),
            P(None, "tp", "wide"),
            P(None, "wide", "tp"),
            P(None, "wide", "tp"),
            P(None, "wide", "tp"),
            P(None, "wide", "tp"),
            P(None, "tp", "wide"),
            P(None, "tp", "wide"),
            P(None, "tp", "wide"),
            P(None, "tp", "wide"),
            P(),
            P(),
            P(),
            P(None, None, "tp"),
            P(None, None, "tp"),
            P(None, None, "tp"),
            P(None, "tp"),
            P(None, "tp"),
            P(None, "tp"),
        ),
        check_vma=False,
    )
```

```python
import functools

import jax
import jax.numpy as jnp
from jax import lax
from jax.experimental import pallas as pl
from jax.experimental.pallas import tpu as pltpu
from jax.sharding import PartitionSpec as P

D = 1024
HDIM = 64
FF = 4096
SEQ = 640
VALID = 577
LAYERS = 2
STEP = 10


NORM_EPS = 1e-05
BETA_ONE = 0.9
BETA_TWO = 0.999
ADAM_EPS = 1e-08
WEIGHT_DECAY = 0.01
VECTOR_RATE = 0.4
MASKED = -1e30
LOW = jnp.bfloat16
WIDE = jnp.float32
TILE = 128
MIB = 1 << 20
COST_PART = 1.0

def adamw_step(weight, moment, square, gradient, step_rate, decay_rate):
    moment = BETA_ONE * moment + (1.0 - BETA_ONE) * gradient
    square = BETA_TWO * square + (1.0 - BETA_TWO) * gradient * gradient
    moment_hat = moment / (1.0 - BETA_ONE**STEP)
    square_hat = square / (1.0 - BETA_TWO**STEP)
    weight = weight - step_rate * (
        moment_hat / (jnp.sqrt(square_hat) + ADAM_EPS) + decay_rate * weight
    )
    return (weight, moment, square)


def core_swap(values):
    return lax.ppermute(values, "wide", [(i, i ^ 1) for i in range(lax.axis_size("wide"))])


def pair_swap(values, bit):
    flip = 2 << bit
    return lax.ppermute(values, "wide", [(i, i ^ flip) for i in range(lax.axis_size("wide"))])


def cross_swap(values, second):
    moves = [(i, i ^ (2 << ((i + second) % 2))) for i in range(lax.axis_size("wide"))]
    return lax.ppermute(values, "wide", moves)


def neighbours():
    pair, core = lax.axis_index("wide") // 2, lax.axis_index("wide") % 2
    return pair, pair ^ (1 << core), pair ^ (2 >> core), pair ^ 3


def tp_shift(values, distance):
    count = lax.axis_size("tp")
    return lax.ppermute(values, "tp", [(i, (i + distance) % count) for i in range(count)])


def tp_flip(values, bit):
    count = lax.axis_size("tp")
    return lax.ppermute(values, "tp", [(i, i ^ (1 << bit)) for i in range(count)])


class Move:
    def __init__(self, move, values):
        self.move, self.values, self.got = move, values, None

    def send(self, after=()):
        values = self.values
        if after:
            values, _ = lax.optimization_barrier((values, tuple(after)))
        self.got = self.move(values)
        return self.got


def first_way(values):
    return Move(lambda v: cross_swap(v, 0), values)


def second_way(values):
    return Move(lambda v: cross_swap(v, 1), values)


def along_tp(values, distance):
    return Move(lambda v: tp_shift(v, distance), values)


def behind(values, first):
    return lax.optimization_barrier((values, first))[0]


class Steps:
    def __init__(self):
        self.ended = ()
        self.sent = []

    def gate(self, values):
        return behind(values, self.ended)

    def send(self, *moves, wait=True):
        for move in moves:
            move.send(self.ended)
        if wait:
            self.sent += moves

    def end(self, *arrays):
        self.ended = arrays + tuple(move.got for move in self.sent)
        for move in self.sent:
            move.got = self.gate(move.got)
        self.sent = []


def pair_bits():
    return (lax.axis_size("wide") // 2).bit_length() - 1


def by_core(mine, other, axis):
    lower = lax.axis_index("wide") % 2 == 0
    return jnp.where(
        lower,
        jnp.concatenate([mine, other], axis=axis),
        jnp.concatenate([other, mine], axis=axis),
    )


def half_of(values, which, axis):
    span = values.shape[axis] // 2
    return lax.dynamic_slice_in_dim(values, which * span, span, axis)


def relative(values, axis):
    pairs = lax.axis_size("wide") // 2
    pair = lax.axis_index("wide") // 2
    span = values.shape[axis] // pairs
    shape = values.shape
    for bit in range(pair_bits()):
        step = span << bit
        split = values.reshape(shape[:axis] + (-1, 2, step) + shape[axis + 1 :])
        lower, upper = (lax.index_in_dim(split, k, axis + 1) for k in (0, 1))
        flipped = jnp.concatenate([upper, lower], axis=axis + 1).reshape(shape)
        values = jnp.where((pair >> bit) & 1 == 1, flipped, values)
    return values


def piece_places():
    if pair_bits() == 2:
        starts = [pair * (D // 4) for pair in neighbours()]
    else:
        starts = [0] * 4
    return jnp.stack([jnp.asarray(v, jnp.int32) for v in starts + [lax.axis_index("tp")]])


GATHERED = ((0, 4, 0), (0, 4, 1), (0, 4, 2), (0, 2, 3), (2, 2, 3))
def gathered_spans():
    return GATHERED if pair_bits() == 2 else ((0, lax.axis_size("tp"), 0),)


def tp_moves(block):
    return [along_tp(block, d) for d in range(1, lax.axis_size("tp"))]


class Gather:
    def __init__(self, own):
        self.own = own
        self.near_moves, self.far_moves = [], []
        if pair_bits() == 2:
            self.near_moves = [first_way(own), second_way(own)]

    def near(self):
        return self.near_moves

    def far(self):
        if self.near_moves:
            half = self.own.shape[0] // 2
            first, second = (move.got for move in self.near_moves)
            self.far_moves = [second_way(first[:half]), first_way(second[half:])]
        return self.far_moves

    def pieces(self):
        if self.near_moves:
            return [self.own] + [move.got for move in self.near_moves + self.far_moves]
        own = self.own
        for bit in range(pair_bits()):
            own = jnp.concatenate([own, pair_swap(own, bit)], axis=1)
        return [relative(own, 1)]


def add_low(*terms):
    total = terms[0].astype(WIDE)
    for term in terms[1:]:
        total = total + term.astype(WIDE)
    return total


def own_sum_kernel(own, first, second, out):
    out[...] = add_low(own[...], first[...], second[...]).astype(LOW)


def merge_kernel(whole_part, half_part, out):
    out[...] = add_low(whole_part[...], half_part[...]).astype(LOW)


def merge(whole_part, half_part, first):
    span, rows, columns = half_part.shape
    block = pl.BlockSpec((1, rows, columns), lambda d: (first + d, 0, 0))
    return pl.pallas_call(
        merge_kernel,
        grid=(span,),
        in_specs=[block, pl.BlockSpec((1, rows, columns), lambda d: (d, 0, 0))],
        out_specs=block,
        out_shape=jax.ShapeDtypeStruct(whole_part.shape, LOW),
        input_output_aliases={0: 0},
        compiler_params=pltpu.CompilerParams(vmem_limit_bytes=24 * MIB),
        cost_estimate=cost(2),
    )(whole_part, half_part)


class Scatter:
    def __init__(self, pieces):
        self.pieces = pieces
        self.far_moves, self.rest_moves = [], []
        if len(pieces) > 1:
            self.far_moves = [second_way(pieces[-2]), first_way(pieces[-1])]

    def far(self):
        return self.far_moves

    def rest(self):
        if self.far_moves:
            low, high = (move.got for move in self.far_moves)
            first = merge(self.pieces[1], low, 0)
            second = merge(self.pieces[2], high, high.shape[0])
            self.rest_moves = [first_way(first), second_way(second)]
        return self.rest_moves

    def merged(self):
        return tuple(move.values for move in self.rest_moves)

    def total(self, after=()):
        own = behind(self.pieces[0], after)
        if not self.far_moves:
            own = relative(own, 1)
            for bit in reversed(range(pair_bits())):
                keep = own.shape[1] // 2
                own = add_low(own[:, :keep], pair_swap(own[:, keep:], bit)).astype(LOW)
            return own
        return pl.pallas_call(
            own_sum_kernel,
            out_shape=jax.ShapeDtypeStruct(own.shape, LOW),
            compiler_params=pltpu.CompilerParams(vmem_limit_bytes=24 * MIB),
            cost_estimate=cost(2),
        )(own, *[move.got for move in self.rest_moves])


def both_halves(total):
    core = lax.axis_index("wide") % 2
    return total, core_swap(half_of(total, 1 - core, 0).astype(LOW))


def scatter_tp(blocks):
    return lax.psum_scatter(blocks, "tp", scatter_dimension=0, tiled=False)


def by_source_kernel(place, *refs):
    *blocks, out = refs
    total = len(blocks)
    for d, block in enumerate(blocks):
        out[lax.rem(place[0] + (total - d), total)] = block[...]


def by_source(got):
    place = lax.axis_index("tp").astype(jnp.int32).reshape(1)
    return pl.pallas_call(
        by_source_kernel,
        in_specs=[pl.BlockSpec(memory_space=pltpu.SMEM)]
        + [pl.BlockSpec(memory_space=pltpu.VMEM)] * len(got),
        out_shape=jax.ShapeDtypeStruct((len(got),) + got[0].shape, got[0].dtype),
        compiler_params=pltpu.CompilerParams(vmem_limit_bytes=16 * MIB),
        cost_estimate=cost(1),
    )(place, *got)


class Exchange:
    def __init__(self, blocks):
        tp_index = lax.axis_index("tp")
        tp_count = lax.axis_size("tp")
        own, *others = (
            lax.dynamic_index_in_dim(blocks, (tp_index + d) % tp_count, 0, keepdims=False)
            for d in range(tp_count)
        )
        self.own = own
        self.moves = [along_tp(block, d + 1) for d, block in enumerate(others)]

    def result(self):
        return by_source([self.own] + [move.got for move in self.moves])


def image_parts(values):
    core = lax.axis_index("wide") % 2
    slots = jnp.stack([values[:, 0], values[:, 1]])
    other = core_swap(half_of(slots, 1 - core, 1))
    return Exchange(by_core(half_of(slots, core, 1), other, 0))


def image_rows(exchange):
    rows = exchange.result()
    return by_core(rows, core_swap(rows), 1).reshape(-1, rows.shape[2])


def group_parts(arrays):
    core = lax.axis_index("wide") % 2
    tp_count = lax.axis_size("tp")
    halves = [half_of(a.reshape(tp_count, -1, a.shape[1]), core, 1) for a in arrays]
    return Exchange(jnp.concatenate(halves, axis=1))


def group_rows(exchange, count):
    core = lax.axis_index("wide") % 2
    images = exchange.result()
    other = core_swap(half_of(images, 1 - core, 0))
    mine = half_of(images, core, 0)
    rows = images.shape[1] // count
    outs = []
    for k in range(count):
        here = slice(k * rows, (k + 1) * rows)
        slots = by_core(mine[:, here], other[:, here], 1)
        outs.append(jnp.stack([slots[0], slots[1]], axis=1))
    return outs


def vector_tp(values):
    for bit in range(lax.axis_size("tp").bit_length() - 1):
        values = values + tp_flip(values, bit)
    return values


def vector_plane(values):
    for bit in range(pair_bits()):
        values = values + pair_swap(values, bit)
    return values


def cost(time):
    return pl.CostEstimate(
        flops=int(time * COST_PART * 1.1e9),
        bytes_accessed=int(time * COST_PART * 3.4e6),
        transcendentals=0,
    )


SCALARS = pl.BlockSpec(memory_space=pltpu.SMEM)
FAR = pl.BlockSpec(memory_space=pl.ANY)


def whole(shape):
    return pl.BlockSpec(shape, lambda *_: (0,) * len(shape))


def mat(left, right):
    return jnp.dot(left, right, preferred_element_type=WIDE)


def mat_back(left, right):
    return lax.dot_general(left, right, (((1,), (1,)), ((), ())), preferred_element_type=WIDE)


def flip(values):
    return values.T


def fetch(places, refs, held, sems, column, width, turned=False):
    copies = []
    for ref, (first, span, place) in zip(refs, gathered_spans()):
        rows = pl.ds(pl.multiple_of(places[place], TILE), ref.shape[1])
        columns = pl.ds(column, width)
        if turned:
            total = held.shape[0]
            for z in range(span):
                block = lax.rem(places[4] + (total - first - z), total)
                copies.append((ref.at[z, :, columns], held.at[block, rows, :]))
        else:
            copies.append((ref.at[:, :, columns], held.at[pl.ds(first, span), rows, :]))
    return [pltpu.make_async_copy(*pair, sems.at[k]) for k, pair in enumerate(copies)]


def fetch_joined(places, refs, held, sems, column, width, turned=False):
    copies = []
    for ref, (first, span, place) in zip(refs, gathered_spans()):
        rows = pl.ds(pl.multiple_of(places[place], TILE), ref.shape[1])
        total = held.shape[1] // width
        for z in range(span):
            block = lax.rem(places[4] + (total - first - z), total) if turned else first + z
            there = held.at[rows, pl.ds(pl.multiple_of(block * width, TILE), width)]
            copies.append((ref.at[z, :, pl.ds(column, width)], there))
    return [pltpu.make_async_copy(*pair, sems.at[k]) for k, pair in enumerate(copies)]


def start_all(copies):
    for copy in copies:
        copy.start()


def wait_all(copies):
    for copy in copies:
        copy.wait()


def norm_parts(values):
    center = values - jnp.mean(values, axis=-1, keepdims=True)
    scale = lax.rsqrt(jnp.mean(center * center, axis=-1, keepdims=True) + NORM_EPS)
    return center * scale, scale


def norm_back(values, gain, grad):
    unit, scale = norm_parts(values)
    scaled = grad * gain
    inner = scaled - jnp.mean(scaled, axis=-1, keepdims=True)
    inner = inner - unit * jnp.mean(scaled * unit, axis=-1, keepdims=True)
    return (
        inner * scale,
        jnp.sum(grad * unit, axis=0, keepdims=True),
        jnp.sum(grad, axis=0, keepdims=True),
    )


def pack_attn_kernel(core, qkv, out, mine, other):
    half = qkv.shape[3] // 2

    def put(ref, first):
        for kind in range(3):
            ref[:, kind * half : (kind + 1) * half] = qkv[
                0, :, kind, first * half : (first + 1) * half
            ].astype(LOW)
        ref[:, 3 * half :] = out[0, first * half : (first + 1) * half, :].T.astype(LOW)

    @pl.when(core[0] == 0)
    def _():
        put(mine, 0)
        put(other, 1)

    @pl.when(core[0] == 1)
    def _():
        put(mine, 1)
        put(other, 0)


def pack_mlp_kernel(core, up, down, mine, other):
    half = up.shape[2] // 2

    def put(ref, first):
        ref[:, :half] = up[0, :, first * half : (first + 1) * half].astype(LOW)
        ref[:, half:] = down[0, first * half : (first + 1) * half, :].T.astype(LOW)

    @pl.when(core[0] == 0)
    def _():
        put(mine, 0)
        put(other, 1)

    @pl.when(core[0] == 1)
    def _():
        put(mine, 1)
        put(other, 0)


def adam_kernel(is_attn, rates, core, *refs):
    grads, refs = refs[: 2 if is_attn else 4], refs[2 if is_attn else 4 :]
    ins, outs = refs[:6], refs[-8:]
    half_rows = grads[1].shape[0]
    first = pl.ds(pl.multiple_of(core[0] * half_rows, 16), half_rows)

    def grad_of(mine, which, columns):
        total, other = grads[2 * which : 2 * which + 2] if not is_attn else grads
        return (total[first, columns] if mine else other[:, columns]).astype(WIDE)

    def step(which, index, grad):
        weight, moment, square = (r[index] for r in ins[3 * which : 3 * which + 3])
        new, moment, square = adamw_step(weight, moment, square, grad, rates[which], WEIGHT_DECAY)
        for out, value in zip(outs[4 * which :], (new, moment, square, new.astype(LOW))):
            out[index] = value

    def put(here):
        width = ins[0].shape[-1] // 2
        for side in (0, 1):
            columns = slice(side * width, (side + 1) * width)
            if is_attn:
                for kind in range(3):
                    part = grad_of(side == here, 0, slice(kind * width, (kind + 1) * width))
                    step(0, (0, slice(None), kind, columns), part)
                rest = grad_of(side == here, 0, slice(3 * width, 4 * width))
            else:
                step(0, (0, slice(None), columns), grad_of(side == here, 0, slice(None)))
                rest = grad_of(side == here, 1, slice(None))
            step(1, (0, columns, slice(None)), rest.T)

    pl.when(core[0] == 0)(lambda: put(0))
    pl.when(core[0] == 1)(lambda: put(1))


def adam(is_attn, rates, layer, core, grads, arrays, before):
    shapes = [
        jax.ShapeDtypeStruct(arrays[3 * m].shape, LOW if k == 3 else WIDE)
        for m in range(2)
        for k in range(4)
    ]
    first = 1 + len(grads) + len(arrays)
    return pl.pallas_call(
        functools.partial(adam_kernel, is_attn, rates),
        grid=(1,),
        in_specs=[SCALARS]
        + [whole(g.shape) for g in grads]
        + [layer_block(a, layer) for a in arrays]
        + [FAR] * len(before),
        out_specs=[layer_block(s, layer) for s in shapes],
        out_shape=shapes,
        input_output_aliases={first + k: k for k in range(len(before))},
        compiler_params=pltpu.CompilerParams(vmem_limit_bytes=60 * MIB),
        cost_estimate=cost(5),
    )(core, *grads, *arrays, *before)


def layer_block(array, layer):
    shape = (1,) + array.shape[1:]
    return pl.BlockSpec(shape, lambda *_: (layer,) + (0,) * (len(shape) - 1))


def pack(kernel, layer, core, first, second, columns):
    rows = lax.axis_size("wide")
    shape = jax.ShapeDtypeStruct((D // rows, columns), LOW)
    return pl.pallas_call(
        kernel,
        grid=(1,),
        in_specs=[SCALARS, layer_block(first, layer), layer_block(second, layer)],
        out_specs=[whole(shape.shape)] * 2,
        out_shape=[shape] * 2,
        compiler_params=pltpu.CompilerParams(vmem_limit_bytes=16 * MIB),
        cost_estimate=cost(1),
    )(core, first, second)


def project_kernel(layer, joined, turned, places, *refs):
    if joined:
        stream, own, got, vectors, bias, *refs = refs
        *weights, kept, normed, proj, held, sems = refs
    else:
        stream, vectors, bias, *refs = refs
        *weights, normed, proj, held, sems = refs
    width = held.shape[2]
    copies = fetch(places, weights, held, sems, 0, width, turned)
    pl.when(pl.program_id(0) == 0)(lambda: start_all(copies))
    values = stream[...].astype(WIDE)
    if joined:
        values = values + (add_low(own[...], got[...]) + vectors[layer - 1, 5:6, :])
        kept[...] = values
    low = (norm_parts(values)[0] * vectors[layer, 0:1, :] + vectors[layer, 1:2, :]).astype(LOW)
    normed[...] = low
    pl.when(pl.program_id(0) == 0)(lambda: wait_all(copies))
    for z in range(held.shape[0]):
        here = slice(z * width, (z + 1) * width)
        proj[:, here] = (mat(low, held[z]) + bias[:, here]).astype(LOW)


def project(layer, stream, partial, vectors, bias, places, pieces, turned):
    rows = stream.shape[0]
    steps = 2
    tp_count = lax.axis_size("tp")
    columns = bias.shape[1]
    tile = pl.BlockSpec((rows // steps, D), lambda i: (i, 0))
    streams = [stream] + list(partial)
    out_shape = [
        jax.ShapeDtypeStruct((rows, D), LOW),
        jax.ShapeDtypeStruct((rows, columns), LOW),
    ]
    out_specs = [tile, pl.BlockSpec((rows // steps, columns), lambda i: (i, 0))]
    if partial:
        out_shape = [jax.ShapeDtypeStruct((rows, D), WIDE)] + out_shape
        out_specs = [tile] + out_specs
    return pl.pallas_call(
        functools.partial(project_kernel, layer, bool(partial), turned),
        grid=(steps,),
        in_specs=[SCALARS]
        + [tile] * len(streams)
        + [whole(vectors.shape), whole(bias.shape)]
        + [FAR] * len(pieces),
        out_specs=out_specs,
        out_shape=out_shape,
        scratch_shapes=[
            pltpu.VMEM((tp_count, D, columns // tp_count), LOW),
            pltpu.SemaphoreType.DMA((tp_count * len(pieces),)),
        ],
        compiler_params=pltpu.CompilerParams(vmem_limit_bytes=40 * MIB),
        cost_estimate=cost(6),
    )(places, *streams, vectors, bias, *pieces)


def head_rows(values):
    turned = flip(values)
    upper = lax.broadcasted_iota(jnp.int32, turned.shape, 0) < HDIM
    zero = jnp.zeros_like(turned)
    return jnp.where(upper, turned, zero), jnp.where(upper, zero, turned)


def put_head_rows(held, values):
    first, second = head_rows(values)
    for t in range(held.shape[0]):
        held[t, :, :TILE] = first[:, t * TILE : (t + 1) * TILE]
        held[t, :, TILE:] = second[:, t * TILE : (t + 1) * TILE]


def put_head_columns(held, values):
    left = lax.broadcasted_iota(jnp.int32, values.shape, 1) < HDIM
    zero = jnp.zeros_like(values)
    first, second = jnp.where(left, values, zero), jnp.where(left, zero, values)
    for t in range(held.shape[0]):
        held[t, :TILE, :] = first[t * TILE : (t + 1) * TILE, :]
        held[t, TILE:, :] = second[t * TILE : (t + 1) * TILE, :]


def merge_heads(values):
    upper = lax.broadcasted_iota(jnp.int32, (2 * HDIM, TILE), 0) < HDIM
    return jnp.where(upper, values[:, :TILE], values[:, TILE:]).T


def keep_positions(scores):
    clear = VALID // 8 * 8
    rows = clear + lax.broadcasted_iota(jnp.int32, (scores.shape[0] - clear, scores.shape[1]), 0)
    last = jnp.where(rows < VALID, scores[clear:], MASKED)
    return jnp.concatenate([scores[:clear], last], axis=0)


def attend_kernel(turned, places, proj, *refs):
    *weights, attended, totals, partial, held_out, held_att, query_rows, sems = refs
    z = pl.program_id(0)
    width = 2 * HDIM
    tiles = query_rows.shape[0]
    copies = fetch_joined(places, weights, held_out, sems, 3 * width, width, turned)
    pl.when(z == 0)(lambda: start_all(copies))
    put_head_rows(query_rows, proj[:, :width] * LOW(HDIM**-0.5))
    value_rows = flip(proj[:, 2 * width :])
    key_rows = proj[:, width : 2 * width]

    def one(t, carried):
        scores = keep_positions(mat(key_rows, query_rows[t]))
        highest = jnp.max(scores, axis=0, keepdims=True)
        exponent = jnp.exp(scores - highest)
        total = jnp.sum(exponent, axis=0, keepdims=True)
        probs = (exponent * (1.0 / total)).astype(LOW)
        totals[0, pl.ds(t, 1), :] = highest + jnp.log(total)
        result = merge_heads(mat(value_rows, probs)).astype(LOW)
        attended[pl.ds(pl.multiple_of(t * TILE, TILE), TILE), :] = result
        return carried

    lax.fori_loop(0, tiles, one, 0, unroll=True)
    for k in range(held_att.shape[1] // width):

        @pl.when(z == k)
        def _():
            held_att[:, k * width : (k + 1) * width] = attended[...]

    @pl.when(z == pl.num_programs(0) - 1)
    def _():
        wait_all(copies)
        partial[...] = mat_back(held_att[...], held_out[...]).astype(LOW)


def attend(proj, places, pieces, turned):
    rows = proj.shape[0]
    tp_count = lax.axis_size("tp")
    width = 2 * HDIM
    tiles = rows // TILE
    return pl.pallas_call(
        functools.partial(attend_kernel, turned),
        grid=(tp_count,),
        in_specs=[SCALARS, pl.BlockSpec((rows, 3 * width), lambda z: (0, z))]
        + [FAR] * len(pieces),
        out_specs=[
            pl.BlockSpec((rows, width), lambda z: (0, z)),
            pl.BlockSpec((1, tiles, 2 * TILE), lambda z: (z, 0, 0)),
            whole((rows, D)),
        ],
        out_shape=[
            jax.ShapeDtypeStruct((rows, tp_count * width), LOW),
            jax.ShapeDtypeStruct((tp_count, tiles, 2 * TILE), WIDE),
            jax.ShapeDtypeStruct((rows, D), LOW),
        ],
        scratch_shapes=[
            pltpu.VMEM((D, tp_count * width), LOW),
            pltpu.VMEM((rows, tp_count * width), LOW),
            pltpu.VMEM((tiles, width, 2 * TILE), LOW),
            pltpu.SemaphoreType.DMA((tp_count * len(pieces),)),
        ],
        compiler_params=pltpu.CompilerParams(vmem_limit_bytes=40 * MIB),
        cost_estimate=cost(18),
    )(places, proj, *pieces)


def mlp_kernel(layer, turned, count, down_too, places, stream, own, got, vectors, bias, *refs):
    ups, refs = refs[:count], refs[count:]
    if down_too:
        downs, refs = refs[:count], refs[count:]
        middle, normed, pre_act, hidden, partial, held_up, up_sems, held_down, down_sems = refs
    else:
        middle, normed, pre_act, hidden, held_up, up_sems = refs
    width = held_up.shape[2]
    first = pl.program_id(0) == 0
    up_copies = fetch(places, ups, held_up, up_sems, 0, width, turned)
    pl.when(first)(lambda: start_all(up_copies))
    if down_too:
        down_copies = fetch(places, downs, held_down, down_sems, 0, width, turned)
        pl.when(first)(lambda: start_all(down_copies))
    values = stream[...].astype(WIDE) + (add_low(own[...], got[...]) + vectors[layer, 4:5, :])
    middle[...] = values
    low = (norm_parts(values)[0] * vectors[layer, 2:3, :] + vectors[layer, 3:4, :]).astype(LOW)
    normed[...] = low
    total = None
    pl.when(first)(lambda: wait_all(up_copies))
    for z in range(held_up.shape[0]):
        here = slice(z * width, (z + 1) * width)
        pre = mat(low, held_up[z]) + bias[:, here]
        pre_act[:, here] = pre
        act = (pre / (1.0 + jnp.exp(-1.702 * pre))).astype(LOW)
        hidden[:, here] = act
        if down_too:
            if z == 0:
                pl.when(first)(lambda: wait_all(down_copies))
            term = mat_back(act, held_down[z])
            total = term if total is None else total + term
    if down_too:
        partial[...] = total.astype(LOW)


def mlp(layer, stream, partial, vectors, bias, places, ups, downs, turned):
    rows = stream.shape[0]
    steps = 2
    tp_count = lax.axis_size("tp")
    columns = bias.shape[1]
    tile = pl.BlockSpec((rows // steps, D), lambda i: (i, 0))
    broad = pl.BlockSpec((rows // steps, columns), lambda i: (i, 0))
    held = [
        pltpu.VMEM((tp_count, D, columns // tp_count), LOW),
        pltpu.SemaphoreType.DMA((tp_count * len(ups),)),
    ]
    down_too = 1 if downs else 0
    return pl.pallas_call(
        functools.partial(mlp_kernel, layer, turned, len(ups), bool(downs)),
        grid=(steps,),
        in_specs=[SCALARS]
        + [tile] * 3
        + [whole(vectors.shape), whole(bias.shape)]
        + [FAR] * (len(ups) + len(downs)),
        out_specs=[tile, tile, broad, broad] + [tile] * down_too,
        out_shape=[
            jax.ShapeDtypeStruct((rows, D), WIDE),
            jax.ShapeDtypeStruct((rows, D), LOW),
            jax.ShapeDtypeStruct((rows, columns), WIDE),
            jax.ShapeDtypeStruct((rows, columns), LOW),
        ]
        + [jax.ShapeDtypeStruct((rows, D), LOW)] * down_too,
        scratch_shapes=held * (1 + down_too),
        compiler_params=pltpu.CompilerParams(vmem_limit_bytes=52 * MIB),
        cost_estimate=cost(15 if downs else 9),
    )(places, stream, *partial, vectors, bias, *ups, *downs)


def mlp_down_kernel(turned, places, hidden, *refs):
    *downs, partial, held, sems = refs
    width = held.shape[2]
    copies = fetch(places, downs, held, sems, 0, width, turned)
    start_all(copies)
    wait_all(copies)
    total = None
    for z in range(held.shape[0]):
        term = mat_back(hidden[:, z * width : (z + 1) * width], held[z])
        total = term if total is None else total + term
    partial[...] = total.astype(LOW)


def mlp_down(hidden, places, downs, turned):
    rows, columns = hidden.shape
    tp_count = lax.axis_size("tp")
    return pl.pallas_call(
        functools.partial(mlp_down_kernel, turned),
        grid=(1,),
        in_specs=[SCALARS, whole(hidden.shape)] + [FAR] * len(downs),
        out_specs=whole((rows, D)),
        out_shape=jax.ShapeDtypeStruct((rows, D), LOW),
        scratch_shapes=[
            pltpu.VMEM((tp_count, D, columns // tp_count), LOW),
            pltpu.SemaphoreType.DMA((tp_count * len(downs),)),
        ],
        compiler_params=pltpu.CompilerParams(vmem_limit_bytes=48 * MIB),
        cost_estimate=cost(8),
    )(places, hidden, *downs)


def put_pieces(places, held, outs, shape, columns=slice(None)):
    z = pl.program_id(0)
    for out, (first, span, place) in zip(outs, shape):

        @pl.when((z >= first) & (z < first + span))
        def _():
            rows = pl.ds(pl.multiple_of(places[place], TILE), out.shape[1])
            out[0, :, columns] = held[rows, :]


def down_grad_kernel(places, grad, hidden, *refs):
    *outs, row_sum, low_turned, result = refs

    @pl.when(pl.program_id(0) == 0)
    def _():
        values = grad[...].astype(LOW)
        low_turned[...] = flip(values)
        row_sum[...] = jnp.sum(values.astype(WIDE), axis=0, keepdims=True)

    result[...] = mat(low_turned[...], hidden[...]).astype(LOW)
    put_pieces(places, result, outs, gathered_spans())


def mlp_back_kernel(count, turned, places, grad, normed, pre_act, *refs):
    ups, downs, refs = refs[:count], refs[count : 2 * count], refs[2 * count :]
    outs, refs = refs[:count], refs[count:]
    partial, bias_sum, held_up, held_down, low, normed_turned, result, total, sems = refs
    z = pl.program_id(0)
    width = held_up.shape[2]
    down_copies = fetch(places, downs, held_down, sems.at[1], 0, width, turned)
    up_copies = fetch(places, ups, held_up, sems.at[0], 0, width, turned)

    @pl.when(z == 0)
    def _():
        start_all(down_copies)
        start_all(up_copies)
        low[...] = grad[...].astype(LOW)
        normed_turned[...] = flip(normed[...])

    pre = pre_act[...]
    gate = 1.0 / (1.0 + jnp.exp(-1.702 * pre))
    slope = gate * (1.0 + 1.702 * pre * (1.0 - gate))
    pl.when(z == 0)(lambda: wait_all(down_copies))
    grad_pre = (mat(low[...], held_down[z]) * slope).astype(LOW)
    bias_sum[0] = jnp.sum(grad_pre.astype(WIDE), axis=0, keepdims=True)
    result[...] = mat(normed_turned[...], grad_pre).astype(LOW)
    put_pieces(places, result, outs, gathered_spans())
    pl.when(z == 0)(lambda: wait_all(up_copies))
    term = mat_back(grad_pre, held_up[z])

    @pl.when(z == 0)
    def _():
        total[...] = term

    @pl.when(z > 0)
    def _():
        total[...] += term

    @pl.when(z == pl.num_programs(0) - 1)
    def _():
        partial[...] = total[...].astype(LOW)


def piece_outs(width):
    spans = gathered_spans()
    rows = D // 4 if len(spans) > 1 else D

    def spec(first, span):
        return pl.BlockSpec((1, rows, width), lambda z: (jnp.clip(z - first, 0, span - 1), 0, 0))

    shapes = [jax.ShapeDtypeStruct((span, rows, width), LOW) for _, span, _ in spans]
    return shapes, [spec(first, span) for first, span, _ in spans]


def down_grad(grad, hidden, places):
    rows, columns = hidden.shape
    tp_count = lax.axis_size("tp")
    width = columns // tp_count
    shapes, specs = piece_outs(width)
    outs = pl.pallas_call(
        down_grad_kernel,
        grid=(tp_count,),
        in_specs=[SCALARS, whole((rows, D)), pl.BlockSpec((rows, width), lambda z: (0, z))],
        out_specs=specs + [whole((1, D))],
        out_shape=shapes + [jax.ShapeDtypeStruct((1, D), WIDE)],
        scratch_shapes=[pltpu.VMEM((D, rows), LOW), pltpu.VMEM((D, width), LOW)],
        compiler_params=pltpu.CompilerParams(vmem_limit_bytes=40 * MIB),
        cost_estimate=cost(7),
    )(places, grad, hidden)
    return outs[:-1], outs[-1]


def mlp_back(grad, normed, pre_act, places, ups, downs, turned):
    rows, columns = pre_act.shape
    tp_count = lax.axis_size("tp")
    width = columns // tp_count
    shapes, specs = piece_outs(width)
    held = pltpu.VMEM((tp_count, D, width), LOW)
    outs = pl.pallas_call(
        functools.partial(mlp_back_kernel, len(ups), turned),
        grid=(tp_count,),
        in_specs=[
            SCALARS,
            whole((rows, D)),
            whole((rows, D)),
            pl.BlockSpec((rows, width), lambda z: (0, z)),
        ]
        + [FAR] * (len(ups) + len(downs)),
        out_specs=specs + [whole((rows, D)), pl.BlockSpec((1, 1, width), lambda z: (z, 0, 0))],
        out_shape=shapes
        + [
            jax.ShapeDtypeStruct((rows, D), LOW),
            jax.ShapeDtypeStruct((tp_count, 1, width), WIDE),
        ],
        scratch_shapes=[
            held,
            held,
            pltpu.VMEM((rows, D), LOW),
            pltpu.VMEM((D, rows), LOW),
            pltpu.VMEM((D, width), LOW),
            pltpu.VMEM((rows, D), WIDE),
            pltpu.SemaphoreType.DMA((2, tp_count * len(ups))),
        ],
        compiler_params=pltpu.CompilerParams(vmem_limit_bytes=56 * MIB),
        cost_estimate=cost(20),
    )(places, grad, normed, pre_act, *ups, *downs)
    return outs[:-2], *outs[-2:]


def middle_back_kernel(
    layer, count, turned, places, grad, own, got, middle, vectors, attended, *refs
):
    weights, refs = refs[:count], refs[count:]
    grad_out, grad_mid, grad_att, sums, held, low, kept_sums, sems = refs
    step = pl.program_id(0)
    width = 2 * HDIM
    copies = fetch_joined(places, weights, held, sems, 3 * width, width, turned)
    pl.when(step == 0)(lambda: start_all(copies))
    back, gain_sum, shift_sum = norm_back(
        middle[...], vectors[layer, 2:3, :], add_low(own[...], got[...])
    )
    values = grad[...] + back
    grad_mid[...] = values
    values = values.astype(LOW)
    tile = values.shape[0]
    low[pl.ds(pl.multiple_of(step * tile, tile), tile), :] = values
    parts = jnp.concatenate(
        [gain_sum, shift_sum, jnp.sum(values.astype(WIDE), axis=0, keepdims=True)], axis=0
    )

    @pl.when(step == 0)
    def _():
        kept_sums[0:3, :] = parts

    @pl.when(step > 0)
    def _():
        kept_sums[0:3, :] += parts

    @pl.when(step == pl.num_programs(0) - 1)
    def _():
        sums[...] = kept_sums[...]
        grad_out[...] = mat(flip(low[...]), attended[...]).astype(LOW)
        wait_all(copies)
        grad_att[...] = mat(low[...], held[...]).astype(LOW)


def middle_back(
    layer, grad, partial, middle, vectors, attended, places, pieces, turned
):
    rows = grad.shape[0]
    steps = 4
    tp_count = lax.axis_size("tp")
    columns = attended.shape[1]
    tile = pl.BlockSpec((rows // steps, D), lambda i: (i, 0))
    outs = pl.pallas_call(
        functools.partial(middle_back_kernel, layer, len(pieces), turned),
        grid=(steps,),
        in_specs=[SCALARS]
        + [tile] * 4
        + [whole(vectors.shape), whole((rows, columns))]
        + [FAR] * len(pieces),
        out_specs=[whole((D, columns)), tile, whole((rows, columns)), whole((8, D))],
        out_shape=[
            jax.ShapeDtypeStruct((D, columns), LOW),
            jax.ShapeDtypeStruct((rows, D), WIDE),
            jax.ShapeDtypeStruct((rows, columns), LOW),
            jax.ShapeDtypeStruct((8, D), WIDE),
        ],
        scratch_shapes=[
            pltpu.VMEM((D, columns), LOW),
            pltpu.VMEM((rows, D), LOW),
            pltpu.VMEM((8, D), WIDE),
            pltpu.SemaphoreType.DMA((tp_count * len(pieces),)),
        ],
        compiler_params=pltpu.CompilerParams(vmem_limit_bytes=48 * MIB),
        cost_estimate=cost(9),
    )(places, grad, *partial, middle, vectors, attended, *pieces)
    return outs


def attend_back_kernel(
    count, turned, places, proj, totals, grad_att, normed, grad_out, *refs
):
    weights, refs = refs[:count], refs[count:]
    outs, refs = refs[: len(gathered_spans())], refs[len(gathered_spans()) :]
    (
        partial,
        sums,
        held,
        normed_turned,
        query_rows,
        grad_rows,
        query_columns,
        grad_columns,
        grad_proj,
        result,
        total,
        key_sum,
        value_sum,
        key_turned,
        sems,
    ) = refs
    z = pl.program_id(0)
    width = 2 * HDIM
    tiles = query_rows.shape[0]
    copies = fetch(places, weights, held, sems, 0, 3 * width, turned)

    @pl.when(z == 0)
    def _():
        start_all(copies)
        normed_turned[...] = flip(normed[...])

    scaled = proj[:, :width] * LOW(HDIM**-0.5)
    put_head_rows(query_rows, scaled)
    put_head_columns(query_columns, scaled)
    put_head_rows(grad_rows, grad_att[...])
    put_head_columns(grad_columns, grad_att[...])
    key_rows = proj[:, width : 2 * width]
    value_rows = proj[:, 2 * width :]
    key_turned[...] = flip(key_rows)
    key_sum[...] = jnp.zeros_like(key_sum)
    value_sum[...] = jnp.zeros_like(value_sum)

    def one(t, carried):
        scores = keep_positions(mat(key_rows, query_rows[t]))
        probs = jnp.exp(scores - totals[0, pl.ds(t, 1), :])
        value_sum[...] += mat(probs.astype(LOW), grad_columns[t])
        grad_probs = mat(value_rows, grad_rows[t])
        inner = jnp.sum(probs * grad_probs, axis=0, keepdims=True)
        grad_scores = (probs * (grad_probs - inner)).astype(LOW)
        key_sum[...] += mat(grad_scores, query_columns[t])
        grad_query = merge_heads(mat(key_turned[...], grad_scores)) * HDIM**-0.5
        grad_proj[pl.ds(pl.multiple_of(t * TILE, TILE), TILE), :width] = grad_query.astype(LOW)
        return carried

    lax.fori_loop(0, tiles, one, 0, unroll=True)
    grad_proj[:, width : 2 * width] = key_sum[...].astype(LOW)
    grad_proj[:, 2 * width :] = value_sum[...].astype(LOW)
    grads = grad_proj[...]
    sums[0] = jnp.sum(grads.astype(WIDE), axis=0, keepdims=True)
    result[...] = mat(normed_turned[...], grads).astype(LOW)
    put_pieces(places, result, outs, gathered_spans(), slice(0, 3 * width))
    put_pieces(places, grad_out, outs, gathered_spans(), slice(3 * width, 4 * width))
    pl.when(z == 0)(lambda: wait_all(copies))
    term = mat_back(grads, held[z])

    @pl.when(z == 0)
    def _():
        total[...] = term

    @pl.when(z > 0)
    def _():
        total[...] += term

    @pl.when(z == pl.num_programs(0) - 1)
    def _():
        partial[...] = total[...].astype(LOW)


def attend_back(
    proj, totals, grad_att, normed, grad_out, places, pieces, turned
):
    rows = proj.shape[0]
    tp_count = lax.axis_size("tp")
    width = 2 * HDIM
    tiles = rows // TILE
    shapes, specs = piece_outs(4 * width)
    outs = pl.pallas_call(
        functools.partial(attend_back_kernel, len(pieces), turned),
        grid=(tp_count,),
        in_specs=[
            SCALARS,
            pl.BlockSpec((rows, 3 * width), lambda z: (0, z)),
            pl.BlockSpec((1, tiles, 2 * TILE), lambda z: (z, 0, 0)),
            pl.BlockSpec((rows, width), lambda z: (0, z)),
            whole((rows, D)),
            pl.BlockSpec((D, width), lambda z: (0, z)),
        ]
        + [FAR] * len(pieces),
        out_specs=specs
        + [whole((rows, D)), pl.BlockSpec((1, 1, 3 * width), lambda z: (z, 0, 0))],
        out_shape=shapes
        + [
            jax.ShapeDtypeStruct((rows, D), LOW),
            jax.ShapeDtypeStruct((tp_count, 1, 3 * width), WIDE),
        ],
        scratch_shapes=[
            pltpu.VMEM((tp_count, D, 3 * width), LOW),
            pltpu.VMEM((D, rows), LOW),
            pltpu.VMEM((tiles, width, 2 * TILE), LOW),
            pltpu.VMEM((tiles, width, 2 * TILE), LOW),
            pltpu.VMEM((tiles, 2 * TILE, width), LOW),
            pltpu.VMEM((tiles, 2 * TILE, width), LOW),
            pltpu.VMEM((rows, 3 * width), LOW),
            pltpu.VMEM((D, 3 * width), LOW),
            pltpu.VMEM((rows, D), WIDE),
            pltpu.VMEM((rows, width), WIDE),
            pltpu.VMEM((rows, width), WIDE),
            pltpu.VMEM((width, rows), LOW),
            pltpu.SemaphoreType.DMA((tp_count * len(pieces),)),
        ],
        compiler_params=pltpu.CompilerParams(vmem_limit_bytes=48 * MIB),
        cost_estimate=cost(31),
    )(places, proj, totals, grad_att, normed, grad_out, *pieces)
    return outs[:-2], *outs[-2:]


def input_back_kernel(layer, grad, own, got, stream, vectors, grad_in, sums, kept):
    back, gain_sum, shift_sum = norm_back(
        stream[...].astype(WIDE), vectors[layer, 0:1, :], add_low(own[...], got[...])
    )
    grad_in[...] = (grad[...] + back).astype(grad_in.dtype)
    parts = jnp.concatenate([gain_sum, shift_sum], axis=0)

    @pl.when(pl.program_id(0) == 0)
    def _():
        kept[0:2, :] = parts

    @pl.when(pl.program_id(0) > 0)
    def _():
        kept[0:2, :] += parts

    sums[...] = kept[...]


def input_back(layer, grad, partial, stream, vectors, dtype):
    rows = grad.shape[0]
    steps = 4
    tile = pl.BlockSpec((rows // steps, D), lambda i: (i, 0))
    return pl.pallas_call(
        functools.partial(input_back_kernel, layer),
        grid=(steps,),
        in_specs=[tile] * 4 + [whole(vectors.shape)],
        out_specs=[tile, whole((8, D))],
        out_shape=[jax.ShapeDtypeStruct((rows, D), dtype), jax.ShapeDtypeStruct((8, D), WIDE)],
        scratch_shapes=[pltpu.VMEM((8, D), WIDE)],
        compiler_params=pltpu.CompilerParams(vmem_limit_bytes=24 * MIB),
        cost_estimate=cost(4),
    )(grad, *partial, stream, vectors)


def shards(
    tokens,
    cotangent,
    counts,
    qkv_weight,
    qkv_moment,
    qkv_square,
    out_weight,
    out_moment,
    out_square,
    up_weight,
    up_moment,
    up_square,
    down_weight,
    down_moment,
    down_square,
    row_vectors,
    row_moment,
    row_square,
    qv_bias,
    qv_moment,
    qv_square,
    up_bias,
    bias_moment,
    bias_square,
):
    row_count, slot_count, model_width = tokens.shape
    tp_count = lax.axis_size("tp")
    seq_len = row_count * tp_count
    half_width = qkv_weight.shape[3] // 2
    half_hidden = up_weight.shape[2] // 2
    core = lax.axis_index("wide") % 2
    tp_index = lax.axis_index("tp")
    core_scalar = core.astype(jnp.int32).reshape(1)

    places = piece_places()
    def bundle_rows(kernel, layer, first, second, columns, start):
        mine, other = pack(kernel, layer, start, first, second, columns)
        return by_core(mine, core_swap(other), 0)

    steps = Steps()
    near, across, back = (0, 1, 2)
    owns = [
        bundle_rows(pack_attn_kernel, 0, qkv_weight, out_weight, 4 * half_width, core_scalar)
    ]
    steps.end(owns[0])

    attn_moves = tp_moves(owns[0])
    steps.send(attn_moves[near], attn_moves[back])
    later = steps.gate(core_scalar)
    tokens, cotangent, counts, qv_bias_here, up_bias_here = (
        steps.gate(v) for v in (tokens, cotangent, counts, qv_bias, up_bias)
    )
    owns.append(bundle_rows(pack_mlp_kernel, 0, up_weight, down_weight, 2 * half_hidden, later))
    owns.append(bundle_rows(pack_attn_kernel, 1, qkv_weight, out_weight, 4 * half_width, later))
    owns.append(bundle_rows(pack_mlp_kernel, 1, up_weight, down_weight, 2 * half_hidden, later))
    token_parts = image_parts(tokens)

    group_count = jnp.where(tp_index // slot_count == core, counts, core_swap(counts))[0]
    live = (tp_index % slot_count) < group_count
    valid = (lax.iota(jnp.int32, seq_len) < VALID) & live

    own_bias = jnp.concatenate(
        [half_of(qv_bias_here, core, 2).reshape(-1), half_of(up_bias_here, core, 1).reshape(-1)]
    ).reshape(-1, TILE)
    bias_moves = tp_moves(own_bias)
    steps.end(own_bias, token_parts.own)

    up_own, down_own = owns[1][:, :half_hidden], owns[1][:, half_hidden:]
    up_moves, down_moves = tp_moves(up_own), tp_moves(down_own)
    steps.send(
        attn_moves[across],
        token_parts.moves[near],
        token_parts.moves[back],
        bias_moves[near],
        bias_moves[back],
    )
    steps.end(up_own, down_own)
    attn = Gather(jnp.stack([owns[0]] + [move.got for move in attn_moves]))

    steps.send(*attn.near(), up_moves[near], up_moves[back], token_parts.moves[across])
    steps.end()

    stream = image_rows(token_parts)
    steps.send(*attn.far(), up_moves[across], bias_moves[across])
    steps.end(stream)
    ups = Gather(jnp.stack([up_own] + [move.got for move in up_moves]))
    bias_blocks = by_source([own_bias] + [move.got for move in bias_moves]).reshape(tp_count, -1)
    qv_size = LAYERS * 2 * half_width
    qv_blocks = bias_blocks[:, :qv_size].reshape(tp_count, LAYERS, 2, half_width)
    up_blocks = bias_blocks[:, qv_size:].reshape(tp_count, LAYERS, half_hidden)

    def proj_bias(layer):
        qv_layer = qv_blocks[:, layer]
        return jnp.stack(
            [qv_layer[:, 0], jnp.zeros_like(qv_layer[:, 0]), qv_layer[:, 1]], axis=1
        ).reshape(1, -1)

    def up_bias_of(layer):
        return up_blocks[:, layer].reshape(1, -1)

    attn_rows = lax.all_gather(steps.gate(owns[2]), "tp")
    up_rows = lax.all_gather(behind(owns[3][:, :half_hidden], attn_rows), "tp")
    down_rows = lax.all_gather(behind(owns[3][:, half_hidden:], up_rows), "tp")
    steps.send(*ups.near(), down_moves[near], down_moves[back])
    attn_zero = attn.pieces()
    normed, proj = project(
        0, stream, (), row_vectors, proj_bias(0), places, attn_zero, True
    )
    attended, totals, part = attend(proj, places, attn_zero, True)
    steps.end(part)
    part = steps.gate(part)
    partial = (part, core_swap(part))
    steps.send(*ups.far(), down_moves[across])
    grad_parts = image_parts(steps.gate(cotangent))
    steps.end(grad_parts.own)
    downs = Gather(jnp.stack([down_own] + [move.got for move in down_moves]))
    steps.send(*downs.near(), grad_parts.moves[near], grad_parts.moves[back])
    steps.end()

    attn = Gather(steps.gate(attn_rows))
    steps.send(*downs.far(), *attn.near(), grad_parts.moves[across])
    steps.end()
    up_zero, down_zero = ups.pieces(), downs.pieces()
    ups = Gather(steps.gate(up_rows))
    steps.send(*attn.far())
    middle, normed_two, pre_act, hidden, part = mlp(
        0, stream, partial, row_vectors, up_bias_of(0), places, up_zero, down_zero, True
    )
    stored = [(stream, normed, proj, attended, totals, middle, normed_two, pre_act, hidden)]
    steps.end(part)
    part = steps.gate(part)
    partial = (part, core_swap(part))
    attn_one = attn.pieces()
    downs = Gather(steps.gate(down_rows))
    steps.send(*ups.near(), *downs.near())
    stream, normed, proj = project(
        1, middle, partial, row_vectors, proj_bias(1), places, attn_one, False
    )
    attended, totals, part = attend(proj, places, attn_one, False)
    steps.end(part)
    part = steps.gate(part)
    partial = (part, core_swap(part))
    steps.send(*ups.far())
    grad = jnp.where(valid[:, None], image_rows(grad_parts).astype(WIDE), 0.0)
    steps.end(*partial, grad)
    partial = tuple(steps.gate(v) for v in partial)
    grad = steps.gate(grad)
    steps.send(*downs.far())
    up_one = ups.pieces()
    middle, normed_two, pre_act, hidden = mlp(
        1, stream, partial, row_vectors, up_bias_of(1), places, up_one, (), False
    )
    stored.append((stream, normed, proj, attended, totals, middle, normed_two, pre_act, hidden))
    steps.end(hidden)
    down_one = downs.pieces()
    bundles = [(attn_zero, up_zero, down_zero), (attn_one, up_one, down_one)]

    def mlp_grads(layer, grad):
        _, ups, downs = bundles[layer]
        *_, normed_two, pre_act, _ = stored[layer]
        return mlp_back(grad, normed_two, pre_act, places, ups, downs, layer == 0)

    def attn_grads(layer, grad, part):
        stream, normed, proj, attended, totals, middle, *_ = stored[layer]
        attn = bundles[layer][0]
        grad_out, grad_mid, grad_att, sums = middle_back(
            layer,
            grad,
            (part, core_swap(part)),
            middle,
            row_vectors,
            attended,
            places,
            attn,
            layer == 0,
        )
        return (grad_mid, sums) + tuple(
            attend_back(
                proj, totals, grad_att, normed, grad_out, places, attn, layer == 0
            )
        )

    def vector_grad(input_sums, middle_sums, last_sum, proj_sums, bias_sum):
        proj_sums = proj_sums.reshape(tp_count, 3, half_width)
        return jnp.concatenate(
            [
                input_sums[:2].reshape(-1),
                middle_sums[:3].reshape(-1),
                last_sum.reshape(-1),
                proj_sums[:, 0].reshape(-1),
                proj_sums[:, 2].reshape(-1),
                bias_sum[:, 0].reshape(-1),
            ]
        )

    attn_new, wide_new = (), ()
    rate = D ** (-0.5)
    attn_rates, wide_rates = (rate, (D * 16 / SEQ) ** (-0.5)), (rate, FF ** (-0.5))
    attn_state = (qkv_weight, qkv_moment, qkv_square, out_weight, out_moment, out_square)
    wide_state = (up_weight, up_moment, up_square, down_weight, down_moment, down_square)

    pieces, last_sum = down_grad(grad, hidden, places)
    steps.end(last_sum)
    down_one_grad = Scatter(pieces)
    steps.send(*down_one_grad.far())
    pieces, part, bias_sum = mlp_grads(1, steps.gate(grad))
    steps.end(part)
    part = steps.gate(part)

    up_one_grad = Scatter(pieces)
    steps.send(*down_one_grad.rest(), *up_one_grad.far())
    grad_mid, middle_sums, pieces, part, proj_sums = attn_grads(1, grad, part)
    steps.end(part)
    part = steps.gate(part)

    attn_one_grad = Scatter(pieces)
    steps.send(*up_one_grad.rest(), *attn_one_grad.far())
    total = down_one_grad.total(up_one_grad.merged())
    down_grad_sum = scatter_tp(total)
    part = behind(part, total)
    grad, input_sums = input_back(
        1, grad_mid, (part, core_swap(part)), stored[1][0], row_vectors, WIDE
    )
    vector_one = vector_grad(input_sums, middle_sums, last_sum, proj_sums, bias_sum)
    pieces, last_sum = down_grad(grad, stored[0][-1], places)
    steps.end(last_sum)

    down_zero_grad = Scatter(pieces)
    steps.send(*attn_one_grad.rest(), *down_zero_grad.far())
    total = up_one_grad.total(attn_one_grad.merged())
    up_grad_sum = scatter_tp(total)
    pieces, part, bias_sum = mlp_grads(0, steps.gate(behind(grad, total)))
    steps.end(part)
    part = steps.gate(part)

    up_zero_grad = Scatter(pieces)
    steps.send(*down_zero_grad.rest(), *up_zero_grad.far())
    total = attn_one_grad.total(down_zero_grad.merged())
    attn_grad = scatter_tp(total)
    part = behind(part, total)
    grad_mid, middle_sums, pieces, part, proj_sums = attn_grads(0, grad, part)
    steps.end(part)
    part = steps.gate(part)

    attn_zero_grad = Scatter(pieces)
    steps.send(*up_zero_grad.rest(), *attn_zero_grad.far())
    grad, input_sums = input_back(
        0, grad_mid, (part, core_swap(part)), stored[0][0], row_vectors, LOW
    )
    total = down_zero_grad.total((grad,))
    down_zero_sum = scatter_tp(total)
    vector_zero = vector_grad(input_sums, middle_sums, last_sum, proj_sums, bias_sum)
    vectors = jnp.stack([vector_zero, vector_one])
    last_part = mlp_down(behind(steps.gate(hidden), total), places, down_one, False)
    wide_new = adam(
        False,
        wide_rates,
        1,
        behind(steps.gate(core_scalar), last_part),
        both_halves(steps.gate(up_grad_sum)) + both_halves(steps.gate(down_grad_sum)),
        wide_state,
        (),
    )
    last = middle + (add_low(last_part, core_swap(last_part)) + row_vectors[1, 5])
    last = jnp.where(valid[:, None], last, 0.0).astype(LOW)
    out_parts = group_parts([grad, last])
    vectors = vector_tp(vectors)
    steps.end(out_parts.own, vectors, wide_new[0])

    steps.send(*attn_zero_grad.rest())
    total = up_zero_grad.total(attn_zero_grad.merged())
    up_zero_sum = scatter_tp(total)
    steps.send(*out_parts.moves)
    steps.end(total)

    parts = Exchange(attn_zero_grad.total())
    steps.send(*parts.moves)
    vectors = vector_plane(steps.gate(vectors))
    attn_new = adam(
        True,
        attn_rates,
        1,
        steps.gate(core_scalar),
        both_halves(steps.gate(attn_grad)),
        attn_state,
        (),
    )
    input_grad, activations = group_rows(out_parts, 2)
    input_grad = input_grad.astype(WIDE)
    wide_new = adam(
        False,
        wide_rates,
        0,
        behind(core_scalar, attn_new[0]),
        both_halves(steps.gate(up_zero_sum)) + both_halves(steps.gate(down_zero_sum)),
        wide_state,
        wide_new,
    )
    steps.end(input_grad, activations, vectors, attn_new[0], wide_new[0])
    terms = [parts.own] + [move.got for move in parts.moves]
    attn_halves = both_halves(add_low(*terms).astype(LOW))
    attn_new = adam(True, attn_rates, 0, core_scalar, attn_halves, attn_state, attn_new)
    vector_totals = vectors
    qkv_new, qkv_moment_new, qkv_square_new, qkv_copy = attn_new[:4]
    out_new, out_moment_new, out_square_new, out_copy = attn_new[4:]
    up_new, up_moment_new, up_square_new, up_copy = wide_new[:4]
    down_new, down_moment_new, down_square_new, down_copy = wide_new[4:]

    def own_block(values):
        mine = lax.dynamic_index_in_dim(values, tp_index, values.ndim - 2, keepdims=False)
        return by_core(mine, core_swap(mine), mine.ndim - 1)

    row_size = 6 * model_width
    block_size = tp_count * half_width
    row_sum = vector_totals[:, :row_size].reshape(LAYERS, 6, model_width)
    qv_total = own_block(
        vector_totals[:, row_size : row_size + 2 * block_size].reshape(
            LAYERS, 2, tp_count, half_width
        )
    )
    up_total = own_block(
        vector_totals[:, row_size + 2 * block_size :].reshape(LAYERS, tp_count, half_hidden)
    )
    row_new, row_moment_new, row_square_new = adamw_step(
        row_vectors, row_moment, row_square, row_sum, VECTOR_RATE, 0.0
    )
    qv_new, qv_moment_new, qv_square_new = adamw_step(
        qv_bias, qv_moment, qv_square, qv_total, VECTOR_RATE, 0.0
    )
    up_bias_new, bias_moment_new, bias_square_new = adamw_step(
        up_bias, bias_moment, bias_square, up_total, VECTOR_RATE, 0.0
    )
    return (
        activations,
        input_grad,
        qkv_new,
        qkv_moment_new,
        qkv_square_new,
        qkv_copy,
        out_new,
        out_moment_new,
        out_square_new,
        out_copy,
        up_new,
        up_moment_new,
        up_square_new,
        up_copy,
        down_new,
        down_moment_new,
        down_square_new,
        down_copy,
        row_new,
        row_moment_new,
        row_square_new,
        qv_new,
        qv_moment_new,
        qv_square_new,
        up_bias_new,
        bias_moment_new,
        bias_square_new,
    )


def solution(mesh):
    return jax.shard_map(
        shards,
        mesh=mesh,
        in_specs=(
            P("tp", "wide", None),
            P("tp", "wide", None),
            P("wide"),
            P(None, "wide", None, "tp"),
            P(None, "wide", None, "tp"),
            P(None, "wide", None, "tp"),
            P(None, "tp", "wide"),
            P(None, "tp", "wide"),
            P(None, "tp", "wide"),
            P(None, "wide", "tp"),
            P(None, "wide", "tp"),
            P(None, "wide", "tp"),
            P(None, "tp", "wide"),
            P(None, "tp", "wide"),
            P(None, "tp", "wide"),
            P(),
            P(),
            P(),
            P(None, None, "tp"),
            P(None, None, "tp"),
            P(None, None, "tp"),
            P(None, "tp"),
            P(None, "tp"),
            P(None, "tp"),
        ),
        out_specs=(
            P("tp", "wide", None),
            P("tp", "wide", None),
            P(None, "wide", None, "tp"),
            P(None, "wide", None, "tp"),
            P(None, "wide", None, "tp"),
            P(None, "wide", None, "tp"),
            P(None, "tp", "wide"),
            P(None, "tp", "wide"),
            P(None, "tp", "wide"),
            P(None, "tp", "wide"),
            P(None, "wide", "tp"),
            P(None, "wide", "tp"),
            P(None, "wide", "tp"),
            P(None, "wide", "tp"),
            P(None, "tp", "wide"),
            P(None, "tp", "wide"),
            P(None, "tp", "wide"),
            P(None, "tp", "wide"),
            P(),
            P(),
            P(),
            P(None, None, "tp"),
            P(None, None, "tp"),
            P(None, None, "tp"),
            P(None, "tp"),
            P(None, "tp"),
            P(None, "tp"),
        ),
        check_vma=False,
    )
```
